128 devices in a mesh: gx: 16 (over z, x_hi, core), gy: 4 (over y), gz: 2 (over x_lo).
Axes of the slice: x: 4 (x_hi: 2, x_lo: 2; x = x_hi * 2 + x_lo), y: 4, z: 4, core: 2. Of those that a mesh axis runs over, the one named last changes fastest.
Arguments:
- electric: float32 [3, 160, 128, 512], P(None, 'gz', 'gx', 'gy'), may hold values from -6 to 6
- magnetic: float32 [3, 160, 128, 512], P(None, 'gz', 'gx', 'gy'), may hold values from -6 to 6
- material: int32 [160, 128, 512], P('gz', 'gx', 'gy'), may hold values from 0 to 4, as said below
- decay: float32 [5], replicated, may hold values from 0.5 to 1
- gain: float32 [5], replicated, may hold values from 0.15 to 0.45
- kernels: float32 [2, 24, 15, 15], replicated, may hold values from -0.0390625 to 0.0390625
Outputs:
- electric_out: float32 [3, 160, 128, 512], P(None, 'gz', 'gx', 'gy')
- image: float32 [128, 512], P(('gx', 'gz'), 'gy')
The draws below stay inside these ranges and needn't reach their ends.
Inputs may be any that keep to these rules, and one draw needn't show every extreme that they name: `material`: 0 vacuum, 1 molybdenum, 2 silicon, 3 absorber, 4 capping.
All inputs are finite; a program needn't handle non-finite values.
Results may differ from the reference program's by a relative error of at most 0.00028.
Values sent between devices are 32-bit elements; how exact they have to be, the bound alone decides.
No kernel may reach another device: no remote copies, remote signals or barrier semaphores. Data moves between devices by JAX's collectives and lax.ppermute only.
A program may use at most 128 MiB of HBM per device.

```python
import jax
import jax.numpy as jnp
from jax import lax

STEPS = 6
NKER = 24
KS = 15
NMAT = 5
NX = 128
NY = 512
NZ = 160


def draw_material(key, part):
    key = jax.random.fold_in(key, 7)
    rough_key, block_key = jax.random.split(key)
    roughness = jax.random.randint(rough_key, (NX, NY), 0, 2)
    blocks = jax.random.randint(block_key, (NX // 2, NY // 2), 0, 2)
    pattern = jnp.repeat(jnp.repeat(blocks, 2, axis=0), 2, axis=1)
    depths = (NZ - 1 - jnp.arange(NZ, dtype=jnp.int32))[:, None, None]
    vacuum_end = max(NZ // 16, 1)
    absorber_end = vacuum_end + max(NZ // 8, 1)
    capping_end = absorber_end + max(NZ // 128, 1)
    period = (depths - capping_end + roughness[None]) % 7
    layers = jnp.where(period < 3, 1, 2)
    material = jnp.where(depths < capping_end, 4, layers)
    material = jnp.where(depths < absorber_end, 3 * pattern[None], material)
    material = jnp.where(depths < vacuum_end, 0, material)
    return material.astype(jnp.int32)


def levels(key, dims, pieces, low, high):
    level, own = 1.0, jax.random.fold_in(key, 6)
    for axis_at, parts in pieces:
        steps = jnp.exp(jax.random.uniform(jax.random.fold_in(own, axis_at), (parts,), jnp.float32, low / len(pieces), high / len(pieces)))
        level = level * jnp.repeat(steps, dims[axis_at] // parts).reshape([-1 if axis == axis_at else 1 for axis in range(len(dims))])
    return level


def centred(own_key, extent, width, limit, shards=(), held_as=jnp.bfloat16):
    result = width * jax.random.normal(own_key, extent, jnp.float32)
    if shards:
        result = result * levels(own_key, extent, shards, -0.22, 0.18)
    return jnp.clip(result, -limit, limit).astype(held_as)


def setup_inputs(seed: int = 0) -> dict:
    key_list = jax.random.split(jax.random.key(seed), 7)
    electric = centred(key_list[0], (3, NZ, NX, NY), 1.0, 6.0, ((1, 2), (2, 16), (3, 4)), jnp.float32)
    magnetic = centred(key_list[1], (3, NZ, NX, NY), 1.0, 6.0, ((1, 2), (2, 16), (3, 4)), jnp.float32)
    material = draw_material(jax.random.fold_in(key_list[6], 71), 0)
    decay = jnp.clip(jax.random.uniform(key_list[3], (NMAT,), jnp.float32, 0.5, 1.0), 0.5, 1.0)
    gain = jnp.clip(jax.random.uniform(key_list[4], (NMAT,), jnp.float32, 0.15, 0.45), 0.15, 0.45)
    kernels = centred(key_list[5], (2, NKER, KS, KS), (4 * NKER * KS * KS) ** -0.5, 0.0390625, (), jnp.float32)
    return dict(electric=electric, magnetic=magnetic, material=material, decay=decay, gain=gain, kernels=kernels)


courant = 0.5


def lookup(material, table):
    values = jnp.zeros(material.shape, jnp.float32)
    for material_id in range(table.shape[0]):
        values = jnp.where(material == material_id, table[material_id], values)
    return values


def ahead(source, axis_id, periodic):
    if periodic:
        return jnp.roll(source, -1, axis_id) - source
    remainder = lax.slice_in_dim(source, 1, source.shape[axis_id], axis=axis_id)
    border = jnp.zeros_like(lax.slice_in_dim(source, 0, 1, axis=axis_id))
    return jnp.concatenate([remainder, border], axis_id) - source


def behind(source, axis_id, periodic):
    if periodic:
        return source - jnp.roll(source, 1, axis_id)
    remainder = lax.slice_in_dim(source, 0, source.shape[axis_id] - 1, axis=axis_id)
    border = jnp.zeros_like(lax.slice_in_dim(source, 0, 1, axis=axis_id))
    return source - jnp.concatenate([border, remainder], axis_id)


def image_rows(padded, kernels, rows, cols):
    taps = kernels.shape[2]
    amplitude = jnp.zeros((kernels.shape[0] * kernels.shape[1], padded.shape[0] * rows * cols), jnp.float32)
    for row_tap in range(taps):
        weights = kernels[:, :, row_tap, :].reshape(-1, taps)
        shifted = jnp.stack([padded[:, row_tap:row_tap + rows, col_tap:col_tap + cols] for col_tap in range(taps)])
        amplitude = amplitude + jnp.dot(weights, shifted.reshape(taps, -1), precision=lax.Precision.HIGHEST)
    return jnp.sum(amplitude * amplitude, 0).reshape(padded.shape[0], rows, cols).sum(0)


def reference(electric, magnetic, material, decay, gain, kernels):
    decay_cells = lookup(material, decay)
    gain_cells = lookup(material, gain)
    electric_x, electric_y, electric_z = electric[0], electric[1], electric[2]
    magnetic_x, magnetic_y, magnetic_z = magnetic[0], magnetic[1], magnetic[2]
    for step_index in range(STEPS):
        magnetic_x = magnetic_x - courant * (ahead(electric_z, 2, True) - ahead(electric_y, 0, False))
        magnetic_y = magnetic_y - courant * (ahead(electric_x, 0, False) - ahead(electric_z, 1, True))
        magnetic_z = magnetic_z - courant * (ahead(electric_y, 1, True) - ahead(electric_x, 2, True))
        electric_x = decay_cells * electric_x + gain_cells * (behind(magnetic_z, 2, True) - behind(magnetic_y, 0, False))
        electric_y = decay_cells * electric_y + gain_cells * (behind(magnetic_x, 0, False) - behind(magnetic_z, 1, True))
        electric_z = decay_cells * electric_z + gain_cells * (behind(magnetic_y, 1, True) - behind(magnetic_x, 2, True))
    plane = jnp.stack([electric_x[-1], electric_y[-1]])
    reach = kernels.shape[2] // 2
    padded = jnp.pad(plane, ((0, 0), (reach, reach), (reach, reach)), mode="wrap")
    image = image_rows(padded, kernels, plane.shape[1], plane.shape[2])
    return jnp.stack([electric_x, electric_y, electric_z]), image
```

```python
import functools

import jax
import jax.numpy as jnp
from jax import lax
from jax.experimental import pallas as pl
from jax.experimental.pallas import tpu as pltpu
from jax.sharding import PartitionSpec as P

STEPS = 6
W = STEPS
NC = 7
EY, EZ, EX, MY, MZ, MX, MAT = range(7)
SOURCE = ((0, 1), (0, 2), (0, 0), (1, 1), (1, 2), (1, 0))
ROWS = 8 + 2 * W
SPLIT = 5
TILES = 11
VMEM = 56 * 1024 * 1024


def around(value, axis, steps):
    count = lax.axis_size(axis)
    return lax.ppermute(value, axis, [(i, (i + steps) % count) for i in range(count)])


def copy_all(copies):
    for copy in copies:
        copy.start()
    for copy in copies:
        copy.wait()


def z_message_kernel(el, mg, mat, out, matv, sems):
    gz = lax.axis_index("gz")

    def part(first):
        copies = [
            pltpu.make_async_copy(mat.at[pl.ds(first * 8, 8 * W)], matv, sems.at[6])
        ]
        for c, (which, comp) in enumerate(SOURCE):
            src = (el, mg)[which]
            copies.append(
                pltpu.make_async_copy(
                    src.at[comp, pl.ds(first * 8, 8 * W)], out.at[c], sems.at[c]
                )
            )
        copy_all(copies)

    @pl.when(gz == 0)
    def _():
        part(80 - W)

    @pl.when(gz == 1)
    def _():
        part(0)

    out[MAT] = matv[...].astype(jnp.float32)


def z_message(el, mg, mat):
    return pl.pallas_call(
        z_message_kernel,
        out_shape=jax.ShapeDtypeStruct((NC, 8 * W, 128), jnp.float32),
        in_specs=[pl.BlockSpec(memory_space=pl.ANY)] * 3,
        out_specs=pl.BlockSpec(memory_space=pltpu.VMEM),
        scratch_shapes=[
            pltpu.VMEM((8 * W, 128), jnp.int32),
            pltpu.SemaphoreType.DMA((7,)),
        ],
        compiler_params=pltpu.CompilerParams(vmem_limit_bytes=VMEM),
        name="z_message",
    )(el, mg, mat)


def pack_kernel(ta, tb, el, mg, mat, zh, own, up, down, strip, ext, matv, planes, strips, sems, osem):
    gz = lax.axis_index("gz")
    layers = 8 * (tb - ta)
    la = 8 * ta

    def load(side):
        low, high = (0, 80) if side == 0 else (W, 80 + W)
        zlow, zhigh = (80, 80 + W) if side == 0 else (0, W)
        a, b = max(low, la), min(high, la + layers)
        za, zb = max(zlow, la), min(zhigh, la + layers)
        size = 8 * (b - a)
        copies = [
            pltpu.make_async_copy(
                mat.at[pl.ds(8 * (a - low), size)], matv.at[pl.ds(8 * (a - la), size)], sems.at[6]
            )
        ]
        for c, (which, comp) in enumerate(SOURCE):
            src = (el, mg)[which]
            copies.append(
                pltpu.make_async_copy(
                    src.at[comp, pl.ds(8 * (a - low), size)],
                    ext.at[c, pl.ds(8 * (a - la), size)],
                    sems.at[c],
                )
            )
        if zb > za:
            copies.append(
                pltpu.make_async_copy(
                    zh.at[:, pl.ds(8 * (za - zlow), 8 * (zb - za))],
                    ext.at[:, pl.ds(8 * (za - la), 8 * (zb - za))],
                    sems.at[7],
                )
            )
        copy_all(copies)
        for l in range(a - la, b - la):
            ext[MAT, 8 * l : 8 * l + 8, :] = matv[8 * l : 8 * l + 8, :].astype(jnp.float32)

    @pl.when(gz == 0)
    def _():
        load(0)

    @pl.when(gz == 1)
    def _():
        load(1)

    for l in range(max(80 + W - la, 0), layers):
        for c in range(NC):
            ext[c, 8 * l : 8 * l + 8, :] = jnp.full((8, 128), -1.0 if c == MAT else 0.0)

    lane = lax.broadcasted_iota(jnp.int32, (8, 128), 1)
    masks = [((lane - 16 * c + W + 128) % 128) < 2 * W for c in range(NC)]

    def row(r, _):
        for t in range(tb - ta):
            total = None
            for c in range(NC):
                v = ext[c, pl.ds(64 * t + r, 8, stride=8), :]
                if MY <= c <= MX:
                    v = v * 2.0
                planes[r * NC + c, 8 * t : 8 * t + 8, :] = v
                if c == 0:
                    total = v
                else:
                    total = jnp.where(masks[c], pltpu.roll(v, 16 * c, 1), total)
            strips[r, 8 * t : 8 * t + 8, :] = total
        return 0

    lax.fori_loop(0, 8, row, 0)
    copy_all(
        [
            pltpu.make_async_copy(planes.at[pl.ds(21, 35)], up.at[pl.ds(0, 35)], osem.at[0]),
            pltpu.make_async_copy(planes.at[pl.ds(14, 5)], up.at[pl.ds(35, 5)], osem.at[1]),
            pltpu.make_async_copy(planes.at[pl.ds(0, 37)], down, osem.at[2]),
            pltpu.make_async_copy(planes, own, osem.at[3]),
            pltpu.make_async_copy(strips, strip, osem.at[4]),
        ]
    )


def pack(ta, tb, el, mg, mat, zh):
    layers = 8 * (tb - ta)
    f32 = jnp.float32
    return pl.pallas_call(
        functools.partial(pack_kernel, ta, tb),
        out_shape=[
            jax.ShapeDtypeStruct((8 * NC, layers, 128), f32),
            jax.ShapeDtypeStruct((40, layers, 128), f32),
            jax.ShapeDtypeStruct((37, layers, 128), f32),
            jax.ShapeDtypeStruct((8, layers, 128), f32),
        ],
        in_specs=[pl.BlockSpec(memory_space=pl.ANY)] * 4,
        out_specs=[pl.BlockSpec(memory_space=pl.ANY)] * 4,
        scratch_shapes=[
            pltpu.VMEM((NC, 8 * layers, 128), f32),
            pltpu.VMEM((8 * layers, 128), jnp.int32),
            pltpu.VMEM((8 * NC, layers, 128), f32),
            pltpu.VMEM((8, layers, 128), f32),
            pltpu.SemaphoreType.DMA((8,)),
            pltpu.SemaphoreType.DMA((5,)),
        ],
        compiler_params=pltpu.CompilerParams(vmem_limit_bytes=VMEM),
        cost_estimate=pl.CostEstimate(flops=0, bytes_accessed=12_000_000, transcendentals=0),
        name="pack_%d" % ta,
    )(el, mg, mat, zh)


def steps_kernel(ta, tb, pieces, lo, hi, decay, gain, *refs):
    n = len(pieces)
    strips, inputs = refs[:3], refs[3 : 3 + 3 * n]
    upper = tb == TILES
    if upper:
        out, plane, f0, f1, g0, g1, sv, stage, sems, osem = refs[3 + 3 * n :]
    else:
        _, out, f0, f1, g0, g1, sv, stage, sems, osem = refs[3 + 3 * n :]
    tiles = tb - ta
    gz = lax.axis_index("gz")
    layers = pl.ds(8 * ta, 8 * tiles)
    moves = [
        (strips[0].at[:, layers], sv.at[pl.ds(W, 8)]),
        (strips[1].at[:, layers], sv.at[pl.ds(0, W)]),
        (strips[2].at[:, layers], sv.at[pl.ds(W + 8, W)]),
    ]
    for k, (pa, pb, first) in enumerate(pieces):
        own, low, high = inputs[3 * k : 3 * k + 3]
        size = 8 * (pb - pa)
        src = pl.ds(8 * (pa - first), size)
        dst = pl.ds(8 + 8 * (pa - ta), size)
        moves += [
            (own.at[:, src], f0.at[pl.ds(W * NC, 8 * NC), dst]),
            (low.at[pl.ds(0, 35), src], f0.at[pl.ds(NC, 35), dst]),
            (low.at[pl.ds(35, 5), src], f0.at[pl.ds(0, 5), dst]),
            (high.at[:, src], f0.at[pl.ds((W + 8) * NC, 37), dst]),
        ]
    copies = [pltpu.make_async_copy(x, y, sems.at[i]) for i, (x, y) in enumerate(moves)]
    copy_all(copies)

    top = 8 + 8 * tiles
    zero = jnp.zeros((8, 128), jnp.float32)
    fields = (f0, f1)
    gains = (g0, g1)

    def prepare(r, _):
        base = r * NC
        for t in range(tiles):
            v = sv[r, 8 * t : 8 * t + 8, :]
            for c in range(NC):
                f1[base + c, 8 + 8 * t : 16 + 8 * t, :] = (
                    pltpu.roll(v, 128 - 16 * c, 1) if c else v
                )
        for f in fields:
            f[base + MX, 0:8, :] = zero
            f[base + MY, 0:8, :] = zero
            f[base + EX, top : top + 8, :] = zero
            f[base + EY, top : top + 8, :] = zero
        return 0

    lax.fori_loop(0, ROWS, prepare, 0)

    def tables(r, _):
        for t in range(tiles):
            for f, g in zip(fields, gains):
                ids = f[r * NC + MAT, 8 + 8 * t : 16 + 8 * t, :]
                d_cells, g_cells = zero, zero
                for i in range(5):
                    hit = ids == float(i)
                    d_cells = jnp.where(hit, decay[i], d_cells)
                    g_cells = jnp.where(hit, gain[i] * 0.5, g_cells)
                f[r * NC + MAT, 8 + 8 * t : 16 + 8 * t, :] = d_cells
                g[r, 8 + 8 * t : 16 + 8 * t, :] = g_cells
        return 0

    lax.fori_loop(1, ROWS - 1, tables, 0)

    lane = lax.broadcasted_iota(jnp.int32, (8, 128), 1)
    last, first_lane = lane == 127, lane == 0

    def next_y(a, b):
        ra, rb = pltpu.roll(a, 127, 1), pltpu.roll(b, 127, 1)
        return jnp.where(last, rb, ra), jnp.where(last, ra, rb)

    def previous_y(a, b):
        ra, rb = pltpu.roll(a, 1, 1), pltpu.roll(b, 1, 1)
        return jnp.where(first_lane, rb, ra), jnp.where(first_lane, ra, rb)

    def row(r, full):
        base = r * NC
        for t in range(tiles):
            p = 8 + 8 * t

            def pair(c, shift=0, rows=0):
                return [f[base + rows * NC + c, p + shift : p + shift + 8, :] for f in fields]

            ex, ey, ez = pair(EX), pair(EY), pair(EZ)
            mx, my, mz = pair(MX), pair(MY), pair(MZ)
            ex_z = pair(EX, 1)
            ey_x, ez_x = pair(EY, 0, 1), pair(EZ, 0, 1)
            ex_y = next_y(*ex)
            if full:
                ey_z = pair(EY, 1)
                ez_y = next_y(*ez)
            for k, f in enumerate(fields):
                if full:
                    mx[k] = mx[k] - ((ez_y[k] - ez[k]) - (ey_z[k] - ey[k]))
                    f[base + MX, p : p + 8, :] = mx[k]
                my[k] = my[k] - ((ex_z[k] - ex[k]) - (ez_x[k] - ez[k]))
                mz[k] = mz[k] - ((ey_x[k] - ey[k]) - (ex_y[k] - ex[k]))
                f[base + MY, p : p + 8, :] = my[k]
                f[base + MZ, p : p + 8, :] = mz[k]
            if not full:
                continue
            mx_z, my_z = pair(MX, -1), pair(MY, -1)
            my_x, mz_x = pair(MY, 0, -1), pair(MZ, 0, -1)
            mz_y, mx_y = previous_y(*mz), previous_y(*mx)
            for k, f in enumerate(fields):
                d = f[base + MAT, p : p + 8, :]
                g = gains[k][r, p : p + 8, :]
                f[base + EX, p : p + 8, :] = d * ex[k] + g * (
                    (mz[k] - mz_y[k]) - (my[k] - my_z[k])
                )
                f[base + EY, p : p + 8, :] = d * ey[k] + g * (
                    (mx[k] - mx_z[k]) - (mz[k] - mz_x[k])
                )
                f[base + EZ, p : p + 8, :] = d * ez[k] + g * (
                    (my[k] - my_x[k]) - (mx[k] - mx_y[k])
                )

    def step(s, _):
        left = STEPS - 1 - s
        row(W - 1 - left, False)

        def inner(r, _):
            row(r, True)
            return 0

        lax.fori_loop(W - left, W + 8 + left, inner, 0)
        return 0

    lax.fori_loop(0, STEPS, step, 0)

    t_lo, t_hi = lo // 8 - ta, -(-hi // 8) - ta

    def emit(r, _):
        for c, source in ((0, EX), (1, EY), (2, EZ)):
            for t in range(t_lo, t_hi):
                stage[c, pl.ds(64 * (t - t_lo) + r, 8, stride=8), :] = f0[
                    (r + W) * NC + source, 8 + 8 * t : 16 + 8 * t, :
                ]
        return 0

    lax.fori_loop(0, 8, emit, 0)
    if upper:
        at = 8 * (80 + W - 1 - lo)
        plane[0] = stage[0, at : at + 8, :]
        plane[1] = stage[1, at : at + 8, :]

    def write(side):
        low, high = (0, 80) if side == 0 else (W, 80 + W)
        a, b = max(low, lo), min(high, hi)
        size = 8 * (b - a)
        copy_all(
            [
                pltpu.make_async_copy(
                    stage.at[c, pl.ds(8 * (a - lo), size)],
                    out.at[c, pl.ds(8 * (a - low), size)],
                    osem.at[c],
                )
                for c in range(3)
            ]
        )

    @pl.when(gz == 0)
    def _():
        write(0)

    @pl.when(gz == 1)
    def _():
        write(1)


def run_steps(ta, tb, pieces, lo, hi, decay, gain, arrays, before=None):
    f32 = jnp.float32
    tiles = tb - ta
    upper = tb == TILES
    smem = pl.BlockSpec(memory_space=pltpu.SMEM)
    hbm = pl.BlockSpec(memory_space=pl.ANY)
    z = 16 + 8 * tiles
    out_shape = [jax.ShapeDtypeStruct((3, 640, 128), f32)]
    out_specs = [hbm]
    args = [decay, gain, *arrays]
    aliases = {}
    if upper:
        out_shape.append(jax.ShapeDtypeStruct((2, 8, 128), f32))
        out_specs.append(pl.BlockSpec(memory_space=pltpu.VMEM))
    else:
        aliases = {len(args): 0}
        args.append(before)
    return pl.pallas_call(
        functools.partial(steps_kernel, ta, tb, pieces, lo, hi),
        out_shape=out_shape,
        in_specs=[smem, smem] + [hbm] * (len(args) - 2),
        out_specs=out_specs,
        scratch_shapes=[
            pltpu.VMEM((ROWS * NC, z, 128), f32),
            pltpu.VMEM((ROWS * NC, z, 128), f32),
            pltpu.VMEM((ROWS, z, 128), f32),
            pltpu.VMEM((ROWS, z, 128), f32),
            pltpu.VMEM((ROWS, 8 * tiles, 128), f32),
            pltpu.VMEM((3, 64 * (-(-hi // 8) - lo // 8), 128), f32),
            pltpu.SemaphoreType.DMA((3 + 4 * len(pieces),)),
            pltpu.SemaphoreType.DMA((3,)),
        ],
        input_output_aliases=aliases,
        compiler_params=pltpu.CompilerParams(vmem_limit_bytes=VMEM),
        cost_estimate=pl.CostEstimate(flops=0, bytes_accessed=20_000_000, transcendentals=0),
        name="steps_%d" % ta,
    )(*args)


def image_kernel(weights, centre, before, after, out, sh, rhs):
    gz = lax.axis_index("gz")
    lane = lax.broadcasted_iota(jnp.int32, (24, 128), 1)
    for q in range(15):
        shift = q - 7
        for c in range(2):
            v = centre[c]
            if shift > 0:
                v = jnp.where(
                    lane >= 128 - shift,
                    pltpu.roll(after[c], 128 - shift, 1),
                    pltpu.roll(v, 128 - shift, 1),
                )
            elif shift < 0:
                v = jnp.where(
                    lane < -shift, pltpu.roll(before[c], -shift, 1), pltpu.roll(v, -shift, 1)
                )
            sh[q, c] = v

    def fill(side):
        for q in range(15):
            for c in range(2):
                for i in range(4):
                    start = 4 * side + 1 + i
                    rhs[16 * q : 16 * q + 16, (4 * c + i) * 128 : (4 * c + i + 1) * 128] = sh[
                        q, c, start : start + 16, :
                    ]

    @pl.when(gz == 0)
    def _():
        fill(0)

    @pl.when(gz == 1)
    def _():
        fill(1)

    amplitude = jnp.dot(
        weights[...],
        rhs[...],
        precision=lax.Precision.HIGHEST,
        preferred_element_type=jnp.float32,
    )
    power = jnp.sum(amplitude * amplitude, axis=0, keepdims=True)
    for i in range(4):
        out[i : i + 1, :] = (
            power[:, i * 128 : (i + 1) * 128] + power[:, (4 + i) * 128 : (5 + i) * 128]
        )


def image_of(weights, centre, before, after):
    return pl.pallas_call(
        image_kernel,
        out_shape=jax.ShapeDtypeStruct((4, 128), jnp.float32),
        in_specs=[pl.BlockSpec(memory_space=pltpu.VMEM)] * 4,
        out_specs=pl.BlockSpec(memory_space=pltpu.VMEM),
        scratch_shapes=[
            pltpu.VMEM((15, 2, 24, 128), jnp.float32),
            pltpu.VMEM((240, 1024), jnp.float32),
        ],
        compiler_params=pltpu.CompilerParams(vmem_limit_bytes=VMEM),
        name="image",
    )(weights, centre, before, after)


def behind(value, *others):
    return lax.optimization_barrier((value, *others))[0]


def on_device(electric, magnetic, material, decay, gain, kernels):
    el = electric.reshape(3, 640, 128)
    mg = magnetic.reshape(3, 640, 128)
    mat = material.reshape(640, 128)
    weights = jnp.pad(
        kernels.transpose(0, 1, 3, 2).reshape(48, 15, 15), ((0, 0), (0, 0), (0, 1))
    ).reshape(48, 240)
    zh = around(z_message(el, mg, mat), "gz", 1)

    own_u, up_u, down_u, strip_u = pack(SPLIT, TILES, el, mg, mat, zh)
    low_u, high_u = around(up_u, "gx", 1), around(down_u, "gx", -1)
    own_l, up_l, down_l, strip_l = pack(0, SPLIT, el, mg, mat, zh)
    strips = jnp.concatenate([strip_l, strip_u], 1)
    from_low, from_high = around(strips, "gy", 1), around(strips, "gy", -1)
    lane = lax.broadcasted_iota(jnp.int32, strips.shape, 2)
    strips = jnp.where(lane % 16 < 8, from_high, from_low)
    s_low, s_high = around(strips[8 - W :], "gx", 1), around(strips[:W], "gx", -1)
    up_l, down_l = behind((up_l, down_l), strips)
    low_l, high_l = around(up_l, "gx", 1), around(down_l, "gx", -1)

    sides = [strips, s_low, s_high]
    field, plane = run_steps(
        SPLIT,
        TILES,
        [(SPLIT, TILES, SPLIT)],
        8 * (SPLIT + 1),
        8 * TILES,
        decay,
        gain,
        [*sides, own_u, low_u, high_u],
    )
    top = lax.ppermute(plane, "gz", [(1, 0)])
    top = jnp.where(lax.axis_index("gz") == 1, plane, top)
    top = jnp.stack([top, around(top, "gy", 1), around(top, "gy", -1)])
    top = jnp.concatenate([around(top, "gx", 1), top, around(top, "gx", -1)], 2)
    image = image_of(weights, top[0], top[1], top[2])
    (field,) = run_steps(
        0,
        SPLIT + 2,
        [(0, SPLIT, 0), (SPLIT, SPLIT + 2, SPLIT)],
        0,
        8 * (SPLIT + 1),
        decay,
        gain,
        [*sides, own_l, low_l, high_l, own_u, low_u, high_u],
        field,
    )
    return (field.reshape(3, 80, 8, 128), image)


def solution(mesh):
    in_specs = (
        P(None, "gz", "gx", "gy"),
        P(None, "gz", "gx", "gy"),
        P("gz", "gx", "gy"),
        P(),
        P(),
        P(),
    )
    out_specs = (P(None, "gz", "gx", "gy"), P(("gx", "gz"), "gy"))
    return jax.shard_map(
        on_device, mesh=mesh, in_specs=in_specs, out_specs=out_specs, check_vma=False
    )
```

```python
import functools

import jax
import jax.numpy as jnp
from jax import lax
from jax.experimental import pallas as pl
from jax.experimental.pallas import tpu as pltpu
from jax.sharding import PartitionSpec as P

STEPS = 6
W = STEPS
Y, Z, X = range(3)
NC = 7
SOURCE = ((0, 1), (0, 2), (0, 0), (1, 1), (1, 2), (1, 0))
ROWS = 8 + 2 * W
BASE = 4
HELD = BASE + ROWS + 2
CUT = 4
TILES = 7
ON = 5
LAG = 4
VMEM = 56 * 1024 * 1024
F32 = jnp.float32
HBM = pl.BlockSpec(memory_space=pl.ANY)
LOCAL = pl.BlockSpec(memory_space=pltpu.VMEM)


def around(value, axis, steps):
    count = lax.axis_size(axis)
    return lax.ppermute(value, axis, [(i, (i + steps) % count) for i in range(count)])


def copy_all(pairs, sems):
    copies = [pltpu.make_async_copy(a, b, sems.at[i]) for i, (a, b) in enumerate(pairs)]
    for copy in copies:
        copy.start()
    for copy in copies:
        copy.wait()


def params():
    return pltpu.CompilerParams(vmem_limit_bytes=VMEM)


def cost(us):
    return pl.CostEstimate(flops=0, bytes_accessed=int(us * 3e6), transcendentals=0)


def pack_kernel(ta, tb, el, mg, mat, *refs):
    if ta:
        own, up, down, strip, ext, matv, planes, strips, sems = refs
    else:
        strip_above, own, up, down, strip, ext, matv, planes, strips, sems = refs
    tiles = tb - ta
    rows = pl.ds(64 * ta, 64 * tiles)
    loads = [(mat.at[rows], matv)]
    for c, (which, comp) in enumerate(SOURCE):
        loads.append(((el, mg)[which].at[comp, rows], ext.at[c]))
    copy_all(loads, sems)

    lane = lax.broadcasted_iota(jnp.int32, (8, 128), 1)
    masks = [((lane - 16 * c + W + 128) % 128) < 2 * W for c in range(NC)]

    def row(r, _):
        for t in range(tiles):
            z = 8 * t
            total = None
            for c in range(NC):
                if c == 6:
                    v = matv[pl.ds(64 * t + r, 8, stride=8), :].astype(F32)
                    planes[48 + r, z : z + 8, :] = v
                else:
                    v = ext[c, pl.ds(64 * t + r, 8, stride=8), :]
                    if c >= 3:
                        v = v * 2.0
                    planes[24 * (c // 3) + 3 * r + c % 3, z : z + 8, :] = v
                turned = pltpu.roll(v, 16 * c, 1) if c else v
                total = jnp.where(masks[c], turned, total) if c else v
            strips[r, z : z + 8, :] = total
        return 0

    lax.fori_loop(0, 8, row, 0)
    pairs = [(planes, own)]
    pairs += [
        (planes.at[pl.ds(a, n)], up.at[pl.ds(b, n)])
        for a, b, n in ((6, 0, 18), (30, 18, 2), (33, 20, 15), (51, 35, 5))
    ]
    pairs += [
        (planes.at[pl.ds(a, n)], down.at[pl.ds(b, n)])
        for a, b, n in ((0, 0, 17), (24, 17, 15), (48, 32, 5))
    ]
    if ta:
        pairs.append((strips, strip))
    else:
        pairs.append((strips, strip.at[:, pl.ds(0, 8 * tiles)]))
        pairs.append((strip_above, strip.at[:, pl.ds(8 * tiles, 80 - 8 * tiles)]))
    copy_all(pairs, sems)


def pack(ta, tb, el, mg, mat, *strip_above):
    layers = 8 * (tb - ta)
    return pl.pallas_call(
        functools.partial(pack_kernel, ta, tb),
        out_shape=[
            jax.ShapeDtypeStruct((8 * NC, layers, 128), F32),
            jax.ShapeDtypeStruct((40, layers, 128), F32),
            jax.ShapeDtypeStruct((37, layers, 128), F32),
            jax.ShapeDtypeStruct((8, layers if ta else 80, 128), F32),
        ],
        in_specs=[HBM] * (3 + len(strip_above)),
        out_specs=[HBM] * 4,
        scratch_shapes=[
            pltpu.VMEM((6, 8 * layers, 128), F32),
            pltpu.VMEM((8 * layers, 128), jnp.int32),
            pltpu.VMEM((8 * NC, layers, 128), F32),
            pltpu.VMEM((8, layers, 128), F32),
            pltpu.SemaphoreType.DMA((10,)),
        ],
        compiler_params=params(),
        cost_estimate=cost(3),
        name="pack_upper" if ta else "pack_lower",
    )(el, mg, mat, *strip_above)


def edge_kernel(from_low, from_high, own_u, own_l, strips, edge, sems):
    gz = lax.axis_index("gz")
    lane = lax.broadcasted_iota(jnp.int32, (8, 80, 128), 2)
    strips[...] = jnp.where(lane % 16 < 8, from_high[...], from_low[...])

    @pl.when(gz == 0)
    def _():
        copy_all([(own_u.at[:, pl.ds(8 * (9 - CUT), 8)], edge.at[pl.ds(0, 56)])], sems)
        edge[56:64] = strips[:, 72:80, :]

    @pl.when(gz == 1)
    def _():
        copy_all([(own_l.at[:, pl.ds(0, 8)], edge.at[pl.ds(0, 56)])], sems)
        edge[56:64] = strips[:, 0:8, :]


def edges(from_low, from_high, own_u, own_l):
    return pl.pallas_call(
        edge_kernel,
        out_shape=[
            jax.ShapeDtypeStruct((8, 80, 128), F32),
            jax.ShapeDtypeStruct((64, 8, 128), F32),
        ],
        in_specs=[LOCAL, LOCAL, HBM, HBM],
        out_specs=[LOCAL, LOCAL],
        scratch_shapes=[pltpu.SemaphoreType.DMA((1,))],
        compiler_params=params(),
        cost_estimate=cost(1),
        name="edges",
    )(from_low, from_high, own_u, own_l)


def corner_kernel(strips, edge, up, down, sems):
    pairs = [
        (edge.at[pl.ds(a, n)], up.at[pl.ds(b, n)])
        for a, b, n in ((6, 0, 18), (30, 18, 2), (33, 20, 15), (51, 35, 5), (58, 100, 6))
    ]
    pairs += [
        (edge.at[pl.ds(a, n)], down.at[pl.ds(b, n)])
        for a, b, n in ((0, 0, 17), (24, 17, 15), (48, 32, 5), (56, 97, 6))
    ]
    pairs.append((strips.at[pl.ds(20, 60)], up.at[pl.ds(40, 60)]))
    pairs.append((strips.at[pl.ds(0, 60)], down.at[pl.ds(37, 60)]))
    copy_all(pairs, sems)


def corners(strips, edge):
    return pl.pallas_call(
        corner_kernel,
        out_shape=[
            jax.ShapeDtypeStruct((106, 8, 128), F32),
            jax.ShapeDtypeStruct((103, 8, 128), F32),
        ],
        in_specs=[HBM, HBM],
        out_specs=[HBM, HBM],
        scratch_shapes=[pltpu.SemaphoreType.DMA((11,))],
        compiler_params=params(),
        cost_estimate=cost(1),
        name="corners",
    )(strips, edge)


def steps_kernel(upper, decay, gain, strips, edge, low_c, high_c, *refs):
    gz = lax.axis_index("gz")
    if upper:
        own_u, low_u, high_u, out, plane, *scratch = refs
        sets = [((own_u, low_u, high_u), 8 * (10 - CUT), 0)]
        halo, counts = TILES - 1, gz == 0
        held = [(t, t + CUT) for t in range(TILES - 1)]
    else:
        own_u, low_u, high_u, own_l, low_l, high_l, _, out, *scratch = refs
        sets = [
            ((own_l, low_l, high_l), 8 * CUT, 8),
            ((own_u, low_u, high_u), 8 * (TILES - 1 - CUT), 8 + 8 * CUT),
        ]
        halo, counts = 0, gz == 1
        held = [(t, t - 1) for t in range(1, TILES)]
    ea0, ea1, eb0, eb1, ma0, ma1, mb0, mb1, d0, d1, g0, g1, ya, yb, ym, stage, sems = scratch
    es, ms, yes = ((ea0, ea1), (eb0, eb1)), ((ma0, ma1), (mb0, mb1)), (ya, yb)
    ds_, gs = (d0, d1), (g0, g1)

    moves = []
    for (own, low, high), layers, to in sets:
        src, zf, zd = pl.ds(0, layers), pl.ds(8 + to, layers), pl.ds(to, layers)
        first, mid, last_ = BASE, BASE + W, BASE + W + 8
        for ref, a, n, dst, b, z in (
            (own, 0, 24, ea0, 3 * mid, zf),
            (own, 24, 24, ma0, 3 * mid, zf),
            (own, 48, 8, d0, mid, zd),
            (low, 0, 18, ea0, 3 * first, zf),
            (low, 18, 2, ma0, 3 * first, zf),
            (low, 20, 15, ma0, 3 * first + 3, zf),
            (low, 35, 5, d0, first + 1, zd),
            (high, 0, 17, ea0, 3 * last_, zf),
            (high, 17, 15, ma0, 3 * last_, zf),
            (high, 32, 5, d0, last_, zd),
        ):
            moves.append((ref.at[pl.ds(a, n), src], dst.at[pl.ds(b, n), z]))
    copies = [pltpu.make_async_copy(a, b, sems.at[i]) for i, (a, b) in enumerate(moves)]
    for copy in copies:
        copy.start()

    zero = jnp.zeros((8, 128), F32)
    top = 8 + 8 * TILES

    def unpack(ref, first, ref_z, first_z, count, row):
        def body(r, _):
            at = BASE + row + r
            for t, tile in held + [(halo, None)]:
                v = ref_z[first_z + r] if tile is None else ref[first + 10 * r + tile]
                z = 8 * t
                for c in range(NC):
                    turned = pltpu.roll(v, 128 - 16 * c, 1) if c else v
                    if c < 3:
                        ea1[3 * at + c, 8 + z : 16 + z, :] = turned
                    elif c < 6:
                        ma1[3 * at + c - 3, 8 + z : 16 + z, :] = turned
                    else:
                        d1[at, z : z + 8, :] = turned
            return 0

        lax.fori_loop(0, count, body, 0)

    unpack(low_c, 40, low_c, 100, W, 0)
    unpack(strips, 0, edge, 56, 8, W)
    unpack(high_c, 37, high_c, 97, W, W + 8)

    def ends(r, _):
        for pair in ms:
            for m in pair:
                m[3 * r + X, 0:8, :] = zero
                m[3 * r + Y, 0:8, :] = zero
        for pair in es:
            for e in pair:
                e[3 * r + X, top : top + 8, :] = zero
                e[3 * r + Y, top : top + 8, :] = zero
        return 0

    lax.fori_loop(0, HELD, ends, 0)
    hz = 8 * halo

    @pl.when(counts)
    def _():
        for ref, a, n, dst, b, to in (
            (edge, 0, 24, ea0, 3 * (BASE + W), 8),
            (edge, 24, 24, ma0, 3 * (BASE + W), 8),
            (edge, 48, 8, d0, BASE + W, 0),
            (low_c, 0, 18, ea0, 3 * BASE, 8),
            (low_c, 18, 2, ma0, 3 * BASE, 8),
            (low_c, 20, 15, ma0, 3 * BASE + 3, 8),
            (low_c, 35, 5, d0, BASE + 1, 0),
            (high_c, 0, 17, ea0, 3 * (BASE + W + 8), 8),
            (high_c, 17, 15, ma0, 3 * (BASE + W + 8), 8),
            (high_c, 32, 5, d0, BASE + W + 8, 0),
        ):
            for i in range(n):
                dst[b + i, hz + to : hz + to + 8, :] = ref[a + i]

    @pl.when(jnp.logical_not(counts))
    def _():
        def clear(i, _):
            for ref in (ea0, ea1, ma0, ma1):
                ref[3 * BASE + i, hz + 8 : hz + 16, :] = zero
            return 0

        lax.fori_loop(0, 3 * ROWS, clear, 0)

    for copy in copies:
        copy.wait()

    live = jnp.where(counts, 1.0, 0.0).astype(F32)

    def tables(r, _):
        for t in range(TILES):
            z = 8 * t
            for d, g in zip(ds_, gs):
                ids = d[r, z : z + 8, :]
                d_cells, g_cells = zero, zero
                for i in range(5):
                    hit = ids == float(i)
                    d_cells = jnp.where(hit, decay[i], d_cells)
                    g_cells = jnp.where(hit, gain[i] * 0.5, g_cells)
                if t == halo:
                    d_cells, g_cells = d_cells * live, g_cells * live
                d[r, z : z + 8, :] = d_cells
                g[r, z : z + 8, :] = g_cells
        return 0

    lax.fori_loop(BASE + 1, BASE + ROWS - 1, tables, 0)

    lane = lax.broadcasted_iota(jnp.int32, (8, 128), 1)
    last, first_lane = lane == 127, lane == 0
    units = [(row, t) for row in range(2) for t in range(TILES)]

    def first_turn(i, _):
        kept = []
        for row, t in units:
            r = BASE + 2 * i + row
            for j, c in enumerate((X, Z)):
                pair = [pltpu.roll(e[3 * r + c, 8 + 8 * t : 16 + 8 * t, :], 127, 1) for e in es[0]]
                kept.append((4 * r + 2 * j, 8 * t, pair))
        for i, z, (a, b) in kept:
            ya[i, z : z + 8, :] = jnp.where(last, b, a)
            ya[i + 1, z : z + 8, :] = jnp.where(last, a, b)
        return 0

    lax.fori_loop(0, ROWS // 2, first_turn, 0)

    def block(old, m, start):
        new = 1 - old
        base = start + 2 * m
        b3, b4 = 3 * base, 4 * base
        waiting = []

        def keep():
            for y, b, i, z, (a, c), edge_lane in waiting.pop(0):
                y[b + i, z : z + 8, :] = jnp.where(edge_lane, c, a)
                y[b + (i + 1), z : z + 8, :] = jnp.where(edge_lane, a, c)

        for row, t in units:
            e, z = row - 2, 8 * t
            turned = [[], []]
            for k in range(2):

                def magnetic(c, r=e, shift=0):
                    return ms[new][k][b3 + (3 * r + c), 8 + z + shift : 16 + z + shift, :]

                def electric(c):
                    return es[old][k][b3 + (3 * e + c), 8 + z : 16 + z, :]

                mx_y = ym[4 * row + k, z : z + 8, :]
                mz_y = ym[4 * row + 2 + k, z : z + 8, :]
                mx, my, mz = magnetic(X), magnetic(Y), magnetic(Z)
                d = ds_[k][base + e, z : z + 8, :]
                g = gs[k][base + e, z : z + 8, :]
                ex = d * electric(X) + g * ((mz - mz_y) - (my - magnetic(Y, e, -1)))
                ey = d * electric(Y) + g * ((mx - magnetic(X, e, -1)) - (mz - magnetic(Z, e - 1)))
                ez = d * electric(Z) + g * ((my - magnetic(Y, e - 1)) - (mx - mx_y))
                for c, v in ((X, ex), (Y, ey), (Z, ez)):
                    es[new][k][b3 + (3 * e + c), 8 + z : 16 + z, :] = v
                turned[0].append(pltpu.roll(ex, 127, 1))
                turned[1].append(pltpu.roll(ez, 127, 1))
            waiting.append(
                [(yes[new], b4, 4 * e + 2 * j, z, turned[j], last) for j in range(2)]
            )
            if len(waiting) > LAG:
                keep()
        for row, t in units:
            z = 8 * t
            turned = [[], []]
            for k in range(2):

                def electric(c, r=row, shift=0):
                    return es[old][k][b3 + (3 * r + c), 8 + z + shift : 16 + z + shift, :]

                def magnetic(c):
                    return ms[old][k][b3 + (3 * row + c), 8 + z : 16 + z, :]

                ex_y = yes[old][b4 + (4 * row + k), z : z + 8, :]
                ez_y = yes[old][b4 + (4 * row + 2 + k), z : z + 8, :]
                ex, ey, ez = electric(X), electric(Y), electric(Z)
                cx = (ez_y - ez) - (electric(Y, row, 1) - ey)
                cy = (electric(X, row, 1) - ex) - (electric(Z, row + 1) - ez)
                cz = (electric(Y, row + 1) - ey) - (ex_y - ex)
                if t == halo and not upper:
                    cx, cy, cz = cx * live, cy * live, cz * live
                mx, my, mz = magnetic(X) - cx, magnetic(Y) - cy, magnetic(Z) - cz
                for c, v in ((X, mx), (Y, my), (Z, mz)):
                    ms[new][k][b3 + (3 * row + c), 8 + z : 16 + z, :] = v
                turned[0].append(pltpu.roll(mx, 1, 1))
                turned[1].append(pltpu.roll(mz, 1, 1))
            waiting.append([(ym, 0, 4 * row + 2 * j, z, turned[j], first_lane) for j in range(2)])
            if len(waiting) > LAG:
                keep()
        while waiting:
            keep()
        return start

    def two_steps(s, _):
        for old in range(2):
            left = STEPS - 1 - old - 2 * s
            lax.fori_loop(0, W + left, functools.partial(block, old), BASE + W - left - 2)
        return 0

    lax.fori_loop(0, STEPS // 2, two_steps, 0)

    def emit(r, _):
        for c, source in enumerate((X, Y, Z)):
            for t in range(ON):
                stage[c, pl.ds(64 * t + r, 8, stride=8), :] = ea0[
                    3 * (r + BASE + W) + source, 16 + 8 * t : 24 + 8 * t, :
                ]
        return 0

    lax.fori_loop(0, 8, emit, 0)
    if upper:
        plane[0] = stage[0, 64 * ON - 8 : 64 * ON, :]
        plane[1] = stage[1, 64 * ON - 8 : 64 * ON, :]
    copy_all([(stage, out.at[:, pl.ds(64 * ON if upper else 0, 64 * ON)])], sems)


def run_steps(upper, decay, gain, sides, arrays):
    smem = pl.BlockSpec(memory_space=pltpu.SMEM)
    out_shape = [jax.ShapeDtypeStruct((3, 640, 128), F32)]
    out_specs = [HBM]
    aliases = {}
    if upper:
        out_shape.append(jax.ShapeDtypeStruct((2, 8, 128), F32))
        out_specs.append(LOCAL)
    else:
        aliases = {6 + len(arrays) - 1: 0}
    z = 16 + 8 * TILES
    field = pltpu.VMEM((3 * HELD, z, 128), F32)
    table = pltpu.VMEM((HELD, 8 * TILES, 128), F32)
    turned = pltpu.VMEM((4 * HELD, 8 * TILES, 128), F32)
    return pl.pallas_call(
        functools.partial(steps_kernel, upper),
        out_shape=out_shape,
        in_specs=[smem, smem] + [LOCAL] * 4 + [HBM] * len(arrays),
        out_specs=out_specs,
        scratch_shapes=[field] * 8
        + [table] * 4
        + [turned] * 2
        + [
            pltpu.VMEM((8, 8 * TILES, 128), F32),
            pltpu.VMEM((3, 64 * ON, 128), F32),
            pltpu.SemaphoreType.DMA((20,)),
        ],
        input_output_aliases=aliases,
        compiler_params=params(),
        cost_estimate=cost(15),
        name="steps_upper" if upper else "steps_lower",
    )(decay, gain, *sides, *arrays)


def image_kernel(weights, centre, before, after, out, sh, rhs):
    gz = lax.axis_index("gz")
    lane = lax.broadcasted_iota(jnp.int32, (24, 128), 1)
    for q in range(15):
        shift = q - 7
        for c in range(2):
            v = centre[c]
            if shift > 0:
                v = jnp.where(
                    lane >= 128 - shift,
                    pltpu.roll(after[c], 128 - shift, 1),
                    pltpu.roll(v, 128 - shift, 1),
                )
            elif shift < 0:
                v = jnp.where(
                    lane < -shift, pltpu.roll(before[c], -shift, 1), pltpu.roll(v, -shift, 1)
                )
            sh[q, c] = v

    def fill(side):
        for q in range(15):
            for c in range(2):
                for i in range(4):
                    start = 4 * side + 1 + i
                    rhs[16 * q : 16 * q + 16, (4 * c + i) * 128 : (4 * c + i + 1) * 128] = sh[
                        q, c, start : start + 16, :
                    ]

    @pl.when(gz == 0)
    def _():
        fill(0)

    @pl.when(gz == 1)
    def _():
        fill(1)

    amplitude = jnp.dot(
        weights[...],
        rhs[...],
        precision=lax.Precision.HIGHEST,
        preferred_element_type=jnp.float32,
    )
    power = jnp.sum(amplitude * amplitude, axis=0, keepdims=True)
    for i in range(4):
        out[i : i + 1, :] = (
            power[:, i * 128 : (i + 1) * 128] + power[:, (4 + i) * 128 : (5 + i) * 128]
        )


def image_of(weights, centre, before, after):
    return pl.pallas_call(
        image_kernel,
        out_shape=jax.ShapeDtypeStruct((4, 128), jnp.float32),
        in_specs=[pl.BlockSpec(memory_space=pltpu.VMEM)] * 4,
        out_specs=pl.BlockSpec(memory_space=pltpu.VMEM),
        scratch_shapes=[
            pltpu.VMEM((15, 2, 24, 128), jnp.float32),
            pltpu.VMEM((240, 1024), jnp.float32),
        ],
        compiler_params=pltpu.CompilerParams(vmem_limit_bytes=VMEM),
        name="image",
    )(weights, centre, before, after)


def behind(value, *others):
    return lax.optimization_barrier((value, *others))[0]


def on_device(electric, magnetic, material, decay, gain, kernels):
    el = electric.reshape(3, 640, 128)
    mg = magnetic.reshape(3, 640, 128)
    mat = material.reshape(640, 128)
    weights = jnp.pad(
        kernels.transpose(0, 1, 3, 2).reshape(48, 15, 15), ((0, 0), (0, 0), (0, 1))
    ).reshape(48, 240)

    own_u, up_u, down_u, strip_u = pack(CUT, 10, el, mg, mat)
    low_u, high_u = around(up_u, "gx", 1), around(down_u, "gx", -1)
    own_l, up_l, down_l, strip = pack(0, CUT, el, mg, mat, strip_u)
    strips, edge = edges(around(strip, "gy", 1), around(strip, "gy", -1), own_u, own_l)
    strips = strips.reshape(80, 8, 128)
    edge = around(edge, "gz", 1)
    up_c, down_c = corners(strips, edge)
    low_c, high_c = around(up_c, "gx", 1), around(down_c, "gx", -1)
    up_l, down_l = behind((up_l, down_l), up_c)
    low_l, high_l = around(up_l, "gx", 1), around(down_l, "gx", -1)

    sides = [strips, edge, low_c, high_c]
    field, plane = run_steps(True, decay, gain, sides, [own_u, low_u, high_u])
    top = lax.ppermute(plane, "gz", [(1, 0)])
    top = jnp.where(lax.axis_index("gz") == 1, plane, top)
    top = jnp.stack([top, around(top, "gy", 1), around(top, "gy", -1)])
    top = jnp.concatenate([around(top, "gx", 1), top, around(top, "gx", -1)], 2)
    image = image_of(weights, top[0], top[1], top[2])
    (field,) = run_steps(
        False, decay, gain, sides, [own_u, low_u, high_u, own_l, low_l, high_l, field]
    )
    return (field.reshape(3, 80, 8, 128), image)


def solution(mesh):
    in_specs = (
        P(None, "gz", "gx", "gy"),
        P(None, "gz", "gx", "gy"),
        P("gz", "gx", "gy"),
        P(),
        P(),
        P(),
    )
    out_specs = (P(None, "gz", "gx", "gy"), P(("gx", "gz"), "gy"))
    return jax.shard_map(
        on_device, mesh=mesh, in_specs=in_specs, out_specs=out_specs, check_vma=False
    )
```

```python
import functools

import jax
import jax.numpy as jnp
from jax import lax
from jax.experimental import pallas as pl
from jax.experimental.pallas import tpu as pltpu
from jax.sharding import PartitionSpec as P

STEPS = 6
W = STEPS
Y, Z, X = range(3)
NC = 7
SOURCE = ((0, 1), (0, 2), (0, 0), (1, 1), (1, 2), (1, 0))
ROWS = 8 + 2 * W
BASE = 4
HELD = BASE + ROWS + 2
CUT = 4
TILES = 7
ON = 5
LAG = 4
VMEM = 56 * 1024 * 1024
F32 = jnp.float32
HBM = pl.BlockSpec(memory_space=pl.ANY)
LOCAL = pl.BlockSpec(memory_space=pltpu.VMEM)


def around(value, axis, steps):
    count = lax.axis_size(axis)
    return lax.ppermute(value, axis, [(i, (i + steps) % count) for i in range(count)])


def copy_all(pairs, sems):
    copies = [pltpu.make_async_copy(a, b, sems.at[i]) for i, (a, b) in enumerate(pairs)]
    for copy in copies:
        copy.start()
    for copy in copies:
        copy.wait()


def params():
    return pltpu.CompilerParams(vmem_limit_bytes=VMEM)


def cost(us):
    return pl.CostEstimate(flops=0, bytes_accessed=int(us * 3e6), transcendentals=0)


def pack_kernel(ta, tb, el, mg, mat, *refs):
    own, up, down, strip, ext, matv, planes, strips, sems = refs
    tiles = tb - ta
    rows = pl.ds(64 * ta, 64 * tiles)
    loads = [(mat.at[rows], matv)]
    for c, (which, comp) in enumerate(SOURCE):
        loads.append(((el, mg)[which].at[comp, rows], ext.at[c]))
    copy_all(loads, sems)

    masks = strip_masks()

    def row(r, _):
        for t in range(tiles):
            z = 8 * t
            total = None
            for c in range(NC):
                if c == 6:
                    v = matv[pl.ds(64 * t + r, 8, stride=8), :].astype(F32)
                    planes[48 + r, z : z + 8, :] = v
                else:
                    v = ext[c, pl.ds(64 * t + r, 8, stride=8), :]
                    if c >= 3:
                        v = v * 2.0
                    planes[24 * (c // 3) + 3 * r + c % 3, z : z + 8, :] = v
                turned = pltpu.roll(v, 16 * c, 1) if c else v
                total = jnp.where(masks[c], turned, total) if c else v
            strips[r, z : z + 8, :] = total
        return 0

    lax.fori_loop(0, 8, row, 0)
    pairs = [(planes, own)]
    pairs += [
        (planes.at[pl.ds(a, n)], up.at[pl.ds(b, n)])
        for a, b, n in ((6, 0, 18), (30, 18, 2), (33, 20, 15), (51, 35, 5))
    ]
    pairs += [
        (planes.at[pl.ds(a, n)], down.at[pl.ds(b, n)])
        for a, b, n in ((0, 0, 17), (24, 17, 15), (48, 32, 5))
    ]
    pairs.append((strips, strip))
    copy_all(pairs, sems)


def pack(ta, tb, el, mg, mat):
    layers = 8 * (tb - ta)
    return pl.pallas_call(
        functools.partial(pack_kernel, ta, tb),
        out_shape=[
            jax.ShapeDtypeStruct((8 * NC, layers, 128), F32),
            jax.ShapeDtypeStruct((40, layers, 128), F32),
            jax.ShapeDtypeStruct((37, layers, 128), F32),
            jax.ShapeDtypeStruct((8, layers, 128), F32),
        ],
        in_specs=[HBM] * 3,
        out_specs=[HBM] * 4,
        scratch_shapes=[
            pltpu.VMEM((6, 8 * layers, 128), F32),
            pltpu.VMEM((8 * layers, 128), jnp.int32),
            pltpu.VMEM((8 * NC, layers, 128), F32),
            pltpu.VMEM((8, layers, 128), F32),
            pltpu.SemaphoreType.DMA((10,)),
        ],
        compiler_params=params(),
        cost_estimate=cost(3),
        name="pack_upper" if ta else "pack_lower",
    )(el, mg, mat)


def edge_kernel(el, mg, mat, edge, ext, matv, sems):
    gz = lax.axis_index("gz")

    def load(first):
        rows = pl.ds(64 * first, 64)
        loads = [(mat.at[rows], matv)]
        for c, (which, comp) in enumerate(SOURCE):
            loads.append(((el, mg)[which].at[comp, rows], ext.at[c]))
        copy_all(loads, sems)

    @pl.when(gz == 0)
    def _():
        load(9)

    @pl.when(gz == 1)
    def _():
        load(0)

    for r in range(8):
        for c in range(6):
            v = ext[c, pl.ds(r, 8, stride=8), :]
            edge[24 * (c // 3) + 3 * r + c % 3] = v * 2.0 if c >= 3 else v
        edge[48 + r] = matv[pl.ds(r, 8, stride=8), :].astype(F32)


def edge_layers(el, mg, mat):
    return pl.pallas_call(
        edge_kernel,
        out_shape=jax.ShapeDtypeStruct((56, 8, 128), F32),
        in_specs=[HBM] * 3,
        out_specs=LOCAL,
        scratch_shapes=[
            pltpu.VMEM((6, 64, 128), F32),
            pltpu.VMEM((64, 128), jnp.int32),
            pltpu.SemaphoreType.DMA((7,)),
        ],
        compiler_params=params(),
        cost_estimate=cost(1),
        name="edge_layers",
    )(el, mg, mat)


def strip_masks():
    lane = lax.broadcasted_iota(jnp.int32, (8, 128), 1)
    return [((lane - 16 * c + W + 128) % 128) < 2 * W for c in range(NC)]


def strip_kernel(strip_l, strip_u, edge, out):
    masks = strip_masks()
    for r in range(8):
        for t in range(10):
            at = 8 * t
            out[11 * r + t] = (
                strip_l[r, at : at + 8, :]
                if t < CUT
                else strip_u[r, at - 8 * CUT : at - 8 * CUT + 8, :]
            )
        total = edge[3 * r]
        for c in range(1, NC):
            v = edge[48 + r] if c == 6 else edge[24 * (c // 3) + 3 * r + c % 3]
            total = jnp.where(masks[c], pltpu.roll(v, 16 * c, 1), total)
        out[11 * r + 10] = total


def own_strips(strip_l, strip_u, edge):
    return pl.pallas_call(
        strip_kernel,
        out_shape=jax.ShapeDtypeStruct((88, 8, 128), F32),
        in_specs=[LOCAL] * 3,
        out_specs=LOCAL,
        compiler_params=params(),
        cost_estimate=cost(1),
        name="own_strips",
    )(strip_l, strip_u, edge)


def corner_kernel(from_low, from_high, edge, strips, up, down):
    lane = lax.broadcasted_iota(jnp.int32, (88, 8, 128), 2)
    strips[...] = jnp.where(lane % 16 < 8, from_high[...], from_low[...])
    for a, b, n in ((6, 0, 18), (30, 18, 2), (33, 20, 15), (51, 35, 5)):
        up[b : b + n] = edge[a : a + n]
    for a, b, n in ((0, 0, 17), (24, 17, 15), (48, 32, 5)):
        down[b : b + n] = edge[a : a + n]
    up[40:106] = strips[22:88]
    down[37:103] = strips[0:66]


def corners(from_low, from_high, edge):
    return pl.pallas_call(
        corner_kernel,
        out_shape=[
            jax.ShapeDtypeStruct((88, 8, 128), F32),
            jax.ShapeDtypeStruct((106, 8, 128), F32),
            jax.ShapeDtypeStruct((103, 8, 128), F32),
        ],
        in_specs=[LOCAL] * 3,
        out_specs=[LOCAL] * 3,
        compiler_params=params(),
        cost_estimate=cost(1),
        name="corners",
    )(from_low, from_high, edge)


def steps_kernel(upper, decay, gain, strips, edge, low_c, high_c, *refs):
    gz = lax.axis_index("gz")
    if upper:
        own_u, low_u, high_u, out, plane, *scratch = refs
        sets = [((own_u, low_u, high_u), 8 * (10 - CUT), 0)]
        halo, counts = TILES - 1, gz == 0
        held = [(t, t + CUT) for t in range(TILES - 1)]
    else:
        own_u, low_u, high_u, own_l, low_l, high_l, _, out, *scratch = refs
        sets = [
            ((own_l, low_l, high_l), 8 * CUT, 8),
            ((own_u, low_u, high_u), 8 * (TILES - 1 - CUT), 8 + 8 * CUT),
        ]
        halo, counts = 0, gz == 1
        held = [(t, t - 1) for t in range(1, TILES)]
    ea0, ea1, eb0, eb1, ma0, ma1, mb0, mb1, d0, d1, g0, g1, ya, yb, ym, stage, sems = scratch
    es, ms, yes = ((ea0, ea1), (eb0, eb1)), ((ma0, ma1), (mb0, mb1)), (ya, yb)
    ds_, gs = (d0, d1), (g0, g1)

    moves = []
    for (own, low, high), layers, to in sets:
        src, zf, zd = pl.ds(0, layers), pl.ds(8 + to, layers), pl.ds(to, layers)
        first, mid, last_ = BASE, BASE + W, BASE + W + 8
        for ref, a, n, dst, b, z in (
            (own, 0, 24, ea0, 3 * mid, zf),
            (own, 24, 24, ma0, 3 * mid, zf),
            (own, 48, 8, d0, mid, zd),
            (low, 0, 18, ea0, 3 * first, zf),
            (low, 18, 2, ma0, 3 * first, zf),
            (low, 20, 15, ma0, 3 * first + 3, zf),
            (low, 35, 5, d0, first + 1, zd),
            (high, 0, 17, ea0, 3 * last_, zf),
            (high, 17, 15, ma0, 3 * last_, zf),
            (high, 32, 5, d0, last_, zd),
        ):
            moves.append((ref.at[pl.ds(a, n), src], dst.at[pl.ds(b, n), z]))
    copies = [pltpu.make_async_copy(a, b, sems.at[i]) for i, (a, b) in enumerate(moves)]
    for copy in copies:
        copy.start()

    zero = jnp.zeros((8, 128), F32)
    top = 8 + 8 * TILES

    def unpack(ref, first, count, row):
        def body(r, _):
            at = BASE + row + r
            for t, tile in held + [(halo, 10)]:
                v = ref[first + 11 * r + tile]
                z = 8 * t
                for c in range(NC):
                    turned = pltpu.roll(v, 128 - 16 * c, 1) if c else v
                    if c < 3:
                        ea1[3 * at + c, 8 + z : 16 + z, :] = turned
                    elif c < 6:
                        ma1[3 * at + c - 3, 8 + z : 16 + z, :] = turned
                    else:
                        d1[at, z : z + 8, :] = turned
            return 0

        lax.fori_loop(0, count, body, 0)

    unpack(low_c, 40, W, 0)
    unpack(strips, 0, 8, W)
    unpack(high_c, 37, W, W + 8)

    def ends(r, _):
        for pair in ms:
            for m in pair:
                m[3 * r + X, 0:8, :] = zero
                m[3 * r + Y, 0:8, :] = zero
        for pair in es:
            for e in pair:
                e[3 * r + X, top : top + 8, :] = zero
                e[3 * r + Y, top : top + 8, :] = zero
        return 0

    lax.fori_loop(0, HELD, ends, 0)
    hz = 8 * halo

    @pl.when(counts)
    def _():
        for ref, a, n, dst, b, to in (
            (edge, 0, 24, ea0, 3 * (BASE + W), 8),
            (edge, 24, 24, ma0, 3 * (BASE + W), 8),
            (edge, 48, 8, d0, BASE + W, 0),
            (low_c, 0, 18, ea0, 3 * BASE, 8),
            (low_c, 18, 2, ma0, 3 * BASE, 8),
            (low_c, 20, 15, ma0, 3 * BASE + 3, 8),
            (low_c, 35, 5, d0, BASE + 1, 0),
            (high_c, 0, 17, ea0, 3 * (BASE + W + 8), 8),
            (high_c, 17, 15, ma0, 3 * (BASE + W + 8), 8),
            (high_c, 32, 5, d0, BASE + W + 8, 0),
        ):
            for i in range(n):
                dst[b + i, hz + to : hz + to + 8, :] = ref[a + i]

    @pl.when(jnp.logical_not(counts))
    def _():
        def clear(i, _):
            for ref in (ea0, ea1, ma0, ma1):
                ref[3 * BASE + i, hz + 8 : hz + 16, :] = zero
            return 0

        lax.fori_loop(0, 3 * ROWS, clear, 0)

    for copy in copies:
        copy.wait()

    live = jnp.where(counts, 1.0, 0.0).astype(F32)

    def tables(r, _):
        for t in range(TILES):
            z = 8 * t
            for d, g in zip(ds_, gs):
                ids = d[r, z : z + 8, :]
                d_cells, g_cells = zero, zero
                for i in range(5):
                    hit = ids == float(i)
                    d_cells = jnp.where(hit, decay[i], d_cells)
                    g_cells = jnp.where(hit, gain[i] * 0.5, g_cells)
                if t == halo:
                    d_cells, g_cells = d_cells * live, g_cells * live
                d[r, z : z + 8, :] = d_cells
                g[r, z : z + 8, :] = g_cells
        return 0

    lax.fori_loop(BASE + 1, BASE + ROWS - 1, tables, 0)

    lane = lax.broadcasted_iota(jnp.int32, (8, 128), 1)
    last, first_lane = lane == 127, lane == 0
    units = [(row, t) for row in range(2) for t in range(TILES)]

    def first_turn(i, _):
        kept = []
        for row, t in units:
            r = BASE + 2 * i + row
            for j, c in enumerate((X, Z)):
                pair = [pltpu.roll(e[3 * r + c, 8 + 8 * t : 16 + 8 * t, :], 127, 1) for e in es[0]]
                kept.append((4 * r + 2 * j, 8 * t, pair))
        for i, z, (a, b) in kept:
            ya[i, z : z + 8, :] = jnp.where(last, b, a)
            ya[i + 1, z : z + 8, :] = jnp.where(last, a, b)
        return 0

    lax.fori_loop(0, ROWS // 2, first_turn, 0)

    def block(old, m, start):
        new = 1 - old
        base = start + 2 * m
        b3, b4 = 3 * base, 4 * base
        waiting = []

        def keep():
            for y, b, i, z, (a, c), edge_lane in waiting.pop(0):
                y[b + i, z : z + 8, :] = jnp.where(edge_lane, c, a)
                y[b + (i + 1), z : z + 8, :] = jnp.where(edge_lane, a, c)

        for row, t in units:
            e, z = row - 2, 8 * t
            turned = [[], []]
            for k in range(2):

                def magnetic(c, r=e, shift=0):
                    return ms[new][k][b3 + (3 * r + c), 8 + z + shift : 16 + z + shift, :]

                def electric(c):
                    return es[old][k][b3 + (3 * e + c), 8 + z : 16 + z, :]

                mx_y = ym[4 * row + k, z : z + 8, :]
                mz_y = ym[4 * row + 2 + k, z : z + 8, :]
                mx, my, mz = magnetic(X), magnetic(Y), magnetic(Z)
                d = ds_[k][base + e, z : z + 8, :]
                g = gs[k][base + e, z : z + 8, :]
                ex = d * electric(X) + g * ((mz - mz_y) - (my - magnetic(Y, e, -1)))
                ey = d * electric(Y) + g * ((mx - magnetic(X, e, -1)) - (mz - magnetic(Z, e - 1)))
                ez = d * electric(Z) + g * ((my - magnetic(Y, e - 1)) - (mx - mx_y))
                for c, v in ((X, ex), (Y, ey), (Z, ez)):
                    es[new][k][b3 + (3 * e + c), 8 + z : 16 + z, :] = v
                turned[0].append(pltpu.roll(ex, 127, 1))
                turned[1].append(pltpu.roll(ez, 127, 1))
            waiting.append(
                [(yes[new], b4, 4 * e + 2 * j, z, turned[j], last) for j in range(2)]
            )
            if len(waiting) > LAG:
                keep()
        for row, t in units:
            z = 8 * t
            turned = [[], []]
            for k in range(2):

                def electric(c, r=row, shift=0):
                    return es[old][k][b3 + (3 * r + c), 8 + z + shift : 16 + z + shift, :]

                def magnetic(c):
                    return ms[old][k][b3 + (3 * row + c), 8 + z : 16 + z, :]

                ex_y = yes[old][b4 + (4 * row + k), z : z + 8, :]
                ez_y = yes[old][b4 + (4 * row + 2 + k), z : z + 8, :]
                ex, ey, ez = electric(X), electric(Y), electric(Z)
                cx = (ez_y - ez) - (electric(Y, row, 1) - ey)
                cy = (electric(X, row, 1) - ex) - (electric(Z, row + 1) - ez)
                cz = (electric(Y, row + 1) - ey) - (ex_y - ex)
                if t == halo and not upper:
                    cx, cy, cz = cx * live, cy * live, cz * live
                mx, my, mz = magnetic(X) - cx, magnetic(Y) - cy, magnetic(Z) - cz
                for c, v in ((X, mx), (Y, my), (Z, mz)):
                    ms[new][k][b3 + (3 * row + c), 8 + z : 16 + z, :] = v
                turned[0].append(pltpu.roll(mx, 1, 1))
                turned[1].append(pltpu.roll(mz, 1, 1))
            waiting.append([(ym, 0, 4 * row + 2 * j, z, turned[j], first_lane) for j in range(2)])
            if len(waiting) > LAG:
                keep()
        while waiting:
            keep()
        return start

    def two_steps(s, _):
        for old in range(2):
            left = STEPS - 1 - old - 2 * s
            lax.fori_loop(0, W + left, functools.partial(block, old), BASE + W - left - 2)
        return 0

    lax.fori_loop(0, STEPS // 2, two_steps, 0)

    def emit(r, _):
        for c, source in enumerate((X, Y, Z)):
            for t in range(ON):
                stage[c, pl.ds(64 * t + r, 8, stride=8), :] = ea0[
                    3 * (r + BASE + W) + source, 16 + 8 * t : 24 + 8 * t, :
                ]
        return 0

    lax.fori_loop(0, 8, emit, 0)
    if upper:
        plane[0] = stage[0, 64 * ON - 8 : 64 * ON, :]
        plane[1] = stage[1, 64 * ON - 8 : 64 * ON, :]
    copy_all([(stage, out.at[:, pl.ds(64 * ON if upper else 0, 64 * ON)])], sems)


def run_steps(upper, decay, gain, sides, arrays):
    smem = pl.BlockSpec(memory_space=pltpu.SMEM)
    out_shape = [jax.ShapeDtypeStruct((3, 640, 128), F32)]
    out_specs = [HBM]
    aliases = {}
    if upper:
        out_shape.append(jax.ShapeDtypeStruct((2, 8, 128), F32))
        out_specs.append(LOCAL)
    else:
        aliases = {6 + len(arrays) - 1: 0}
    z = 16 + 8 * TILES
    field = pltpu.VMEM((3 * HELD, z, 128), F32)
    table = pltpu.VMEM((HELD, 8 * TILES, 128), F32)
    turned = pltpu.VMEM((4 * HELD, 8 * TILES, 128), F32)
    return pl.pallas_call(
        functools.partial(steps_kernel, upper),
        out_shape=out_shape,
        in_specs=[smem, smem] + [LOCAL] * 4 + [HBM] * len(arrays),
        out_specs=out_specs,
        scratch_shapes=[field] * 8
        + [table] * 4
        + [turned] * 2
        + [
            pltpu.VMEM((8, 8 * TILES, 128), F32),
            pltpu.VMEM((3, 64 * ON, 128), F32),
            pltpu.SemaphoreType.DMA((20,)),
        ],
        input_output_aliases=aliases,
        compiler_params=params(),
        cost_estimate=cost(15),
        name="steps_upper" if upper else "steps_lower",
    )(decay, gain, *sides, *arrays)


def image_kernel(weights, centre, before, after, out, sh, rhs):
    gz = lax.axis_index("gz")
    lane = lax.broadcasted_iota(jnp.int32, (24, 128), 1)
    for q in range(15):
        shift = q - 7
        for c in range(2):
            v = centre[c]
            if shift > 0:
                v = jnp.where(
                    lane >= 128 - shift,
                    pltpu.roll(after[c], 128 - shift, 1),
                    pltpu.roll(v, 128 - shift, 1),
                )
            elif shift < 0:
                v = jnp.where(
                    lane < -shift, pltpu.roll(before[c], -shift, 1), pltpu.roll(v, -shift, 1)
                )
            sh[q, c] = v

    def fill(side):
        for q in range(15):
            for c in range(2):
                for i in range(4):
                    start = 4 * side + 1 + i
                    rhs[16 * q : 16 * q + 16, (4 * c + i) * 128 : (4 * c + i + 1) * 128] = sh[
                        q, c, start : start + 16, :
                    ]

    @pl.when(gz == 0)
    def _():
        fill(0)

    @pl.when(gz == 1)
    def _():
        fill(1)

    amplitude = jnp.dot(
        weights[...],
        rhs[...],
        precision=lax.Precision.HIGHEST,
        preferred_element_type=jnp.float32,
    )
    power = jnp.sum(amplitude * amplitude, axis=0, keepdims=True)
    for i in range(4):
        out[i : i + 1, :] = (
            power[:, i * 128 : (i + 1) * 128] + power[:, (4 + i) * 128 : (5 + i) * 128]
        )


def image_of(weights, centre, before, after):
    return pl.pallas_call(
        image_kernel,
        out_shape=jax.ShapeDtypeStruct((4, 128), jnp.float32),
        in_specs=[pl.BlockSpec(memory_space=pltpu.VMEM)] * 4,
        out_specs=pl.BlockSpec(memory_space=pltpu.VMEM),
        scratch_shapes=[
            pltpu.VMEM((15, 2, 24, 128), jnp.float32),
            pltpu.VMEM((240, 1024), jnp.float32),
        ],
        compiler_params=pltpu.CompilerParams(vmem_limit_bytes=VMEM),
        name="image",
    )(weights, centre, before, after)


def on_device(electric, magnetic, material, decay, gain, kernels):
    el = electric.reshape(3, 640, 128)
    mg = magnetic.reshape(3, 640, 128)
    mat = material.reshape(640, 128)
    weights = jnp.pad(
        kernels.transpose(0, 1, 3, 2).reshape(48, 15, 15), ((0, 0), (0, 0), (0, 1))
    ).reshape(48, 240)

    edge = around(edge_layers(el, mg, mat), "gz", 1)
    own_u, up_u, down_u, strip_u = pack(CUT, 10, el, mg, mat)
    low_u, high_u = around(up_u, "gx", 1), around(down_u, "gx", -1)
    own_l, up_l, down_l, strip_l = pack(0, CUT, el, mg, mat)
    strips = own_strips(strip_l, strip_u, edge)
    from_low, from_high = around(strips, "gy", 1), around(strips, "gy", -1)
    from_low, from_high, low_u, high_u = lax.optimization_barrier(
        (from_low, from_high, low_u, high_u)
    )
    strips, up_c, down_c = corners(from_low, from_high, edge)
    low_c, high_c = around(up_c, "gx", 1), around(down_c, "gx", -1)
    up_l, down_l, low_c, high_c = lax.optimization_barrier((up_l, down_l, low_c, high_c))
    low_l, high_l = around(up_l, "gx", 1), around(down_l, "gx", -1)

    sides = [strips, edge, low_c, high_c]
    field, plane = run_steps(True, decay, gain, sides, [own_u, low_u, high_u])
    plane, low_l, high_l = lax.optimization_barrier((plane, low_l, high_l))
    top = lax.ppermute(plane, "gz", [(1, 0)])
    top = jnp.where(lax.axis_index("gz") == 1, plane, top)
    top = jnp.stack([top, around(top, "gy", 1), around(top, "gy", -1)])
    top = jnp.concatenate([around(top, "gx", 1), top, around(top, "gx", -1)], 2)
    image = image_of(weights, top[0], top[1], top[2])
    (field,) = run_steps(
        False, decay, gain, sides, [own_u, low_u, high_u, own_l, low_l, high_l, field]
    )
    return (field.reshape(3, 80, 8, 128), image)


def solution(mesh):
    in_specs = (
        P(None, "gz", "gx", "gy"),
        P(None, "gz", "gx", "gy"),
        P("gz", "gx", "gy"),
        P(),
        P(),
        P(),
    )
    out_specs = (P(None, "gz", "gx", "gy"), P(("gx", "gz"), "gy"))
    return jax.shard_map(
        on_device, mesh=mesh, in_specs=in_specs, out_specs=out_specs, check_vma=False
    )
```

```python
import functools

import jax
import jax.numpy as jnp
from jax import lax
from jax.experimental import pallas as pl
from jax.experimental.pallas import tpu as pltpu
from jax.sharding import PartitionSpec as P

STEPS = 6
W = STEPS
Y, Z, X = range(3)
NC = 7
SOURCE = ((0, 1), (0, 2), (0, 0), (1, 1), (1, 2), (1, 0))
ROWS = 8 + 2 * W
BASE = 4
HELD = BASE + ROWS + 2
CUT = 6
LAG = 4
VMEM = 56 * 1024 * 1024
F32 = jnp.float32
HBM = pl.BlockSpec(memory_space=pl.ANY)
LOCAL = pl.BlockSpec(memory_space=pltpu.VMEM)


def around(value, axis, steps):
    count = lax.axis_size(axis)
    return lax.ppermute(value, axis, [(i, (i + steps) % count) for i in range(count)])


def beyond(value, steps):
    ny, nz = lax.axis_size("gy"), lax.axis_size("gz")
    pairs = [
        (y * nz + z, (y + steps) % ny * nz + (z + 1) % nz) for y in range(ny) for z in range(nz)
    ]
    return lax.ppermute(value, ("gy", "gz"), pairs)


def copy_all(pairs, sems):
    copies = [pltpu.make_async_copy(a, b, sems.at[i]) for i, (a, b) in enumerate(pairs)]
    for copy in copies:
        copy.start()
    for copy in copies:
        copy.wait()


def params():
    return pltpu.CompilerParams(vmem_limit_bytes=VMEM)


def cost(us):
    return pl.CostEstimate(flops=0, bytes_accessed=int(us * 3e6), transcendentals=0)


def plane_of(r, c):
    return 48 + r if c == 6 else 24 * (c // 3) + 3 * r + c % 3


def strip_masks():
    lane = lax.broadcasted_iota(jnp.int32, (8, 128), 1)
    return [((lane - 16 * c + W + 128) % 128) < 2 * W for c in range(NC)]


def strip_kernel(el, mg, mat, strips, edge, edge_strips, ext, matv, sems):
    gz = lax.axis_index("gz")
    loads = [(mat, matv)]
    for c, (which, comp) in enumerate(SOURCE):
        loads.append(((el, mg)[which].at[comp], ext.at[c]))
    copy_all(loads, sems)
    masks = strip_masks()

    def layers(c, t, r):
        rows = pl.ds(64 * t + r, 8, stride=8)
        if c == 6:
            return matv[rows, :].astype(F32)
        v = ext[c, rows, :]
        return v * 2.0 if c >= 3 else v

    def row(r, _):
        for t in range(10):
            total = layers(0, t, r)
            for c in range(1, NC):
                total = jnp.where(masks[c], pltpu.roll(layers(c, t, r), 16 * c, 1), total)
            strips[r, 8 * t : 8 * t + 8, :] = total
        return 0

    lax.fori_loop(0, 8, row, 0)

    def edges(t):
        for r in range(8):
            for c in range(NC):
                edge[plane_of(r, c)] = layers(c, t, r)
        edge_strips[...] = strips[:, 8 * t : 8 * t + 8, :]

    @pl.when(gz == 0)
    def _():
        edges(9)

    @pl.when(gz == 1)
    def _():
        edges(0)


def own_strips(el, mg, mat):
    return pl.pallas_call(
        strip_kernel,
        out_shape=[
            jax.ShapeDtypeStruct((8, 80, 128), F32),
            jax.ShapeDtypeStruct((8 * NC, 8, 128), F32),
            jax.ShapeDtypeStruct((8, 8, 128), F32),
        ],
        in_specs=[HBM] * 3,
        out_specs=[LOCAL] * 3,
        scratch_shapes=[
            pltpu.VMEM((6, 640, 128), F32),
            pltpu.VMEM((640, 128), jnp.int32),
            pltpu.SemaphoreType.DMA((7,)),
        ],
        compiler_params=params(),
        cost_estimate=cost(3),
        name="own_strips",
    )(el, mg, mat)


def pack_kernel(el, mg, mat, own_u, up_u, down_u, own_l, up_l, down_l, ext, matv, planes, sems):
    loads = [(mat, matv)]
    for c, (which, comp) in enumerate(SOURCE):
        loads.append(((el, mg)[which].at[comp], ext.at[c]))
    copy_all(loads, sems)

    def rows_of(first, last):
        def row(r, _):
            for t in range(first, last):
                rows = pl.ds(64 * t + r, 8, stride=8)
                for c in range(NC):
                    if c == 6:
                        v = matv[rows, :].astype(F32)
                    else:
                        v = ext[c, rows, :]
                        if c >= 3:
                            v = v * 2.0
                    planes[plane_of(r, c), 8 * t : 8 * t + 8, :] = v
            return 0

        lax.fori_loop(0, 8, row, 0)

    def sends(first, last, own, up, down):
        z, to = pl.ds(8 * first, 8 * (last - first)), pl.ds(0, 8 * (last - first))
        pairs = [(planes.at[:, z], own)]
        for a, b, n in ((6, 0, 18), (30, 18, 2), (33, 20, 15), (51, 35, 5)):
            pairs.append((planes.at[pl.ds(a, n), z], up.at[pl.ds(b, n), to]))
        for a, b, n in ((0, 0, 17), (24, 17, 15), (48, 32, 5)):
            pairs.append((planes.at[pl.ds(a, n), z], down.at[pl.ds(b, n), to]))
        return pairs

    rows_of(CUT, 10)
    pairs = sends(CUT, 10, own_u, up_u, down_u)
    upper = [pltpu.make_async_copy(a, b, sems.at[i]) for i, (a, b) in enumerate(pairs)]
    for copy in upper:
        copy.start()
    rows_of(0, CUT)
    pairs = sends(0, CUT, own_l, up_l, down_l)
    lower = [pltpu.make_async_copy(a, b, sems.at[8 + i]) for i, (a, b) in enumerate(pairs)]
    for copy in lower:
        copy.start()
    for copy in upper + lower:
        copy.wait()


def pack(el, mg, mat):
    shapes = []
    for layers, more in ((8 * (10 - CUT), 8), (8 * CUT, 0)):
        shapes += [
            jax.ShapeDtypeStruct((8 * NC, layers, 128), F32),
            jax.ShapeDtypeStruct((40 + W, layers + more, 128), F32),
            jax.ShapeDtypeStruct((37 + W, layers + more, 128), F32),
        ]
    return pl.pallas_call(
        pack_kernel,
        out_shape=shapes,
        in_specs=[HBM] * 3,
        out_specs=[HBM] * 6,
        scratch_shapes=[
            pltpu.VMEM((6, 640, 128), F32),
            pltpu.VMEM((640, 128), jnp.int32),
            pltpu.VMEM((8 * NC, 80, 128), F32),
            pltpu.SemaphoreType.DMA((16,)),
        ],
        compiler_params=params(),
        cost_estimate=cost(5),
        name="pack",
    )(el, mg, mat)


def fill_kernel(from_low, from_high, edge_low, edge_high, edge, *refs):
    strips, up_u, down_u, up_l, down_l, halo, sems = refs[4:]
    lane = lax.broadcasted_iota(jnp.int32, (8, 80, 128), 2)
    halo[:, 0:80, :] = jnp.where(lane % 16 < 8, from_high[...], from_low[...])
    lane = lax.broadcasted_iota(jnp.int32, (8, 8, 128), 2)
    halo[:, 80:88, :] = jnp.where(lane % 16 < 8, edge_high[...], edge_low[...])
    nu, nl = 8 * (10 - CUT), 8 * CUT
    pairs = [(halo, strips)]
    for message, first, count, parts in (
        (up_u, 8 - W, 40, ((6, 0, 18), (30, 18, 2), (33, 20, 15), (51, 35, 5))),
        (down_u, 0, 37, ((0, 0, 17), (24, 17, 15), (48, 32, 5))),
    ):
        rows = pl.ds(first, W)
        pairs.append(
            (halo.at[rows, pl.ds(nl, nu + 8)], message.at[pl.ds(count, W), pl.ds(0, nu + 8)])
        )
        for a, b, n in parts:
            pairs.append((edge.at[pl.ds(a, n)], message.at[pl.ds(b, n), pl.ds(nu, 8)]))
    for message, first, count in ((up_l, 8 - W, 40), (down_l, 0, 37)):
        pairs.append((halo.at[pl.ds(first, W), pl.ds(0, nl)], message.at[pl.ds(count, W)]))
    copy_all(pairs, sems)


def fill(from_low, from_high, edge_low, edge_high, edge, messages):
    shapes = [jax.ShapeDtypeStruct((8, 88, 128), F32)]
    shapes += [jax.ShapeDtypeStruct(m.shape, F32) for m in messages]
    return pl.pallas_call(
        fill_kernel,
        out_shape=shapes,
        in_specs=[LOCAL] * 5 + [HBM] * 4,
        out_specs=[HBM] * 5,
        scratch_shapes=[pltpu.VMEM((8, 88, 128), F32), pltpu.SemaphoreType.DMA((12,))],
        input_output_aliases={5 + i: 1 + i for i in range(4)},
        compiler_params=params(),
        cost_estimate=cost(1),
        name="fill",
    )(from_low, from_high, edge_low, edge_high, edge, *messages)


def steps_kernel(upper, decay, gain, strips, edge, *refs):
    gz = lax.axis_index("gz")
    nu, nl = 8 * (10 - CUT), 8 * CUT
    own_u, low_u, high_u = refs[:3]
    if upper:
        out, plane, *scratch = refs[3:]
        tiles, halo, counts = 11 - CUT, 10 - CUT, gz == 0
        sets = [((own_u, low_u, high_u), 0, nu, 0, nl)]
    else:
        own_l, low_l, high_l, _, out, *scratch = refs[3:]
        tiles, halo, counts = CUT + 3, 0, gz == 1
        sets = [
            ((own_l, low_l, high_l), 0, nl, 8, 0),
            ((own_u, low_u, high_u), 0, 16, 8 + nl, nl),
        ]
    on = 9 - CUT if upper else CUT + 1
    sets.append(((edge, low_u, high_u), nu, 8, 8 * halo, 80))
    ea0, ea1, eb0, eb1, ma0, ma1, mb0, mb1, d0, d1, g0, g1, ya, yb, ym, sv, stage, sems = scratch
    es, ms, yes = ((ea0, ea1), (eb0, eb1)), ((ma0, ma1), (mb0, mb1)), (ya, yb)
    ds_, gs = (d0, d1), (g0, g1)

    first, mid, last_ = BASE, BASE + W, BASE + W + 8
    groups = []
    for (own, low, high), start, layers, to, strip in sets:
        src, zf, zd = pl.ds(start, layers), pl.ds(8 + to, layers), pl.ds(to, layers)
        mine = pl.ds(0, 8) if own is edge else src
        moves = [
            (strips.at[:, pl.ds(strip, layers)], sv.at[pl.ds(W, 8), zd]),
            (low.at[pl.ds(40, W), src], sv.at[pl.ds(0, W), zd]),
            (high.at[pl.ds(37, W), src], sv.at[pl.ds(W + 8, W), zd]),
        ]
        for ref, a, n, dst, b, z in (
            (own, 0, 24, ea0, 3 * mid, zf),
            (own, 24, 24, ma0, 3 * mid, zf),
            (own, 48, 8, d0, mid, zd),
            (low, 0, 18, ea0, 3 * first, zf),
            (low, 18, 2, ma0, 3 * first, zf),
            (low, 20, 15, ma0, 3 * first + 3, zf),
            (low, 35, 5, d0, first + 1, zd),
            (high, 0, 17, ea0, 3 * last_, zf),
            (high, 17, 15, ma0, 3 * last_, zf),
            (high, 32, 5, d0, last_, zd),
        ):
            moves.append((ref.at[pl.ds(a, n), mine if ref is own else src], dst.at[pl.ds(b, n), z]))
        groups.append(moves)
    copies = []
    for moves in groups:
        for a, b in moves:
            copies.append(pltpu.make_async_copy(a, b, sems.at[len(copies)]))
    for copy in copies:
        copy.start()

    zero = jnp.zeros((8, 128), F32)
    top = 8 + 8 * tiles

    def ends(r, _):
        for pair in ms:
            for m in pair:
                m[3 * r + X, 0:8, :] = zero
                m[3 * r + Y, 0:8, :] = zero
        for pair in es:
            for e in pair:
                e[3 * r + X, top : top + 8, :] = zero
                e[3 * r + Y, top : top + 8, :] = zero
        return 0

    lax.fori_loop(0, HELD, ends, 0)
    for copy in copies:
        copy.wait()

    def unpack(r, _):
        at = BASE + r
        for t in range(tiles):
            z = 8 * t
            v = sv[r, z : z + 8, :]
            for c in range(NC):
                turned = pltpu.roll(v, 128 - 16 * c, 1) if c else v
                if c < 3:
                    ea1[3 * at + c, 8 + z : 16 + z, :] = turned
                elif c < 6:
                    ma1[3 * at + c - 3, 8 + z : 16 + z, :] = turned
                else:
                    d1[at, z : z + 8, :] = turned
        return 0

    lax.fori_loop(0, ROWS, unpack, 0)
    hz = 8 * halo

    @pl.when(jnp.logical_not(counts))
    def _():
        def clear(i, _):
            for ref in (ea0, ea1, ma0, ma1):
                ref[3 * BASE + i, hz + 8 : hz + 16, :] = zero
            return 0

        lax.fori_loop(0, 3 * ROWS, clear, 0)

    live = jnp.where(counts, 1.0, 0.0).astype(F32)

    def tables(r, _):
        for t in range(tiles):
            z = 8 * t
            for d, g in zip(ds_, gs):
                ids = d[r, z : z + 8, :]
                d_cells, g_cells = zero, zero
                for i in range(5):
                    hit = ids == float(i)
                    d_cells = jnp.where(hit, decay[i], d_cells)
                    g_cells = jnp.where(hit, gain[i] * 0.5, g_cells)
                if t == halo:
                    d_cells, g_cells = d_cells * live, g_cells * live
                d[r, z : z + 8, :] = d_cells
                g[r, z : z + 8, :] = g_cells
        return 0

    lax.fori_loop(BASE + 1, BASE + ROWS - 1, tables, 0)

    lane = lax.broadcasted_iota(jnp.int32, (8, 128), 1)
    last, first_lane = lane == 127, lane == 0
    units = [(row, t) for row in range(2) for t in range(tiles)]

    def first_turn(i, _):
        kept = []
        for row, t in units:
            r = BASE + 2 * i + row
            for j, c in enumerate((X, Z)):
                pair = [pltpu.roll(e[3 * r + c, 8 + 8 * t : 16 + 8 * t, :], 127, 1) for e in es[0]]
                kept.append((4 * r + 2 * j, 8 * t, pair))
        for i, z, (a, b) in kept:
            ya[i, z : z + 8, :] = jnp.where(last, b, a)
            ya[i + 1, z : z + 8, :] = jnp.where(last, a, b)
        return 0

    lax.fori_loop(0, ROWS // 2, first_turn, 0)

    def block(old, with_e, with_m, m, start):
        new = 1 - old
        base = start + 2 * m
        b3, b4 = 3 * base, 4 * base
        waiting = []

        def keep():
            for y, b, i, z, (a, c), edge_lane in waiting.pop(0):
                y[b + i, z : z + 8, :] = jnp.where(edge_lane, c, a)
                y[b + (i + 1), z : z + 8, :] = jnp.where(edge_lane, a, c)

        for row, t in units if with_e else ():
            e, z = row - 2, 8 * t
            turned = [[], []]
            for k in range(2):

                def magnetic(c, r=e, shift=0):
                    return ms[new][k][b3 + (3 * r + c), 8 + z + shift : 16 + z + shift, :]

                def electric(c):
                    return es[old][k][b3 + (3 * e + c), 8 + z : 16 + z, :]

                mx_y = ym[4 * row + k, z : z + 8, :]
                mz_y = ym[4 * row + 2 + k, z : z + 8, :]
                mx, my, mz = magnetic(X), magnetic(Y), magnetic(Z)
                d = ds_[k][base + e, z : z + 8, :]
                g = gs[k][base + e, z : z + 8, :]
                ex = d * electric(X) + g * ((mz - mz_y) - (my - magnetic(Y, e, -1)))
                ey = d * electric(Y) + g * ((mx - magnetic(X, e, -1)) - (mz - magnetic(Z, e - 1)))
                ez = d * electric(Z) + g * ((my - magnetic(Y, e - 1)) - (mx - mx_y))
                for c, v in ((X, ex), (Y, ey), (Z, ez)):
                    es[new][k][b3 + (3 * e + c), 8 + z : 16 + z, :] = v
                turned[0].append(pltpu.roll(ex, 127, 1))
                turned[1].append(pltpu.roll(ez, 127, 1))
            waiting.append(
                [(yes[new], b4, 4 * e + 2 * j, z, turned[j], last) for j in range(2)]
            )
            if len(waiting) > LAG:
                keep()
        for row, t in units if with_m else ():
            z = 8 * t
            turned = [[], []]
            for k in range(2):

                def electric(c, r=row, shift=0):
                    return es[old][k][b3 + (3 * r + c), 8 + z + shift : 16 + z + shift, :]

                def magnetic(c):
                    return ms[old][k][b3 + (3 * row + c), 8 + z : 16 + z, :]

                ex_y = yes[old][b4 + (4 * row + k), z : z + 8, :]
                ez_y = yes[old][b4 + (4 * row + 2 + k), z : z + 8, :]
                ex, ey, ez = electric(X), electric(Y), electric(Z)
                cx = (ez_y - ez) - (electric(Y, row, 1) - ey)
                cy = (electric(X, row, 1) - ex) - (electric(Z, row + 1) - ez)
                cz = (electric(Y, row + 1) - ey) - (ex_y - ex)
                if t == halo and not upper:
                    cx, cy, cz = cx * live, cy * live, cz * live
                mx, my, mz = magnetic(X) - cx, magnetic(Y) - cy, magnetic(Z) - cz
                for c, v in ((X, mx), (Y, my), (Z, mz)):
                    ms[new][k][b3 + (3 * row + c), 8 + z : 16 + z, :] = v
                turned[0].append(pltpu.roll(mx, 1, 1))
                turned[1].append(pltpu.roll(mz, 1, 1))
            waiting.append([(ym, 0, 4 * row + 2 * j, z, turned[j], first_lane) for j in range(2)])
            if len(waiting) > LAG:
                keep()
        while waiting:
            keep()
        return start

    def two_steps(s, _):
        for old in range(2):
            left = STEPS - 1 - old - 2 * s
            start = BASE + W - left - 2
            block(old, False, True, 0, start)
            lax.fori_loop(1, W - 1 + left, functools.partial(block, old, True, True), start)
            block(old, True, False, W - 1 + left, start)
        return 0

    lax.fori_loop(0, STEPS // 2, two_steps, 0)

    def emit(r, _):
        for c, source in enumerate((X, Y, Z)):
            for t in range(on):
                stage[c, pl.ds(64 * t + r, 8, stride=8), :] = ea0[
                    3 * (r + BASE + W) + source, 16 + 8 * t : 24 + 8 * t, :
                ]
        return 0

    lax.fori_loop(0, 8, emit, 0)
    if upper:
        plane[0] = stage[0, 64 * on - 8 : 64 * on, :]
        plane[1] = stage[1, 64 * on - 8 : 64 * on, :]
    copy_all([(stage, out.at[:, pl.ds(64 * (CUT + 1) if upper else 0, 64 * on)])], sems)


def run_steps(upper, decay, gain, sides, arrays):
    smem = pl.BlockSpec(memory_space=pltpu.SMEM)
    out_shape = [jax.ShapeDtypeStruct((3, 640, 128), F32)]
    out_specs = [HBM]
    aliases = {}
    if upper:
        out_shape.append(jax.ShapeDtypeStruct((2, 8, 128), F32))
        out_specs.append(LOCAL)
    else:
        aliases = {4 + len(arrays) - 1: 0}
    tiles, on = (11 - CUT, 9 - CUT) if upper else (CUT + 3, CUT + 1)
    z = 16 + 8 * tiles
    field = pltpu.VMEM((3 * HELD, z, 128), F32)
    table = pltpu.VMEM((HELD, 8 * tiles, 128), F32)
    turned = pltpu.VMEM((4 * HELD, 8 * tiles, 128), F32)
    return pl.pallas_call(
        functools.partial(steps_kernel, upper),
        out_shape=out_shape,
        in_specs=[smem, smem] + [HBM] * (2 + len(arrays)),
        out_specs=out_specs,
        scratch_shapes=[field] * 8
        + [table] * 4
        + [turned] * 2
        + [
            pltpu.VMEM((8, 8 * tiles, 128), F32),
            pltpu.VMEM((ROWS, 8 * tiles, 128), F32),
            pltpu.VMEM((3, 64 * on, 128), F32),
            pltpu.SemaphoreType.DMA((39,)),
        ],
        input_output_aliases=aliases,
        compiler_params=params(),
        cost_estimate=cost(15),
        name="steps_upper" if upper else "steps_lower",
    )(decay, gain, *sides, *arrays)


def image_kernel(weights, centre, before, after, out, sh, rhs):
    gz = lax.axis_index("gz")
    lane = lax.broadcasted_iota(jnp.int32, (24, 128), 1)
    for q in range(15):
        shift = q - 7
        for c in range(2):
            v = centre[c]
            if shift > 0:
                v = jnp.where(
                    lane >= 128 - shift,
                    pltpu.roll(after[c], 128 - shift, 1),
                    pltpu.roll(v, 128 - shift, 1),
                )
            elif shift < 0:
                v = jnp.where(
                    lane < -shift, pltpu.roll(before[c], -shift, 1), pltpu.roll(v, -shift, 1)
                )
            sh[q, c] = v

    def fill(side):
        for q in range(15):
            for c in range(2):
                for i in range(4):
                    start = 4 * side + 1 + i
                    rhs[16 * q : 16 * q + 16, (4 * c + i) * 128 : (4 * c + i + 1) * 128] = sh[
                        q, c, start : start + 16, :
                    ]

    @pl.when(gz == 0)
    def _():
        fill(0)

    @pl.when(gz == 1)
    def _():
        fill(1)

    amplitude = jnp.dot(
        weights[...],
        rhs[...],
        precision=lax.Precision.HIGHEST,
        preferred_element_type=jnp.float32,
    )
    power = jnp.sum(amplitude * amplitude, axis=0, keepdims=True)
    for i in range(4):
        out[i : i + 1, :] = (
            power[:, i * 128 : (i + 1) * 128] + power[:, (4 + i) * 128 : (5 + i) * 128]
        )


def image_of(weights, centre, before, after):
    return pl.pallas_call(
        image_kernel,
        out_shape=jax.ShapeDtypeStruct((4, 128), jnp.float32),
        in_specs=[pl.BlockSpec(memory_space=pltpu.VMEM)] * 4,
        out_specs=pl.BlockSpec(memory_space=pltpu.VMEM),
        scratch_shapes=[
            pltpu.VMEM((15, 2, 24, 128), jnp.float32),
            pltpu.VMEM((240, 1024), jnp.float32),
        ],
        compiler_params=pltpu.CompilerParams(vmem_limit_bytes=VMEM),
        name="image",
    )(weights, centre, before, after)


def on_device(electric, magnetic, material, decay, gain, kernels):
    el = electric.reshape(3, 640, 128)
    mg = magnetic.reshape(3, 640, 128)
    mat = material.reshape(640, 128)
    weights = jnp.pad(
        kernels.transpose(0, 1, 3, 2).reshape(48, 15, 15), ((0, 0), (0, 0), (0, 1))
    ).reshape(48, 240)

    strips, edge, edge_strips = own_strips(el, mg, mat)
    edge = around(edge, "gz", 1)
    from_low, from_high = around(strips, "gy", 1), around(strips, "gy", -1)
    edge_low, edge_high = beyond(edge_strips, 1), beyond(edge_strips, -1)
    own_u, up_u, down_u, own_l, up_l, down_l = pack(el, mg, mat)
    strips, up_u, down_u, up_l, down_l = fill(
        from_low, from_high, edge_low, edge_high, edge, [up_u, down_u, up_l, down_l]
    )
    low_u, high_u = around(up_u, "gx", 1), around(down_u, "gx", -1)
    low_l, high_l = around(up_l, "gx", 1), around(down_l, "gx", -1)

    sides = [strips, edge]
    field, plane = run_steps(True, decay, gain, sides, [own_u, low_u, high_u])
    top = lax.ppermute(plane, "gz", [(1, 0)])
    top = jnp.where(lax.axis_index("gz") == 1, plane, top)
    top = jnp.stack([top, around(top, "gy", 1), around(top, "gy", -1)])
    top = jnp.concatenate([around(top, "gx", 1), top, around(top, "gx", -1)], 2)
    image = image_of(weights, top[0], top[1], top[2])
    (field,) = run_steps(
        False, decay, gain, sides, [own_u, low_u, high_u, own_l, low_l, high_l, field]
    )
    return (field.reshape(3, 80, 8, 128), image)


def solution(mesh):
    in_specs = (
        P(None, "gz", "gx", "gy"),
        P(None, "gz", "gx", "gy"),
        P("gz", "gx", "gy"),
        P(),
        P(),
        P(),
    )
    out_specs = (P(None, "gz", "gx", "gy"), P(("gx", "gz"), "gy"))
    return jax.shard_map(
        on_device, mesh=mesh, in_specs=in_specs, out_specs=out_specs, check_vma=False
    )
```

```python
import functools

import jax
import jax.numpy as jnp
from jax import lax
from jax.experimental import pallas as pl
from jax.experimental.pallas import tpu as pltpu
from jax.sharding import PartitionSpec as P

STEPS = 6
W = STEPS
Y, Z, X = range(3)
NC = 7
SOURCE = ((0, 1), (0, 2), (0, 0), (1, 1), (1, 2), (1, 0))
ROWS = 8 + 2 * W
BASE = 4
HELD = BASE + ROWS + 2
CUT = 7
LAG = 4
VMEM = 63 * 1024 * 1024
F32 = jnp.float32
HBM = pl.BlockSpec(memory_space=pl.ANY)
LOCAL = pl.BlockSpec(memory_space=pltpu.VMEM)


def around(value, axis, steps):
    count = lax.axis_size(axis)
    return lax.ppermute(value, axis, [(i, (i + steps) % count) for i in range(count)])


def beyond(value, steps):
    ny, nz = lax.axis_size("gy"), lax.axis_size("gz")
    pairs = [
        (y * nz + z, (y + steps) % ny * nz + (z + 1) % nz) for y in range(ny) for z in range(nz)
    ]
    return lax.ppermute(value, ("gy", "gz"), pairs)


def copy_all(pairs, sems):
    copies = [pltpu.make_async_copy(a, b, sems.at[i]) for i, (a, b) in enumerate(pairs)]
    for copy in copies:
        copy.start()
    for copy in copies:
        copy.wait()


def params():
    return pltpu.CompilerParams(vmem_limit_bytes=VMEM)


def cost(us):
    return pl.CostEstimate(flops=int(us * 1e9), bytes_accessed=int(us * 3e6), transcendentals=0)


def plane_of(r, c):
    return 48 + r if c == 6 else 24 * (c // 3) + 3 * r + c % 3


def strip_masks():
    lane = lax.broadcasted_iota(jnp.int32, (8, 128), 1)
    return [((lane - 16 * c + W + 128) % 128) < 2 * W for c in range(NC)]


def strip_kernel(el, mg, mat, strips, edge, edge_strips, ext, matv, sems):
    gz = lax.axis_index("gz")
    loads = [(mat, matv)]
    for c, (which, comp) in enumerate(SOURCE):
        loads.append(((el, mg)[which].at[comp], ext.at[c]))
    copy_all(loads, sems)
    masks = strip_masks()

    def layers(c, t, r):
        rows = pl.ds(64 * t + r, 8, stride=8)
        if c == 6:
            return matv[rows, :].astype(F32)
        v = ext[c, rows, :]
        return v * 2.0 if c >= 3 else v

    def row(r, _):
        for t in range(10):
            total = layers(0, t, r)
            for c in range(1, NC):
                total = jnp.where(masks[c], pltpu.roll(layers(c, t, r), 16 * c, 1), total)
            strips[r, 8 * t : 8 * t + 8, :] = total
        return 0

    lax.fori_loop(0, 8, row, 0)

    def edges(t):
        for r in range(8):
            for c in range(NC):
                edge[plane_of(r, c)] = layers(c, t, r)
        edge_strips[...] = strips[:, 8 * t : 8 * t + 8, :]

    @pl.when(gz == 0)
    def _():
        edges(9)

    @pl.when(gz == 1)
    def _():
        edges(0)


def own_strips(el, mg, mat):
    return pl.pallas_call(
        strip_kernel,
        out_shape=[
            jax.ShapeDtypeStruct((8, 80, 128), F32),
            jax.ShapeDtypeStruct((8 * NC, 8, 128), F32),
            jax.ShapeDtypeStruct((8, 8, 128), F32),
        ],
        in_specs=[HBM] * 3,
        out_specs=[LOCAL] * 3,
        scratch_shapes=[
            pltpu.VMEM((6, 640, 128), F32),
            pltpu.VMEM((640, 128), jnp.int32),
            pltpu.SemaphoreType.DMA((7,)),
        ],
        compiler_params=params(),
        cost_estimate=cost(3),
        name="own_strips",
    )(el, mg, mat)


def pack_kernel(first, last, el, mg, mat, *refs):
    if first:
        own, up, down, ext, matv, planes, sems = refs
    else:
        strips, own, up, down, ext, matv, planes, sems = refs
    tiles = last - first
    here = pl.ds(64 * first, 64 * tiles)
    loads = [(mat.at[here], matv)]
    for c, (which, comp) in enumerate(SOURCE):
        loads.append(((el, mg)[which].at[comp, here], ext.at[c]))
    copy_all(loads, sems)

    def row(r, _):
        for t in range(tiles):
            rows = pl.ds(64 * t + r, 8, stride=8)
            for c in range(NC):
                if c == 6:
                    v = matv[rows, :].astype(F32)
                else:
                    v = ext[c, rows, :]
                    if c >= 3:
                        v = v * 2.0
                planes[plane_of(r, c), 8 * t : 8 * t + 8, :] = v
        return 0

    lax.fori_loop(0, 8, row, 0)
    z = pl.ds(0, 8 * tiles)
    pairs = [(planes, own)]
    for a, b, n in ((6, 0, 18), (30, 18, 2), (33, 20, 15), (51, 35, 5)):
        pairs.append((planes.at[pl.ds(a, n)], up.at[pl.ds(b, n), z]))
    for a, b, n in ((0, 0, 17), (24, 17, 15), (48, 32, 5)):
        pairs.append((planes.at[pl.ds(a, n)], down.at[pl.ds(b, n), z]))
    if not first:
        pairs.append((strips.at[pl.ds(8 - W, W), z], up.at[pl.ds(40, W)]))
        pairs.append((strips.at[pl.ds(0, W), z], down.at[pl.ds(37, W)]))
    copy_all(pairs, sems)


def pack(first, last, el, mg, mat, *strips):
    layers = 8 * (last - first)
    sent = layers + 8 if first else layers
    return pl.pallas_call(
        functools.partial(pack_kernel, first, last),
        out_shape=[
            jax.ShapeDtypeStruct((8 * NC, layers, 128), F32),
            jax.ShapeDtypeStruct((40 + W, sent, 128), F32),
            jax.ShapeDtypeStruct((37 + W, sent, 128), F32),
        ],
        in_specs=[HBM] * 3 + [LOCAL] * len(strips),
        out_specs=[HBM] * 3,
        scratch_shapes=[
            pltpu.VMEM((6, 8 * layers, 128), F32),
            pltpu.VMEM((8 * layers, 128), jnp.int32),
            pltpu.VMEM((8 * NC, layers, 128), F32),
            pltpu.SemaphoreType.DMA((10,)),
        ],
        compiler_params=params(),
        cost_estimate=cost(3),
        name="pack_upper" if first else "pack_lower",
    )(el, mg, mat, *strips)


def fill_kernel(from_low, from_high, edge_low, edge_high, edge, *refs):
    strips, up_u, down_u, halo, sems = refs[2:]
    lane = lax.broadcasted_iota(jnp.int32, (8, 80, 128), 2)
    halo[:, 0:80, :] = jnp.where(lane % 16 < 8, from_high[...], from_low[...])
    lane = lax.broadcasted_iota(jnp.int32, (8, 8, 128), 2)
    halo[:, 80:88, :] = jnp.where(lane % 16 < 8, edge_high[...], edge_low[...])
    nu, nl = 8 * (10 - CUT), 8 * CUT
    pairs = [(halo, strips)]
    for message, first, count, parts in (
        (up_u, 8 - W, 40, ((6, 0, 18), (30, 18, 2), (33, 20, 15), (51, 35, 5))),
        (down_u, 0, 37, ((0, 0, 17), (24, 17, 15), (48, 32, 5))),
    ):
        rows = pl.ds(first, W)
        pairs.append(
            (halo.at[rows, pl.ds(nl, nu + 8)], message.at[pl.ds(count, W), pl.ds(0, nu + 8)])
        )
        for a, b, n in parts:
            pairs.append((edge.at[pl.ds(a, n)], message.at[pl.ds(b, n), pl.ds(nu, 8)]))
    copy_all(pairs, sems)


def fill(from_low, from_high, edge_low, edge_high, edge, messages):
    shapes = [jax.ShapeDtypeStruct((8, 88, 128), F32)]
    shapes += [jax.ShapeDtypeStruct(m.shape, F32) for m in messages]
    return pl.pallas_call(
        fill_kernel,
        out_shape=shapes,
        in_specs=[LOCAL] * 5 + [HBM] * 2,
        out_specs=[HBM] * 3,
        scratch_shapes=[pltpu.VMEM((8, 88, 128), F32), pltpu.SemaphoreType.DMA((10,))],
        input_output_aliases={5: 1, 6: 2},
        compiler_params=params(),
        cost_estimate=cost(1),
        name="fill",
    )(from_low, from_high, edge_low, edge_high, edge, *messages)


def steps_kernel(upper, decay, gain, strips, edge, *refs):
    gz = lax.axis_index("gz")
    nu, nl = 8 * (10 - CUT), 8 * CUT
    own_u, low_u, high_u = refs[:3]
    if upper:
        out, plane, *scratch = refs[3:]
        tiles, halo, counts = 11 - CUT, 10 - CUT, gz == 0
        sets = [((own_u, low_u, high_u), 0, nu, 0, nl)]
    else:
        own_l, low_l, high_l, _, out, *scratch = refs[3:]
        tiles, halo, counts = CUT + 3, 0, gz == 1
        sets = [
            ((own_l, low_l, high_l), 0, nl, 8, 0),
            ((own_u, low_u, high_u), 0, 16, 8 + nl, nl),
        ]
    on = 9 - CUT if upper else CUT + 1
    sets.append(((edge, low_u, high_u), nu, 8, 8 * halo, 80))
    ea0, ea1, eb0, eb1, ma0, ma1, mb0, mb1, d0, d1, g0, g1, ya, yb, ym, sv, stage, sems = scratch
    es, ms, yes = ((ea0, ea1), (eb0, eb1)), ((ma0, ma1), (mb0, mb1)), (ya, yb)
    ds_, gs = (d0, d1), (g0, g1)

    first, mid, last_ = BASE, BASE + W, BASE + W + 8
    groups = []
    for (own, low, high), start, layers, to, strip in sets:
        src, zf, zd = pl.ds(start, layers), pl.ds(8 + to, layers), pl.ds(to, layers)
        mine = pl.ds(0, 8) if own is edge else src
        moves = [
            (strips.at[:, pl.ds(strip, layers)], sv.at[pl.ds(W, 8), zd]),
            (low.at[pl.ds(40, W), src], sv.at[pl.ds(0, W), zd]),
            (high.at[pl.ds(37, W), src], sv.at[pl.ds(W + 8, W), zd]),
        ]
        for ref, a, n, dst, b, z in (
            (own, 0, 24, ea0, 3 * mid, zf),
            (own, 24, 24, ma0, 3 * mid, zf),
            (own, 48, 8, d0, mid, zd),
            (low, 0, 18, ea0, 3 * first, zf),
            (low, 18, 2, ma0, 3 * first, zf),
            (low, 20, 15, ma0, 3 * first + 3, zf),
            (low, 35, 5, d0, first + 1, zd),
            (high, 0, 17, ea0, 3 * last_, zf),
            (high, 17, 15, ma0, 3 * last_, zf),
            (high, 32, 5, d0, last_, zd),
        ):
            moves.append((ref.at[pl.ds(a, n), mine if ref is own else src], dst.at[pl.ds(b, n), z]))
        groups.append(moves)
    copies = []
    for moves in groups:
        for a, b in moves:
            copies.append(pltpu.make_async_copy(a, b, sems.at[len(copies)]))
    for copy in copies:
        copy.start()

    zero = jnp.zeros((8, 128), F32)
    top = 8 + 8 * tiles

    def ends(r, _):
        for pair in ms:
            for m in pair:
                m[3 * r + X, 0:8, :] = zero
                m[3 * r + Y, 0:8, :] = zero
        for pair in es:
            for e in pair:
                e[3 * r + X, top : top + 8, :] = zero
                e[3 * r + Y, top : top + 8, :] = zero
        return 0

    lax.fori_loop(0, HELD, ends, 0)
    strip_copies = [i for g in range(len(groups)) for i in range(13 * g, 13 * g + 3)]
    for i in strip_copies:
        copies[i].wait()

    def unpack(r, _):
        at = BASE + r
        for t in range(tiles):
            z = 8 * t
            v = sv[r, z : z + 8, :]
            for c in range(NC):
                turned = pltpu.roll(v, 128 - 16 * c, 1) if c else v
                if c < 3:
                    ea1[3 * at + c, 8 + z : 16 + z, :] = turned
                elif c < 6:
                    ma1[3 * at + c - 3, 8 + z : 16 + z, :] = turned
                else:
                    d1[at, z : z + 8, :] = turned
        return 0

    lax.fori_loop(0, ROWS, unpack, 0)
    for i, copy in enumerate(copies):
        if i not in strip_copies:
            copy.wait()
    hz = 8 * halo

    @pl.when(jnp.logical_not(counts))
    def _():
        def clear(i, _):
            for ref in (ea0, ea1, ma0, ma1):
                ref[3 * BASE + i, hz + 8 : hz + 16, :] = zero
            return 0

        lax.fori_loop(0, 3 * ROWS, clear, 0)

    live = jnp.where(counts, 1.0, 0.0).astype(F32)

    def tables(r, _):
        for t in range(tiles):
            z = 8 * t
            for d, g in zip(ds_, gs):
                ids = d[r, z : z + 8, :]
                d_cells, g_cells = zero, zero
                for i in range(5):
                    hit = ids == float(i)
                    d_cells = jnp.where(hit, decay[i], d_cells)
                    g_cells = jnp.where(hit, gain[i] * 0.5, g_cells)
                if t == halo:
                    d_cells, g_cells = d_cells * live, g_cells * live
                d[r, z : z + 8, :] = d_cells
                g[r, z : z + 8, :] = g_cells
        return 0

    lax.fori_loop(BASE + 1, BASE + ROWS - 1, tables, 0)

    lane = lax.broadcasted_iota(jnp.int32, (8, 128), 1)
    last, first_lane = lane == 127, lane == 0
    units = [(row, t) for row in range(2) for t in range(tiles)]

    def turn_two(which, r0):
        kept = []
        for row, t in units:
            for j, c in enumerate((X, Z)):
                pair = [
                    pltpu.roll(e[3 * r0 + (3 * row + c), 8 + 8 * t : 16 + 8 * t, :], 127, 1)
                    for e in es[which]
                ]
                kept.append((4 * row + 2 * j, 8 * t, pair))
        y = yes[which]
        for i, z, (a, b) in kept:
            y[4 * r0 + i, z : z + 8, :] = jnp.where(last, b, a)
            y[4 * r0 + (i + 1), z : z + 8, :] = jnp.where(last, a, b)

    def first_turn(i, _):
        turn_two(0, BASE + 2 * i)
        return 0

    lax.fori_loop(0, ROWS // 2, first_turn, 0)

    def block(old, with_e, with_m, m, start):
        new = 1 - old
        base = start + 2 * m
        b3, b4 = 3 * base, 4 * base
        waiting = []
        jobs = [(ms, row, t) for row, t in units] + [(es, row, t) for row, t in units]
        jobs = jobs if with_e else []

        def turn():
            refs, row, t = jobs.pop(0)
            z = 8 * t
            if refs is ms:
                pairs = [
                    [pltpu.roll(f[b3 + (3 * (row - 2) + c), 8 + z : 16 + z, :], 1, 1) for f in ms[new]]
                    for c in (X, Z)
                ]
                waiting.append((ym, 0, 4 * row, z, pairs, first_lane))
            else:
                pairs = [
                    [pltpu.roll(f[b3 + (3 * (row - 4) + c), 8 + z : 16 + z, :], 127, 1) for f in es[new]]
                    for c in (X, Z)
                ]
                waiting.append((yes[new], b4, 4 * (row - 4), z, pairs, last))

        def keep():
            y, b, i, z, pairs, edge_lane = waiting.pop(0)
            for j, (v0, v1) in enumerate(pairs):
                y[b + (i + 2 * j), z : z + 8, :] = jnp.where(edge_lane, v1, v0)
                y[b + (i + 2 * j + 1), z : z + 8, :] = jnp.where(edge_lane, v0, v1)

        def pace():
            for _ in range(2):
                if jobs:
                    turn()
            for _ in range(2):
                if len(waiting) > LAG or (waiting and not jobs):
                    keep()

        for row, t in units if with_m else ():
            pace()
            z = 8 * t
            for k in range(2):

                def electric(c, r=row, shift=0):
                    return es[old][k][b3 + (3 * r + c), 8 + z + shift : 16 + z + shift, :]

                def magnetic(c):
                    return ms[old][k][b3 + (3 * row + c), 8 + z : 16 + z, :]

                ex_y = yes[old][b4 + (4 * row + k), z : z + 8, :]
                ez_y = yes[old][b4 + (4 * row + 2 + k), z : z + 8, :]
                ex, ey, ez = electric(X), electric(Y), electric(Z)
                cx = (ez_y - ez) - (electric(Y, row, 1) - ey)
                cy = (electric(X, row, 1) - ex) - (electric(Z, row + 1) - ez)
                cz = (electric(Y, row + 1) - ey) - (ex_y - ex)
                if t == halo and not upper:
                    cx, cy, cz = cx * live, cy * live, cz * live
                mx, my, mz = magnetic(X) - cx, magnetic(Y) - cy, magnetic(Z) - cz
                for c, v in ((X, mx), (Y, my), (Z, mz)):
                    ms[new][k][b3 + (3 * row + c), 8 + z : 16 + z, :] = v
        while jobs:
            turn()
            if len(waiting) > LAG:
                keep()
        while waiting:
            keep()
        for row, t in units if with_e else ():
            e, z = row - 2, 8 * t
            for k in range(2):

                def magnetic(c, r=e, shift=0):
                    return ms[new][k][b3 + (3 * r + c), 8 + z + shift : 16 + z + shift, :]

                def electric(c):
                    return es[old][k][b3 + (3 * e + c), 8 + z : 16 + z, :]

                mx_y = ym[4 * row + k, z : z + 8, :]
                mz_y = ym[4 * row + 2 + k, z : z + 8, :]
                mx, my, mz = magnetic(X), magnetic(Y), magnetic(Z)
                d = ds_[k][base + e, z : z + 8, :]
                g = gs[k][base + e, z : z + 8, :]
                ex = d * electric(X) + g * ((mz - mz_y) - (my - magnetic(Y, e, -1)))
                ey = d * electric(Y) + g * ((mx - magnetic(X, e, -1)) - (mz - magnetic(Z, e - 1)))
                ez = d * electric(Z) + g * ((my - magnetic(Y, e - 1)) - (mx - mx_y))
                for c, v in ((X, ex), (Y, ey), (Z, ez)):
                    es[new][k][b3 + (3 * e + c), 8 + z : 16 + z, :] = v
        return start

    def two_steps(s, _):
        for old in range(2):
            left = STEPS - 1 - old - 2 * s
            start = BASE + W - left - 2
            block(old, False, True, 0, start)
            lax.fori_loop(1, W - 1 + left, functools.partial(block, old, True, True), start)
            block(old, True, False, W - 1 + left, start)
            turn_two(1 - old, start + 2 * (W - 2 + left))
        return 0

    lax.fori_loop(0, STEPS // 2, two_steps, 0)

    def emit(r, _):
        for c, source in enumerate((X, Y, Z)):
            for t in range(on):
                stage[c, pl.ds(64 * t + r, 8, stride=8), :] = ea0[
                    3 * (r + BASE + W) + source, 16 + 8 * t : 24 + 8 * t, :
                ]
        return 0

    lax.fori_loop(0, 8, emit, 0)
    if upper:
        plane[0] = stage[0, 64 * on - 8 : 64 * on, :]
        plane[1] = stage[1, 64 * on - 8 : 64 * on, :]
    copy_all([(stage, out.at[:, pl.ds(64 * (CUT + 1) if upper else 0, 64 * on)])], sems)


def run_steps(upper, decay, gain, sides, arrays):
    smem = pl.BlockSpec(memory_space=pltpu.SMEM)
    out_shape = [jax.ShapeDtypeStruct((3, 640, 128), F32)]
    out_specs = [HBM]
    aliases = {}
    if upper:
        out_shape.append(jax.ShapeDtypeStruct((2, 8, 128), F32))
        out_specs.append(LOCAL)
    else:
        aliases = {4 + len(arrays) - 1: 0}
    tiles, on = (11 - CUT, 9 - CUT) if upper else (CUT + 3, CUT + 1)
    z = 16 + 8 * tiles
    field = pltpu.VMEM((3 * HELD, z, 128), F32)
    table = pltpu.VMEM((HELD, 8 * tiles, 128), F32)
    turned = pltpu.VMEM((4 * HELD, 8 * tiles, 128), F32)
    return pl.pallas_call(
        functools.partial(steps_kernel, upper),
        out_shape=out_shape,
        in_specs=[smem, smem] + [HBM] * (2 + len(arrays)),
        out_specs=out_specs,
        scratch_shapes=[field] * 8
        + [table] * 4
        + [turned] * 2
        + [
            pltpu.VMEM((8, 8 * tiles, 128), F32),
            pltpu.VMEM((ROWS, 8 * tiles, 128), F32),
            pltpu.VMEM((3, 64 * on, 128), F32),
            pltpu.SemaphoreType.DMA((39,)),
        ],
        input_output_aliases=aliases,
        compiler_params=params(),
        cost_estimate=cost(100),
        name="steps_upper" if upper else "steps_lower",
    )(decay, gain, *sides, *arrays)


def image_kernel(weights, centre, before, after, out, sh, rhs):
    gz = lax.axis_index("gz")
    lane = lax.broadcasted_iota(jnp.int32, (24, 128), 1)
    for q in range(15):
        shift = q - 7
        for c in range(2):
            v = centre[c]
            if shift > 0:
                v = jnp.where(
                    lane >= 128 - shift,
                    pltpu.roll(after[c], 128 - shift, 1),
                    pltpu.roll(v, 128 - shift, 1),
                )
            elif shift < 0:
                v = jnp.where(
                    lane < -shift, pltpu.roll(before[c], -shift, 1), pltpu.roll(v, -shift, 1)
                )
            sh[q, c] = v

    def fill(side):
        for q in range(15):
            for c in range(2):
                for i in range(4):
                    start = 4 * side + 1 + i
                    rhs[16 * q : 16 * q + 16, (4 * c + i) * 128 : (4 * c + i + 1) * 128] = sh[
                        q, c, start : start + 16, :
                    ]

    @pl.when(gz == 0)
    def _():
        fill(0)

    @pl.when(gz == 1)
    def _():
        fill(1)

    amplitude = jnp.dot(
        weights[...],
        rhs[...],
        precision=lax.Precision.HIGHEST,
        preferred_element_type=jnp.float32,
    )
    power = jnp.sum(amplitude * amplitude, axis=0, keepdims=True)
    for i in range(4):
        out[i : i + 1, :] = (
            power[:, i * 128 : (i + 1) * 128] + power[:, (4 + i) * 128 : (5 + i) * 128]
        )


def image_of(weights, centre, before, after):
    return pl.pallas_call(
        image_kernel,
        out_shape=jax.ShapeDtypeStruct((4, 128), jnp.float32),
        in_specs=[pl.BlockSpec(memory_space=pltpu.VMEM)] * 4,
        out_specs=pl.BlockSpec(memory_space=pltpu.VMEM),
        scratch_shapes=[
            pltpu.VMEM((15, 2, 24, 128), jnp.float32),
            pltpu.VMEM((240, 1024), jnp.float32),
        ],
        compiler_params=pltpu.CompilerParams(vmem_limit_bytes=VMEM),
        name="image",
    )(weights, centre, before, after)


def on_device(electric, magnetic, material, decay, gain, kernels):
    el = electric.reshape(3, 640, 128)
    mg = magnetic.reshape(3, 640, 128)
    mat = material.reshape(640, 128)
    weights = jnp.pad(
        kernels.transpose(0, 1, 3, 2).reshape(48, 15, 15), ((0, 0), (0, 0), (0, 1))
    ).reshape(48, 240)

    strips, edge, edge_strips = own_strips(el, mg, mat)
    edge = around(edge, "gz", 1)
    from_low, from_high = around(strips, "gy", 1), around(strips, "gy", -1)
    edge_low, edge_high = beyond(edge_strips, 1), beyond(edge_strips, -1)
    own_u, up_u, down_u = pack(CUT, 10, el, mg, mat)
    strips, up_u, down_u = fill(from_low, from_high, edge_low, edge_high, edge, [up_u, down_u])
    low_u, high_u = around(up_u, "gx", 1), around(down_u, "gx", -1)
    own_l, up_l, down_l = pack(0, CUT, el, mg, mat, strips)
    low_l, high_l = around(up_l, "gx", 1), around(down_l, "gx", -1)

    sides = [strips, edge]
    field, plane = run_steps(True, decay, gain, sides, [own_u, low_u, high_u])
    top = lax.ppermute(plane, "gz", [(1, 0)])
    top = jnp.where(lax.axis_index("gz") == 1, plane, top)
    top = jnp.stack([top, around(top, "gy", 1), around(top, "gy", -1)])
    top, low_l, high_l = lax.optimization_barrier((top, low_l, high_l))
    top = jnp.concatenate([around(top, "gx", 1), top, around(top, "gx", -1)], 2)
    (field,) = run_steps(
        False, decay, gain, sides, [own_u, low_u, high_u, own_l, low_l, high_l, field]
    )
    image = image_of(weights, top[0], top[1], top[2])
    return (field.reshape(3, 80, 8, 128), image)


def solution(mesh):
    in_specs = (
        P(None, "gz", "gx", "gy"),
        P(None, "gz", "gx", "gy"),
        P("gz", "gx", "gy"),
        P(),
        P(),
        P(),
    )
    out_specs = (P(None, "gz", "gx", "gy"), P(("gx", "gz"), "gy"))
    return jax.shard_map(
        on_device, mesh=mesh, in_specs=in_specs, out_specs=out_specs, check_vma=False
    )
```

```python
import functools

import jax
import jax.numpy as jnp
from jax import lax
from jax.experimental import pallas as pl
from jax.experimental.pallas import tpu as pltpu
from jax.sharding import PartitionSpec as P

STEPS = 6
W = STEPS
Y, Z, X = range(3)
NC = 7
SOURCE = ((0, 1), (0, 2), (0, 0), (1, 1), (1, 2), (1, 0))
ROWS = 8 + 2 * W
BASE = 4
HELD = BASE + ROWS + 2
CUT = 7
HIGH = 11 - CUT
LAG = 4
VMEM = 63 * 1024 * 1024
F32 = jnp.float32
HBM = pl.BlockSpec(memory_space=pl.ANY)
LOCAL = pl.BlockSpec(memory_space=pltpu.VMEM)


def around(value, axis, steps):
    count = lax.axis_size(axis)
    return lax.ppermute(value, axis, [(i, (i + steps) % count) for i in range(count)])


def beyond(value, steps):
    ny, nz = lax.axis_size("gy"), lax.axis_size("gz")
    pairs = [
        (y * nz + z, (y + steps) % ny * nz + (z + 1) % nz) for y in range(ny) for z in range(nz)
    ]
    return lax.ppermute(value, ("gy", "gz"), pairs)


def copy_all(pairs, sems):
    copies = [pltpu.make_async_copy(a, b, sems.at[i]) for i, (a, b) in enumerate(pairs)]
    for copy in copies:
        copy.start()
    for copy in copies:
        copy.wait()


def params():
    return pltpu.CompilerParams(vmem_limit_bytes=VMEM)


def cost(us):
    return pl.CostEstimate(flops=int(us * 1e9), bytes_accessed=int(us * 3e6), transcendentals=0)


def plane_of(r, c):
    return 48 + r if c == 6 else 24 * (c // 3) + 3 * r + c % 3


def strip_masks():
    lane = lax.broadcasted_iota(jnp.int32, (8, 128), 1)
    return [((lane - 16 * c + W + 128) % 128) < 2 * W for c in range(NC)]


def strip_kernel(el, mg, mat, strips, edge, edge_strips, ext, matv, sems):
    gz = lax.axis_index("gz")
    loads = [(mat, matv)]
    for c, (which, comp) in enumerate(SOURCE):
        loads.append(((el, mg)[which].at[comp], ext.at[c]))
    copy_all(loads, sems)
    masks = strip_masks()

    def layers(c, t, r):
        rows = pl.ds(64 * t + r, 8, stride=8)
        if c == 6:
            return matv[rows, :].astype(F32)
        v = ext[c, rows, :]
        return v * 2.0 if c >= 3 else v

    def row(r, _):
        for t in range(10):
            total = layers(0, t, r)
            for c in range(1, NC):
                total = jnp.where(masks[c], pltpu.roll(layers(c, t, r), 16 * c, 1), total)
            strips[r, 8 * t : 8 * t + 8, :] = total
        return 0

    lax.fori_loop(0, 8, row, 0)

    def edges(t):
        for r in range(8):
            for c in range(NC):
                edge[plane_of(r, c)] = layers(c, t, r)
        edge_strips[...] = strips[:, 8 * t : 8 * t + 8, :]

    @pl.when(gz == 0)
    def _():
        edges(9)

    @pl.when(gz == 1)
    def _():
        edges(0)


def own_strips(el, mg, mat):
    return pl.pallas_call(
        strip_kernel,
        out_shape=[
            jax.ShapeDtypeStruct((8, 80, 128), F32),
            jax.ShapeDtypeStruct((8 * NC, 8, 128), F32),
            jax.ShapeDtypeStruct((8, 8, 128), F32),
        ],
        in_specs=[HBM] * 3,
        out_specs=[LOCAL] * 3,
        scratch_shapes=[
            pltpu.VMEM((6, 640, 128), F32),
            pltpu.VMEM((640, 128), jnp.int32),
            pltpu.SemaphoreType.DMA((7,)),
        ],
        compiler_params=params(),
        cost_estimate=cost(3),
        name="own_strips",
    )(el, mg, mat)


def pack_kernel(first, last, el, mg, mat, *refs):
    if first:
        own, up, down, ext, matv, planes, sems = refs
    else:
        strips, own, up, down, ext, matv, planes, sems = refs
    tiles = last - first
    here = pl.ds(64 * first, 64 * tiles)
    loads = [(mat.at[here], matv)]
    for c, (which, comp) in enumerate(SOURCE):
        loads.append(((el, mg)[which].at[comp, here], ext.at[c]))
    copy_all(loads, sems)

    def row(r, _):
        for t in range(tiles):
            rows = pl.ds(64 * t + r, 8, stride=8)
            for c in range(NC):
                if c == 6:
                    v = matv[rows, :].astype(F32)
                else:
                    v = ext[c, rows, :]
                    if c >= 3:
                        v = v * 2.0
                planes[plane_of(r, c), 8 * t : 8 * t + 8, :] = v
        return 0

    lax.fori_loop(0, 8, row, 0)
    z = pl.ds(0, 8 * tiles)
    pairs = [(planes, own)]
    for a, b, n in ((6, 0, 18), (30, 18, 2), (33, 20, 15), (51, 35, 5)):
        pairs.append((planes.at[pl.ds(a, n)], up.at[pl.ds(b, n), z]))
    for a, b, n in ((0, 0, 17), (24, 17, 15), (48, 32, 5)):
        pairs.append((planes.at[pl.ds(a, n)], down.at[pl.ds(b, n), z]))
    if not first:
        pairs.append((strips.at[pl.ds(8 - W, W), z], up.at[pl.ds(40, W)]))
        pairs.append((strips.at[pl.ds(0, W), z], down.at[pl.ds(37, W)]))
    copy_all(pairs, sems)


def pack(first, last, el, mg, mat, *strips):
    layers = 8 * (last - first)
    more = 0 if first else W
    return pl.pallas_call(
        functools.partial(pack_kernel, first, last),
        out_shape=[
            jax.ShapeDtypeStruct((8 * NC, layers, 128), F32),
            jax.ShapeDtypeStruct((40 + more, layers, 128), F32),
            jax.ShapeDtypeStruct((37 + more, layers, 128), F32),
        ],
        in_specs=[HBM] * 3 + [LOCAL] * len(strips),
        out_specs=[HBM] * 3,
        scratch_shapes=[
            pltpu.VMEM((6, 8 * layers, 128), F32),
            pltpu.VMEM((8 * layers, 128), jnp.int32),
            pltpu.VMEM((8 * NC, layers, 128), F32),
            pltpu.SemaphoreType.DMA((10,)),
        ],
        compiler_params=params(),
        cost_estimate=cost(20 if first else 3),
        name="pack_upper" if first else "pack_lower",
    )(el, mg, mat, *strips)


def corner_kernel(from_low, from_high, edge_low, edge_high, edge, strips, up, down):
    lane = lax.broadcasted_iota(jnp.int32, (8, 80, 128), 2)
    strips[:, 0:80, :] = jnp.where(lane % 16 < 8, from_high[...], from_low[...])
    lane = lax.broadcasted_iota(jnp.int32, (8, 8, 128), 2)
    strips[:, 80:88, :] = jnp.where(lane % 16 < 8, edge_high[...], edge_low[...])
    for a, b, n in ((6, 0, 18), (30, 18, 2), (33, 20, 15), (51, 35, 5)):
        up[b : b + n] = edge[a : a + n]
    for a, b, n in ((0, 0, 17), (24, 17, 15), (48, 32, 5)):
        down[b : b + n] = edge[a : a + n]
    for r in range(W):
        for t in range(HIGH):
            z = 8 * (CUT + t)
            up[40 + HIGH * r + t] = strips[8 - W + r, z : z + 8, :]
            down[37 + HIGH * r + t] = strips[r, z : z + 8, :]


def corners(from_low, from_high, edge_low, edge_high, edge):
    return pl.pallas_call(
        corner_kernel,
        out_shape=[
            jax.ShapeDtypeStruct((8, 88, 128), F32),
            jax.ShapeDtypeStruct((40 + W * HIGH, 8, 128), F32),
            jax.ShapeDtypeStruct((37 + W * HIGH, 8, 128), F32),
        ],
        in_specs=[LOCAL] * 5,
        out_specs=[LOCAL] * 3,
        compiler_params=params(),
        cost_estimate=cost(1),
        name="corners",
    )(from_low, from_high, edge_low, edge_high, edge)


def steps_kernel(upper, decay, gain, low_c, high_c, strips, edge, *refs):
    gz = lax.axis_index("gz")
    nu, nl = 8 * (10 - CUT), 8 * CUT
    own_u, low_u, high_u = refs[:3]
    if upper:
        out, plane, *scratch = refs[3:]
        tiles, halo, counts = 11 - CUT, 10 - CUT, gz == 0
        sets = [((own_u, low_u, high_u), 0, nu, 0, nl)]
    else:
        own_l, low_l, high_l, _, out, *scratch = refs[3:]
        tiles, halo, counts = CUT + 3, 0, gz == 1
        sets = [
            ((own_l, low_l, high_l), 0, nl, 8, 0),
            ((own_u, low_u, high_u), 0, 16, 8 + nl, nl),
        ]
    on = 9 - CUT if upper else CUT + 1
    ea0, ea1, eb0, eb1, ma0, ma1, mb0, mb1, d0, d1, g0, g1, ya, yb, ym, sv, stage, sems = scratch
    es, ms, yes = ((ea0, ea1), (eb0, eb1)), ((ma0, ma1), (mb0, mb1)), (ya, yb)
    ds_, gs = (d0, d1), (g0, g1)

    first, mid, last_ = BASE, BASE + W, BASE + W + 8
    hz = 8 * halo
    moves = [(strips.at[:, pl.ds(80, 8)], sv.at[pl.ds(W, 8), pl.ds(hz, 8)])]
    for (own, low, high), start, layers, to, strip in sets:
        zd = pl.ds(to, layers)
        moves.append((strips.at[:, pl.ds(strip, layers)], sv.at[pl.ds(W, 8), zd]))
        if not upper and own is own_l:
            moves.append((low.at[pl.ds(40, W)], sv.at[pl.ds(0, W), zd]))
            moves.append((high.at[pl.ds(37, W)], sv.at[pl.ds(W + 8, W), zd]))
    early = len(moves)
    own_parts = ((0, 24, ea0, 3 * mid), (24, 24, ma0, 3 * mid), (48, 8, d0, mid))
    low_parts = (
        (0, 18, ea0, 3 * first),
        (18, 2, ma0, 3 * first),
        (20, 15, ma0, 3 * first + 3),
        (35, 5, d0, first + 1),
    )
    high_parts = ((0, 17, ea0, 3 * last_), (17, 15, ma0, 3 * last_), (32, 5, d0, last_))
    for (own, low, high), start, layers, to, strip in sets:
        for ref, parts in ((own, own_parts), (low, low_parts), (high, high_parts)):
            for a, n, dst, b in parts:
                z = pl.ds(to if dst is d0 else 8 + to, layers)
                moves.append((ref.at[pl.ds(a, n), pl.ds(start, layers)], dst.at[pl.ds(b, n), z]))
    for a, n, dst, b in own_parts:
        z = pl.ds(hz if dst is d0 else 8 + hz, 8)
        moves.append((edge.at[pl.ds(a, n)], dst.at[pl.ds(b, n), z]))
    copies = [pltpu.make_async_copy(a, b, sems.at[i]) for i, (a, b) in enumerate(moves)]
    for copy in copies:
        copy.start()
    for ref, parts in ((low_c, low_parts), (high_c, high_parts)):
        for a, n, dst, b in parts:
            z = hz if dst is d0 else 8 + hz
            for i in range(n):
                dst[b + i, z : z + 8, :] = ref[a + i]
    here = [(t, t) for t in range(HIGH)]
    if not upper:
        here = [(0, HIGH - 1), (CUT + 1, 0), (CUT + 2, 1)]
    for r in range(W):
        for t, u in here:
            sv[r, 8 * t : 8 * t + 8, :] = low_c[40 + HIGH * r + u]
            sv[W + 8 + r, 8 * t : 8 * t + 8, :] = high_c[37 + HIGH * r + u]

    zero = jnp.zeros((8, 128), F32)
    top = 8 + 8 * tiles

    def ends(r, _):
        for pair in ms:
            for m in pair:
                m[3 * r + X, 0:8, :] = zero
                m[3 * r + Y, 0:8, :] = zero
        for pair in es:
            for e in pair:
                e[3 * r + X, top : top + 8, :] = zero
                e[3 * r + Y, top : top + 8, :] = zero
        return 0

    lax.fori_loop(0, HELD, ends, 0)
    for copy in copies[:early]:
        copy.wait()

    def unpack(r, _):
        at = BASE + r
        for t in range(tiles):
            z = 8 * t
            v = sv[r, z : z + 8, :]
            for c in range(NC):
                turned = pltpu.roll(v, 128 - 16 * c, 1) if c else v
                if c < 3:
                    ea1[3 * at + c, 8 + z : 16 + z, :] = turned
                elif c < 6:
                    ma1[3 * at + c - 3, 8 + z : 16 + z, :] = turned
                else:
                    d1[at, z : z + 8, :] = turned
        return 0

    lax.fori_loop(0, ROWS, unpack, 0)
    for copy in copies[early:]:
        copy.wait()

    @pl.when(jnp.logical_not(counts))
    def _():
        def clear(i, _):
            for ref in (ea0, ea1, ma0, ma1):
                ref[3 * BASE + i, hz + 8 : hz + 16, :] = zero
            return 0

        lax.fori_loop(0, 3 * ROWS, clear, 0)

    live = jnp.where(counts, 1.0, 0.0).astype(F32)

    def tables(r, _):
        for t in range(tiles):
            z = 8 * t
            for d, g in zip(ds_, gs):
                ids = d[r, z : z + 8, :]
                d_cells, g_cells = zero, zero
                for i in range(5):
                    hit = ids == float(i)
                    d_cells = jnp.where(hit, decay[i], d_cells)
                    g_cells = jnp.where(hit, gain[i] * 0.5, g_cells)
                if t == halo:
                    d_cells, g_cells = d_cells * live, g_cells * live
                d[r, z : z + 8, :] = d_cells
                g[r, z : z + 8, :] = g_cells
        return 0

    lax.fori_loop(BASE + 1, BASE + ROWS - 1, tables, 0)

    lane = lax.broadcasted_iota(jnp.int32, (8, 128), 1)
    last, first_lane = lane == 127, lane == 0
    units = [(row, t) for row in range(2) for t in range(tiles)]

    def turn_two(which, r0):
        kept = []
        for row, t in units:
            for j, c in enumerate((X, Z)):
                pair = [
                    pltpu.roll(e[3 * r0 + (3 * row + c), 8 + 8 * t : 16 + 8 * t, :], 127, 1)
                    for e in es[which]
                ]
                kept.append((4 * row + 2 * j, 8 * t, pair))
        y = yes[which]
        for i, z, (a, b) in kept:
            y[4 * r0 + i, z : z + 8, :] = jnp.where(last, b, a)
            y[4 * r0 + (i + 1), z : z + 8, :] = jnp.where(last, a, b)

    def first_turn(i, _):
        turn_two(0, BASE + 2 * i)
        return 0

    lax.fori_loop(0, ROWS // 2, first_turn, 0)

    def block(old, with_e, with_m, m, start):
        new = 1 - old
        base = start + 2 * m
        b3, b4 = 3 * base, 4 * base
        waiting = []
        jobs = [(ms, row, t) for row, t in units] + [(es, row, t) for row, t in units]
        jobs = jobs if with_e else []

        def turn():
            refs, row, t = jobs.pop(0)
            z = 8 * t
            if refs is ms:
                pairs = [
                    [pltpu.roll(f[b3 + (3 * (row - 2) + c), 8 + z : 16 + z, :], 1, 1) for f in ms[new]]
                    for c in (X, Z)
                ]
                waiting.append((ym, 0, 4 * row, z, pairs, first_lane))
            else:
                pairs = [
                    [pltpu.roll(f[b3 + (3 * (row - 4) + c), 8 + z : 16 + z, :], 127, 1) for f in es[new]]
                    for c in (X, Z)
                ]
                waiting.append((yes[new], b4, 4 * (row - 4), z, pairs, last))

        def keep():
            y, b, i, z, pairs, edge_lane = waiting.pop(0)
            for j, (v0, v1) in enumerate(pairs):
                y[b + (i + 2 * j), z : z + 8, :] = jnp.where(edge_lane, v1, v0)
                y[b + (i + 2 * j + 1), z : z + 8, :] = jnp.where(edge_lane, v0, v1)

        def pace():
            for _ in range(2):
                if jobs:
                    turn()
            for _ in range(2):
                if len(waiting) > LAG or (waiting and not jobs):
                    keep()

        for row, t in units if with_m else ():
            pace()
            z = 8 * t
            for k in range(2):

                def electric(c, r=row, shift=0):
                    return es[old][k][b3 + (3 * r + c), 8 + z + shift : 16 + z + shift, :]

                def magnetic(c):
                    return ms[old][k][b3 + (3 * row + c), 8 + z : 16 + z, :]

                ex_y = yes[old][b4 + (4 * row + k), z : z + 8, :]
                ez_y = yes[old][b4 + (4 * row + 2 + k), z : z + 8, :]
                ex, ey, ez = electric(X), electric(Y), electric(Z)
                cx = (ez_y - ez) - (electric(Y, row, 1) - ey)
                cy = (electric(X, row, 1) - ex) - (electric(Z, row + 1) - ez)
                cz = (electric(Y, row + 1) - ey) - (ex_y - ex)
                if t == halo and not upper:
                    cx, cy, cz = cx * live, cy * live, cz * live
                mx, my, mz = magnetic(X) - cx, magnetic(Y) - cy, magnetic(Z) - cz
                for c, v in ((X, mx), (Y, my), (Z, mz)):
                    ms[new][k][b3 + (3 * row + c), 8 + z : 16 + z, :] = v
        while jobs:
            turn()
            if len(waiting) > LAG:
                keep()
        while waiting:
            keep()
        for row, t in units if with_e else ():
            e, z = row - 2, 8 * t
            for k in range(2):

                def magnetic(c, r=e, shift=0):
                    return ms[new][k][b3 + (3 * r + c), 8 + z + shift : 16 + z + shift, :]

                def electric(c):
                    return es[old][k][b3 + (3 * e + c), 8 + z : 16 + z, :]

                mx_y = ym[4 * row + k, z : z + 8, :]
                mz_y = ym[4 * row + 2 + k, z : z + 8, :]
                mx, my, mz = magnetic(X), magnetic(Y), magnetic(Z)
                d = ds_[k][base + e, z : z + 8, :]
                g = gs[k][base + e, z : z + 8, :]
                ex = d * electric(X) + g * ((mz - mz_y) - (my - magnetic(Y, e, -1)))
                ey = d * electric(Y) + g * ((mx - magnetic(X, e, -1)) - (mz - magnetic(Z, e - 1)))
                ez = d * electric(Z) + g * ((my - magnetic(Y, e - 1)) - (mx - mx_y))
                for c, v in ((X, ex), (Y, ey), (Z, ez)):
                    es[new][k][b3 + (3 * e + c), 8 + z : 16 + z, :] = v
        return start

    def two_steps(s, _):
        for old in range(2):
            left = STEPS - 1 - old - 2 * s
            start = BASE + W - left - 2
            block(old, False, True, 0, start)
            lax.fori_loop(1, W - 1 + left, functools.partial(block, old, True, True), start)
            block(old, True, False, W - 1 + left, start)
            turn_two(1 - old, start + 2 * (W - 2 + left))
        return 0

    lax.fori_loop(0, STEPS // 2, two_steps, 0)

    def emit(r, _):
        for c, source in enumerate((X, Y, Z)):
            for t in range(on):
                stage[c, pl.ds(64 * t + r, 8, stride=8), :] = ea0[
                    3 * (r + BASE + W) + source, 16 + 8 * t : 24 + 8 * t, :
                ]
        return 0

    lax.fori_loop(0, 8, emit, 0)
    if upper:
        plane[0] = stage[0, 64 * on - 8 : 64 * on, :]
        plane[1] = stage[1, 64 * on - 8 : 64 * on, :]
    copy_all([(stage, out.at[:, pl.ds(64 * (CUT + 1) if upper else 0, 64 * on)])], sems)


def run_steps(upper, decay, gain, sides, arrays):
    smem = pl.BlockSpec(memory_space=pltpu.SMEM)
    out_shape = [jax.ShapeDtypeStruct((3, 640, 128), F32)]
    out_specs = [HBM]
    aliases = {}
    if upper:
        out_shape.append(jax.ShapeDtypeStruct((2, 8, 128), F32))
        out_specs.append(LOCAL)
    else:
        aliases = {6 + len(arrays) - 1: 0}
    tiles, on = (11 - CUT, 9 - CUT) if upper else (CUT + 3, CUT + 1)
    z = 16 + 8 * tiles
    field = pltpu.VMEM((3 * HELD, z, 128), F32)
    table = pltpu.VMEM((HELD, 8 * tiles, 128), F32)
    turned = pltpu.VMEM((4 * HELD, 8 * tiles, 128), F32)
    return pl.pallas_call(
        functools.partial(steps_kernel, upper),
        out_shape=out_shape,
        in_specs=[smem, smem, LOCAL, LOCAL] + [HBM] * (2 + len(arrays)),
        out_specs=out_specs,
        scratch_shapes=[field] * 8
        + [table] * 4
        + [turned] * 2
        + [
            pltpu.VMEM((8, 8 * tiles, 128), F32),
            pltpu.VMEM((ROWS, 8 * tiles, 128), F32),
            pltpu.VMEM((3, 64 * on, 128), F32),
            pltpu.SemaphoreType.DMA((39,)),
        ],
        input_output_aliases=aliases,
        compiler_params=params(),
        cost_estimate=cost(100),
        name="steps_upper" if upper else "steps_lower",
    )(decay, gain, *sides, *arrays)


def image_kernel(weights, centre, before, after, out, sh, rhs):
    gz = lax.axis_index("gz")
    lane = lax.broadcasted_iota(jnp.int32, (24, 128), 1)
    for q in range(15):
        shift = q - 7
        for c in range(2):
            v = centre[c]
            if shift > 0:
                v = jnp.where(
                    lane >= 128 - shift,
                    pltpu.roll(after[c], 128 - shift, 1),
                    pltpu.roll(v, 128 - shift, 1),
                )
            elif shift < 0:
                v = jnp.where(
                    lane < -shift, pltpu.roll(before[c], -shift, 1), pltpu.roll(v, -shift, 1)
                )
            sh[q, c] = v

    def fill(side):
        for q in range(15):
            for c in range(2):
                for i in range(4):
                    start = 4 * side + 1 + i
                    rhs[16 * q : 16 * q + 16, (4 * c + i) * 128 : (4 * c + i + 1) * 128] = sh[
                        q, c, start : start + 16, :
                    ]

    @pl.when(gz == 0)
    def _():
        fill(0)

    @pl.when(gz == 1)
    def _():
        fill(1)

    amplitude = jnp.dot(
        weights[...],
        rhs[...],
        precision=lax.Precision.HIGHEST,
        preferred_element_type=jnp.float32,
    )
    power = jnp.sum(amplitude * amplitude, axis=0, keepdims=True)
    for i in range(4):
        out[i : i + 1, :] = (
            power[:, i * 128 : (i + 1) * 128] + power[:, (4 + i) * 128 : (5 + i) * 128]
        )


def image_of(weights, centre, before, after):
    return pl.pallas_call(
        image_kernel,
        out_shape=jax.ShapeDtypeStruct((4, 128), jnp.float32),
        in_specs=[pl.BlockSpec(memory_space=pltpu.VMEM)] * 4,
        out_specs=pl.BlockSpec(memory_space=pltpu.VMEM),
        scratch_shapes=[
            pltpu.VMEM((15, 2, 24, 128), jnp.float32),
            pltpu.VMEM((240, 1024), jnp.float32),
        ],
        compiler_params=pltpu.CompilerParams(vmem_limit_bytes=VMEM),
        name="image",
    )(weights, centre, before, after)


def on_device(electric, magnetic, material, decay, gain, kernels):
    el = electric.reshape(3, 640, 128)
    mg = magnetic.reshape(3, 640, 128)
    mat = material.reshape(640, 128)
    weights = jnp.pad(
        kernels.transpose(0, 1, 3, 2).reshape(48, 15, 15), ((0, 0), (0, 0), (0, 1))
    ).reshape(48, 240)

    strips, edge, edge_strips = own_strips(el, mg, mat)
    edge = around(edge, "gz", 1)
    from_low, from_high = around(strips, "gy", 1), around(strips, "gy", -1)
    edge_low, edge_high = beyond(edge_strips, 1), beyond(edge_strips, -1)
    own_u, up_u, down_u = pack(CUT, 10, el, mg, mat)
    up_u, down_u, edge_low, edge_high = lax.optimization_barrier(
        (up_u, down_u, edge_low, edge_high)
    )
    low_u, high_u = around(up_u, "gx", 1), around(down_u, "gx", -1)
    strips, up_c, down_c = corners(from_low, from_high, edge_low, edge_high, edge)
    low_c, high_c = around(up_c, "gx", 1), around(down_c, "gx", -1)
    own_l, up_l, down_l = pack(0, CUT, el, mg, mat, strips)
    low_l, high_l = around(up_l, "gx", 1), around(down_l, "gx", -1)

    sides = [low_c, high_c, strips, edge]
    field, plane = run_steps(True, decay, gain, sides, [own_u, low_u, high_u])
    top = jnp.stack([plane, around(plane, "gy", 1), around(plane, "gy", -1)])
    top = jnp.where(lax.axis_index("gz") == 1, top, lax.ppermute(top, "gz", [(1, 0)]))
    top, low_l, high_l = lax.optimization_barrier((top, low_l, high_l))
    top = jnp.concatenate([around(top, "gx", 1), top, around(top, "gx", -1)], 2)
    (field,) = run_steps(
        False, decay, gain, sides, [own_u, low_u, high_u, own_l, low_l, high_l, field]
    )
    image = image_of(weights, top[0], top[1], top[2])
    return (field.reshape(3, 80, 8, 128), image)


def solution(mesh):
    in_specs = (
        P(None, "gz", "gx", "gy"),
        P(None, "gz", "gx", "gy"),
        P("gz", "gx", "gy"),
        P(),
        P(),
        P(),
    )
    out_specs = (P(None, "gz", "gx", "gy"), P(("gx", "gz"), "gy"))
    return jax.shard_map(
        on_device, mesh=mesh, in_specs=in_specs, out_specs=out_specs, check_vma=False
    )
```

```python
import functools

import jax
import jax.numpy as jnp
from jax import lax
from jax.experimental import pallas as pl
from jax.experimental.pallas import tpu as pltpu
from jax.sharding import PartitionSpec as P

STEPS = 6
W = STEPS
Y, Z, X = range(3)
NC = 7
SOURCE = ((0, 1), (0, 2), (0, 0), (1, 1), (1, 2), (1, 0))
ROWS = 8 + 2 * W
BASE = 4
HELD = BASE + ROWS + 2
CUT = 7
HIGH = 11 - CUT
LAG = 4
VMEM = 63 * 1024 * 1024
F32 = jnp.float32
HBM = pl.BlockSpec(memory_space=pl.ANY)
LOCAL = pl.BlockSpec(memory_space=pltpu.VMEM)


def around(value, axis, steps):
    count = lax.axis_size(axis)
    return lax.ppermute(value, axis, [(i, (i + steps) % count) for i in range(count)])


def beyond(value, steps):
    ny, nz = lax.axis_size("gy"), lax.axis_size("gz")
    pairs = [
        (y * nz + z, (y + steps) % ny * nz + (z + 1) % nz) for y in range(ny) for z in range(nz)
    ]
    return lax.ppermute(value, ("gy", "gz"), pairs)


def copy_all(pairs, sems):
    copies = [pltpu.make_async_copy(a, b, sems.at[i]) for i, (a, b) in enumerate(pairs)]
    for copy in copies:
        copy.start()
    for copy in copies:
        copy.wait()


def params():
    return pltpu.CompilerParams(vmem_limit_bytes=VMEM)


def cost(us):
    return pl.CostEstimate(flops=int(us * 1e9), bytes_accessed=int(us * 3e6), transcendentals=0)


def plane_of(r, c):
    return 48 + r if c == 6 else 24 * (c // 3) + 3 * r + c % 3


def strip_masks():
    lane = lax.broadcasted_iota(jnp.int32, (8, 128), 1)
    return [((lane - 16 * c + W + 128) % 128) < 2 * W for c in range(NC)]


def strip_kernel(el, mg, mat, strips, edge, edge_strips, ext, matv, sems):
    gz = lax.axis_index("gz")
    loads = [(mat, matv)]
    for c, (which, comp) in enumerate(SOURCE):
        loads.append(((el, mg)[which].at[comp], ext.at[c]))
    copy_all(loads, sems)
    masks = strip_masks()

    def layers(c, t, r):
        rows = pl.ds(64 * t + r, 8, stride=8)
        if c == 6:
            return matv[rows, :].astype(F32)
        v = ext[c, rows, :]
        return v * 2.0 if c >= 3 else v

    def row(r, _):
        for t in range(10):
            total = layers(0, t, r)
            for c in range(1, NC):
                total = jnp.where(masks[c], pltpu.roll(layers(c, t, r), 16 * c, 1), total)
            strips[r, 8 * t : 8 * t + 8, :] = total
        return 0

    lax.fori_loop(0, 8, row, 0)

    def edges(t):
        for r in range(8):
            for c in range(NC):
                edge[plane_of(r, c)] = layers(c, t, r)
        edge_strips[...] = strips[:, 8 * t : 8 * t + 8, :]

    @pl.when(gz == 0)
    def _():
        edges(9)

    @pl.when(gz == 1)
    def _():
        edges(0)


def own_strips(el, mg, mat):
    return pl.pallas_call(
        strip_kernel,
        out_shape=[
            jax.ShapeDtypeStruct((8, 80, 128), F32),
            jax.ShapeDtypeStruct((8 * NC, 8, 128), F32),
            jax.ShapeDtypeStruct((8, 8, 128), F32),
        ],
        in_specs=[HBM] * 3,
        out_specs=[LOCAL] * 3,
        scratch_shapes=[
            pltpu.VMEM((6, 640, 128), F32),
            pltpu.VMEM((640, 128), jnp.int32),
            pltpu.SemaphoreType.DMA((7,)),
        ],
        compiler_params=params(),
        cost_estimate=cost(3),
        name="own_strips",
    )(el, mg, mat)


def pack_kernel(el, mg, mat, own_u, up_u, down_u, own_l, up_l, down_l, ext, matv, planes, sems):
    loads = [(mat, matv)]
    for c, (which, comp) in enumerate(SOURCE):
        loads.append(((el, mg)[which].at[comp], ext.at[c]))
    copy_all(loads, sems)

    def rows_of(first, last):
        def row(r, _):
            for t in range(first, last):
                rows = pl.ds(64 * t + r, 8, stride=8)
                for c in range(NC):
                    if c == 6:
                        v = matv[rows, :].astype(F32)
                    else:
                        v = ext[c, rows, :]
                        if c >= 3:
                            v = v * 2.0
                    planes[plane_of(r, c), 8 * t : 8 * t + 8, :] = v
            return 0

        lax.fori_loop(0, 8, row, 0)

    def sends(first, last, own, up, down):
        z = pl.ds(8 * first, 8 * (last - first))
        pairs = []
        for a, b, n in ((6, 0, 18), (30, 18, 2), (33, 20, 15), (51, 35, 5)):
            pairs.append((planes.at[pl.ds(a, n), z], up.at[pl.ds(b, n)]))
        for a, b, n in ((0, 0, 17), (24, 17, 15), (48, 32, 5)):
            pairs.append((planes.at[pl.ds(a, n), z], down.at[pl.ds(b, n)]))
        pairs.append((planes.at[:, z], own))
        return pairs

    rows_of(CUT, 10)
    pairs = sends(CUT, 10, own_u, up_u, down_u)
    upper = [pltpu.make_async_copy(a, b, sems.at[i]) for i, (a, b) in enumerate(pairs)]
    for copy in upper:
        copy.start()
    rows_of(0, CUT)
    pairs = sends(0, CUT, own_l, up_l, down_l)
    lower = [pltpu.make_async_copy(a, b, sems.at[8 + i]) for i, (a, b) in enumerate(pairs)]
    for copy in lower:
        copy.start()
    for copy in upper + lower:
        copy.wait()


def pack(el, mg, mat):
    shapes = []
    for layers, more in ((8 * (10 - CUT), 0), (8 * CUT, W)):
        shapes += [
            jax.ShapeDtypeStruct((8 * NC, layers, 128), F32),
            jax.ShapeDtypeStruct((40 + more, layers, 128), F32),
            jax.ShapeDtypeStruct((37 + more, layers, 128), F32),
        ]
    return pl.pallas_call(
        pack_kernel,
        out_shape=shapes,
        in_specs=[HBM] * 3,
        out_specs=[HBM] * 6,
        scratch_shapes=[
            pltpu.VMEM((6, 640, 128), F32),
            pltpu.VMEM((640, 128), jnp.int32),
            pltpu.VMEM((8 * NC, 80, 128), F32),
            pltpu.SemaphoreType.DMA((16,)),
        ],
        compiler_params=params(),
        cost_estimate=cost(20),
        name="pack",
    )(el, mg, mat)


def corner_kernel(from_low, from_high, edge_low, edge_high, edge, *refs):
    strips, up, down, up_l, down_l, sems = refs[2:]
    lane = lax.broadcasted_iota(jnp.int32, (8, 80, 128), 2)
    strips[:, 0:80, :] = jnp.where(lane % 16 < 8, from_high[...], from_low[...])
    lane = lax.broadcasted_iota(jnp.int32, (8, 8, 128), 2)
    strips[:, 80:88, :] = jnp.where(lane % 16 < 8, edge_high[...], edge_low[...])
    z = pl.ds(0, 8 * CUT)
    copies = [
        pltpu.make_async_copy(strips.at[pl.ds(8 - W, W), z], up_l.at[pl.ds(40, W)], sems.at[0]),
        pltpu.make_async_copy(strips.at[pl.ds(0, W), z], down_l.at[pl.ds(37, W)], sems.at[1]),
    ]
    for copy in copies:
        copy.start()
    for a, b, n in ((6, 0, 18), (30, 18, 2), (33, 20, 15), (51, 35, 5)):
        up[b : b + n] = edge[a : a + n]
    for a, b, n in ((0, 0, 17), (24, 17, 15), (48, 32, 5)):
        down[b : b + n] = edge[a : a + n]
    for r in range(W):
        for t in range(HIGH):
            z = 8 * (CUT + t)
            up[40 + HIGH * r + t] = strips[8 - W + r, z : z + 8, :]
            down[37 + HIGH * r + t] = strips[r, z : z + 8, :]
    for copy in copies:
        copy.wait()


def corners(from_low, from_high, edge_low, edge_high, edge, up_l, down_l):
    return pl.pallas_call(
        corner_kernel,
        out_shape=[
            jax.ShapeDtypeStruct((8, 88, 128), F32),
            jax.ShapeDtypeStruct((40 + W * HIGH, 8, 128), F32),
            jax.ShapeDtypeStruct((37 + W * HIGH, 8, 128), F32),
            jax.ShapeDtypeStruct(up_l.shape, F32),
            jax.ShapeDtypeStruct(down_l.shape, F32),
        ],
        in_specs=[LOCAL] * 5 + [HBM] * 2,
        out_specs=[LOCAL] * 3 + [HBM] * 2,
        scratch_shapes=[pltpu.SemaphoreType.DMA((2,))],
        input_output_aliases={5: 3, 6: 4},
        compiler_params=params(),
        cost_estimate=cost(1),
        name="corners",
    )(from_low, from_high, edge_low, edge_high, edge, up_l, down_l)


def steps_kernel(upper, decay, gain, low_c, high_c, strips, edge, *refs):
    gz = lax.axis_index("gz")
    nu, nl = 8 * (10 - CUT), 8 * CUT
    own_u, low_u, high_u = refs[:3]
    if upper:
        out, plane, *scratch = refs[3:]
        tiles, halo, counts = 11 - CUT, 10 - CUT, gz == 0
        sets = [((own_u, low_u, high_u), 0, nu, 0, nl)]
    else:
        own_l, low_l, high_l, _, out, *scratch = refs[3:]
        tiles, halo, counts = CUT + 3, 0, gz == 1
        sets = [
            ((own_l, low_l, high_l), 0, nl, 8, 0),
            ((own_u, low_u, high_u), 0, 16, 8 + nl, nl),
        ]
    on = 9 - CUT if upper else CUT + 1
    ea0, ea1, eb0, eb1, ma0, ma1, mb0, mb1, d0, d1, g0, g1, ya, yb, ym, sv, stage, sems = scratch
    es, ms, yes = ((ea0, ea1), (eb0, eb1)), ((ma0, ma1), (mb0, mb1)), (ya, yb)
    ds_, gs = (d0, d1), (g0, g1)

    first, mid, last_ = BASE, BASE + W, BASE + W + 8
    hz = 8 * halo
    moves = [(strips.at[:, pl.ds(80, 8)], sv.at[pl.ds(W, 8), pl.ds(hz, 8)])]
    for (own, low, high), start, layers, to, strip in sets:
        zd = pl.ds(to, layers)
        moves.append((strips.at[:, pl.ds(strip, layers)], sv.at[pl.ds(W, 8), zd]))
        if not upper and own is own_l:
            moves.append((low.at[pl.ds(40, W)], sv.at[pl.ds(0, W), zd]))
            moves.append((high.at[pl.ds(37, W)], sv.at[pl.ds(W + 8, W), zd]))
    early = len(moves)
    own_parts = ((0, 24, ea0, 3 * mid), (24, 24, ma0, 3 * mid), (48, 8, d0, mid))
    low_parts = (
        (0, 18, ea0, 3 * first),
        (18, 2, ma0, 3 * first),
        (20, 15, ma0, 3 * first + 3),
        (35, 5, d0, first + 1),
    )
    high_parts = ((0, 17, ea0, 3 * last_), (17, 15, ma0, 3 * last_), (32, 5, d0, last_))
    for (own, low, high), start, layers, to, strip in sets:
        for ref, parts in ((own, own_parts), (low, low_parts), (high, high_parts)):
            for a, n, dst, b in parts:
                z = pl.ds(to if dst is d0 else 8 + to, layers)
                moves.append((ref.at[pl.ds(a, n), pl.ds(start, layers)], dst.at[pl.ds(b, n), z]))
    for a, n, dst, b in own_parts:
        z = pl.ds(hz if dst is d0 else 8 + hz, 8)
        moves.append((edge.at[pl.ds(a, n)], dst.at[pl.ds(b, n), z]))
    copies = [pltpu.make_async_copy(a, b, sems.at[i]) for i, (a, b) in enumerate(moves)]
    for copy in copies:
        copy.start()
    for ref, parts in ((low_c, low_parts), (high_c, high_parts)):
        for a, n, dst, b in parts:
            z = hz if dst is d0 else 8 + hz
            for i in range(n):
                dst[b + i, z : z + 8, :] = ref[a + i]
    here = [(t, t) for t in range(HIGH)]
    if not upper:
        here = [(0, HIGH - 1), (CUT + 1, 0), (CUT + 2, 1)]
    for r in range(W):
        for t, u in here:
            sv[r, 8 * t : 8 * t + 8, :] = low_c[40 + HIGH * r + u]
            sv[W + 8 + r, 8 * t : 8 * t + 8, :] = high_c[37 + HIGH * r + u]

    zero = jnp.zeros((8, 128), F32)
    top = 8 + 8 * tiles

    def ends(r, _):
        for pair in ms:
            for m in pair:
                m[3 * r + X, 0:8, :] = zero
                m[3 * r + Y, 0:8, :] = zero
        for pair in es:
            for e in pair:
                e[3 * r + X, top : top + 8, :] = zero
                e[3 * r + Y, top : top + 8, :] = zero
        return 0

    lax.fori_loop(0, HELD, ends, 0)
    for copy in copies[:early]:
        copy.wait()

    def unpack(r, _):
        at = BASE + r
        for t in range(tiles):
            z = 8 * t
            v = sv[r, z : z + 8, :]
            for c in range(NC):
                turned = pltpu.roll(v, 128 - 16 * c, 1) if c else v
                if c < 3:
                    ea1[3 * at + c, 8 + z : 16 + z, :] = turned
                elif c < 6:
                    ma1[3 * at + c - 3, 8 + z : 16 + z, :] = turned
                else:
                    d1[at, z : z + 8, :] = turned
        return 0

    lax.fori_loop(0, ROWS, unpack, 0)
    for copy in copies[early:]:
        copy.wait()

    @pl.when(jnp.logical_not(counts))
    def _():
        def clear(i, _):
            for ref in (ea0, ea1, ma0, ma1):
                ref[3 * BASE + i, hz + 8 : hz + 16, :] = zero
            return 0

        lax.fori_loop(0, 3 * ROWS, clear, 0)

    live = jnp.where(counts, 1.0, 0.0).astype(F32)

    def tables(r, _):
        for t in range(tiles):
            z = 8 * t
            for d, g in zip(ds_, gs):
                ids = d[r, z : z + 8, :]
                d_cells, g_cells = zero, zero
                for i in range(5):
                    hit = ids == float(i)
                    d_cells = jnp.where(hit, decay[i], d_cells)
                    g_cells = jnp.where(hit, gain[i] * 0.5, g_cells)
                if t == halo:
                    d_cells, g_cells = d_cells * live, g_cells * live
                d[r, z : z + 8, :] = d_cells
                g[r, z : z + 8, :] = g_cells
        return 0

    lax.fori_loop(BASE + 1, BASE + ROWS - 1, tables, 0)

    lane = lax.broadcasted_iota(jnp.int32, (8, 128), 1)
    last, first_lane = lane == 127, lane == 0
    units = [(row, t) for row in range(2) for t in range(tiles)]

    def turn_two(which, r0):
        kept = []
        for row, t in units:
            for j, c in enumerate((X, Z)):
                pair = [
                    pltpu.roll(e[3 * r0 + (3 * row + c), 8 + 8 * t : 16 + 8 * t, :], 127, 1)
                    for e in es[which]
                ]
                kept.append((4 * row + 2 * j, 8 * t, pair))
        y = yes[which]
        for i, z, (a, b) in kept:
            y[4 * r0 + i, z : z + 8, :] = jnp.where(last, b, a)
            y[4 * r0 + (i + 1), z : z + 8, :] = jnp.where(last, a, b)

    def first_turn(i, _):
        turn_two(0, BASE + 2 * i)
        return 0

    lax.fori_loop(0, ROWS // 2, first_turn, 0)

    def block(old, with_e, with_m, m, start):
        new = 1 - old
        base = start + 2 * m
        b3, b4 = 3 * base, 4 * base
        waiting = []
        half = len(units) // 2
        jobs_m = [(ms, row, t) for row, t in units] if with_e else []
        jobs_e = [(es, row, t) for row, t in units] if with_e else []

        def turn(refs, row, t):
            z = 8 * t
            if refs is ms:
                pairs = [
                    [pltpu.roll(f[b3 + (3 * (row - 2) + c), 8 + z : 16 + z, :], 1, 1) for f in ms[new]]
                    for c in (X, Z)
                ]
                waiting.append((ym, 0, 4 * row, z, pairs, first_lane))
            else:
                pairs = [
                    [pltpu.roll(f[b3 + (3 * (row - 4) + c), 8 + z : 16 + z, :], 127, 1) for f in es[new]]
                    for c in (X, Z)
                ]
                waiting.append((yes[new], b4, 4 * (row - 4), z, pairs, last))

        def keep():
            y, b, i, z, pairs, edge_lane = waiting.pop(0)
            for j, (v0, v1) in enumerate(pairs):
                y[b + (i + 2 * j), z : z + 8, :] = jnp.where(edge_lane, v1, v0)
                y[b + (i + 2 * j + 1), z : z + 8, :] = jnp.where(edge_lane, v0, v1)

        def settle(most):
            while len(waiting) > most:
                keep()

        for u, (row, t) in enumerate(units if with_m else ()):
            if jobs_m:
                turn(*jobs_m.pop(0))
                if u >= half:
                    turn(*jobs_e.pop(0))
            settle(LAG)
            z = 8 * t
            for k in range(2):

                def electric(c, r=row, shift=0):
                    return es[old][k][b3 + (3 * r + c), 8 + z + shift : 16 + z + shift, :]

                def magnetic(c):
                    return ms[old][k][b3 + (3 * row + c), 8 + z : 16 + z, :]

                ex_y = yes[old][b4 + (4 * row + k), z : z + 8, :]
                ez_y = yes[old][b4 + (4 * row + 2 + k), z : z + 8, :]
                ex, ey, ez = electric(X), electric(Y), electric(Z)
                cx = (ez_y - ez) - (electric(Y, row, 1) - ey)
                cy = (electric(X, row, 1) - ex) - (electric(Z, row + 1) - ez)
                cz = (electric(Y, row + 1) - ey) - (ex_y - ex)
                if t == halo and not upper:
                    cx, cy, cz = cx * live, cy * live, cz * live
                mx, my, mz = magnetic(X) - cx, magnetic(Y) - cy, magnetic(Z) - cz
                for c, v in ((X, mx), (Y, my), (Z, mz)):
                    ms[new][k][b3 + (3 * row + c), 8 + z : 16 + z, :] = v
        for job in jobs_m:
            turn(*job)
            settle(LAG)
        for row, t in units if with_e else ():
            if jobs_e:
                turn(*jobs_e.pop(0))
            settle(LAG if jobs_e else max(len(waiting) - 2, 0))
            e, z = row - 2, 8 * t
            for k in range(2):

                def magnetic(c, r=e, shift=0):
                    return ms[new][k][b3 + (3 * r + c), 8 + z + shift : 16 + z + shift, :]

                def electric(c):
                    return es[old][k][b3 + (3 * e + c), 8 + z : 16 + z, :]

                mx_y = ym[4 * row + k, z : z + 8, :]
                mz_y = ym[4 * row + 2 + k, z : z + 8, :]
                mx, my, mz = magnetic(X), magnetic(Y), magnetic(Z)
                d = ds_[k][base + e, z : z + 8, :]
                g = gs[k][base + e, z : z + 8, :]
                ex = d * electric(X) + g * ((mz - mz_y) - (my - magnetic(Y, e, -1)))
                ey = d * electric(Y) + g * ((mx - magnetic(X, e, -1)) - (mz - magnetic(Z, e - 1)))
                ez = d * electric(Z) + g * ((my - magnetic(Y, e - 1)) - (mx - mx_y))
                for c, v in ((X, ex), (Y, ey), (Z, ez)):
                    es[new][k][b3 + (3 * e + c), 8 + z : 16 + z, :] = v
        settle(0)
        return start

    def two_steps(s, _):
        for old in range(2):
            left = STEPS - 1 - old - 2 * s
            start = BASE + W - left - 2
            block(old, False, True, 0, start)
            lax.fori_loop(1, W - 1 + left, functools.partial(block, old, True, True), start)
            block(old, True, False, W - 1 + left, start)
            turn_two(1 - old, start + 2 * (W - 2 + left))
        return 0

    lax.fori_loop(0, STEPS // 2, two_steps, 0)

    def emit(r, _):
        for c, source in enumerate((X, Y, Z)):
            for t in range(on):
                stage[c, pl.ds(64 * t + r, 8, stride=8), :] = ea0[
                    3 * (r + BASE + W) + source, 16 + 8 * t : 24 + 8 * t, :
                ]
        return 0

    lax.fori_loop(0, 8, emit, 0)
    if upper:
        plane[0] = stage[0, 64 * on - 8 : 64 * on, :]
        plane[1] = stage[1, 64 * on - 8 : 64 * on, :]
    copy_all([(stage, out.at[:, pl.ds(64 * (CUT + 1) if upper else 0, 64 * on)])], sems)


def run_steps(upper, decay, gain, sides, arrays):
    smem = pl.BlockSpec(memory_space=pltpu.SMEM)
    out_shape = [jax.ShapeDtypeStruct((3, 640, 128), F32)]
    out_specs = [HBM]
    aliases = {}
    if upper:
        out_shape.append(jax.ShapeDtypeStruct((2, 8, 128), F32))
        out_specs.append(LOCAL)
    else:
        aliases = {6 + len(arrays) - 1: 0}
    tiles, on = (11 - CUT, 9 - CUT) if upper else (CUT + 3, CUT + 1)
    z = 16 + 8 * tiles
    field = pltpu.VMEM((3 * HELD, z, 128), F32)
    table = pltpu.VMEM((HELD, 8 * tiles, 128), F32)
    turned = pltpu.VMEM((4 * HELD, 8 * tiles, 128), F32)
    return pl.pallas_call(
        functools.partial(steps_kernel, upper),
        out_shape=out_shape,
        in_specs=[smem, smem, LOCAL, LOCAL] + [HBM] * (2 + len(arrays)),
        out_specs=out_specs,
        scratch_shapes=[field] * 8
        + [table] * 4
        + [turned] * 2
        + [
            pltpu.VMEM((8, 8 * tiles, 128), F32),
            pltpu.VMEM((ROWS, 8 * tiles, 128), F32),
            pltpu.VMEM((3, 64 * on, 128), F32),
            pltpu.SemaphoreType.DMA((39,)),
        ],
        input_output_aliases=aliases,
        compiler_params=params(),
        cost_estimate=cost(100),
        name="steps_upper" if upper else "steps_lower",
    )(decay, gain, *sides, *arrays)


def image_kernel(weights, own, received, out, sh, rhs):
    gz = lax.axis_index("gz")
    centre, before, after = [
        [jnp.where(gz == 1, own[i, c], received[i, c]) for c in range(2)] for i in range(3)
    ]
    lane = lax.broadcasted_iota(jnp.int32, (24, 128), 1)
    for q in range(15):
        shift = q - 7
        for c in range(2):
            v = centre[c]
            if shift > 0:
                v = jnp.where(
                    lane >= 128 - shift,
                    pltpu.roll(after[c], 128 - shift, 1),
                    pltpu.roll(v, 128 - shift, 1),
                )
            elif shift < 0:
                v = jnp.where(
                    lane < -shift, pltpu.roll(before[c], -shift, 1), pltpu.roll(v, -shift, 1)
                )
            sh[q, c] = v

    def fill(side):
        for q in range(15):
            for c in range(2):
                for i in range(4):
                    start = 4 * side + 1 + i
                    rhs[16 * q : 16 * q + 16, (4 * c + i) * 128 : (4 * c + i + 1) * 128] = sh[
                        q, c, start : start + 16, :
                    ]

    @pl.when(gz == 0)
    def _():
        fill(0)

    @pl.when(gz == 1)
    def _():
        fill(1)

    amplitude = jnp.dot(
        weights[...],
        rhs[...],
        precision=lax.Precision.HIGHEST,
        preferred_element_type=jnp.float32,
    )
    power = jnp.sum(amplitude * amplitude, axis=0, keepdims=True)
    for i in range(4):
        out[i : i + 1, :] = (
            power[:, i * 128 : (i + 1) * 128] + power[:, (4 + i) * 128 : (5 + i) * 128]
        )


def image_of(weights, own, received):
    return pl.pallas_call(
        image_kernel,
        out_shape=jax.ShapeDtypeStruct((4, 128), jnp.float32),
        in_specs=[LOCAL] * 3,
        out_specs=LOCAL,
        scratch_shapes=[
            pltpu.VMEM((15, 2, 24, 128), jnp.float32),
            pltpu.VMEM((240, 1024), jnp.float32),
        ],
        compiler_params=pltpu.CompilerParams(vmem_limit_bytes=VMEM),
        name="image",
    )(weights, own, received)


def on_device(electric, magnetic, material, decay, gain, kernels):
    el = electric.reshape(3, 640, 128)
    mg = magnetic.reshape(3, 640, 128)
    mat = material.reshape(640, 128)
    weights = jnp.pad(
        kernels.transpose(0, 1, 3, 2).reshape(48, 15, 15), ((0, 0), (0, 0), (0, 1))
    ).reshape(48, 240)

    strips, edge, edge_strips = own_strips(el, mg, mat)
    edge = around(edge, "gz", 1)
    from_low, from_high = around(strips, "gy", 1), around(strips, "gy", -1)
    edge_low, edge_high = beyond(edge_strips, 1), beyond(edge_strips, -1)
    own_u, up_u, down_u, own_l, up_l, down_l = pack(el, mg, mat)
    up_u, down_u, edge_low, edge_high = lax.optimization_barrier(
        (up_u, down_u, edge_low, edge_high)
    )
    low_u, high_u = around(up_u, "gx", 1), around(down_u, "gx", -1)
    strips, up_c, down_c, up_l, down_l = corners(
        from_low, from_high, edge_low, edge_high, edge, up_l, down_l
    )
    low_c, high_c = around(up_c, "gx", 1), around(down_c, "gx", -1)
    low_l, high_l = around(up_l, "gx", 1), around(down_l, "gx", -1)

    sides = [low_c, high_c, strips, edge]
    field, plane = run_steps(True, decay, gain, sides, [own_u, low_u, high_u])
    top = jnp.stack([plane, around(plane, "gy", 1), around(plane, "gy", -1)])
    top = jnp.concatenate([around(top, "gx", 1), top, around(top, "gx", -1)], 2)
    top, low_l, high_l = lax.optimization_barrier((top, low_l, high_l))
    received = lax.ppermute(top, "gz", [(1, 0)])
    (field,) = run_steps(
        False, decay, gain, sides, [own_u, low_u, high_u, own_l, low_l, high_l, field]
    )
    image = image_of(weights, top, received)
    return (field.reshape(3, 80, 8, 128), image)


def solution(mesh):
    in_specs = (
        P(None, "gz", "gx", "gy"),
        P(None, "gz", "gx", "gy"),
        P("gz", "gx", "gy"),
        P(),
        P(),
        P(),
    )
    out_specs = (P(None, "gz", "gx", "gy"), P(("gx", "gz"), "gy"))
    return jax.shard_map(
        on_device, mesh=mesh, in_specs=in_specs, out_specs=out_specs, check_vma=False
    )
```

```python
import functools

import jax
import jax.numpy as jnp
from jax import lax
from jax.experimental import pallas as pl
from jax.experimental.pallas import tpu as pltpu
from jax.sharding import PartitionSpec as P

STEPS = 6
W = STEPS
Y, Z, X = range(3)
NC = 7
SOURCE = ((0, 1), (0, 2), (0, 0), (1, 1), (1, 2), (1, 0))
ROWS = 8 + 2 * W
BASE = 4
HELD = BASE + ROWS + 2
CUT = 8
HIGH = 11 - CUT
LAG = 4
VMEM = 63 * 1024 * 1024
F32 = jnp.float32
HBM = pl.BlockSpec(memory_space=pl.ANY)
LOCAL = pl.BlockSpec(memory_space=pltpu.VMEM)


def around(value, axis, steps):
    count = lax.axis_size(axis)
    return lax.ppermute(value, axis, [(i, (i + steps) % count) for i in range(count)])


def beyond(value, steps):
    ny, nz = lax.axis_size("gy"), lax.axis_size("gz")
    pairs = [
        (y * nz + z, (y + steps) % ny * nz + (z + 1) % nz) for y in range(ny) for z in range(nz)
    ]
    return lax.ppermute(value, ("gy", "gz"), pairs)


def copy_all(pairs, sems):
    copies = [pltpu.make_async_copy(a, b, sems.at[i]) for i, (a, b) in enumerate(pairs)]
    for copy in copies:
        copy.start()
    for copy in copies:
        copy.wait()


def params():
    return pltpu.CompilerParams(vmem_limit_bytes=VMEM)


def cost(us):
    return pl.CostEstimate(flops=int(us * 1e9), bytes_accessed=int(us * 3e6), transcendentals=0)


def plane_of(r, c):
    return 48 + r if c == 6 else 24 * (c // 3) + 3 * r + c % 3


def strip_masks():
    lane = lax.broadcasted_iota(jnp.int32, (8, 128), 1)
    return [((lane - 16 * c + W + 128) % 128) < 2 * W for c in range(NC)]


def strip_kernel(el, mg, mat, strips, edge, edge_strips, ext, matv, sems):
    gz = lax.axis_index("gz")
    loads = [(mat, matv)]
    for c, (which, comp) in enumerate(SOURCE):
        loads.append(((el, mg)[which].at[comp], ext.at[c]))
    copy_all(loads, sems)
    masks = strip_masks()

    def layers(c, t, r):
        rows = pl.ds(64 * t + r, 8, stride=8)
        if c == 6:
            return matv[rows, :].astype(F32)
        v = ext[c, rows, :]
        return v * 2.0 if c >= 3 else v

    def row(r, _):
        for t in range(10):
            total = layers(0, t, r)
            for c in range(1, NC):
                total = jnp.where(masks[c], pltpu.roll(layers(c, t, r), 16 * c, 1), total)
            strips[r, 8 * t : 8 * t + 8, :] = total
        return 0

    lax.fori_loop(0, 8, row, 0)

    def edges(t):
        for r in range(8):
            for c in range(NC):
                edge[plane_of(r, c)] = layers(c, t, r)
        edge_strips[...] = strips[:, 8 * t : 8 * t + 8, :]

    @pl.when(gz == 0)
    def _():
        edges(9)

    @pl.when(gz == 1)
    def _():
        edges(0)


def own_strips(el, mg, mat):
    return pl.pallas_call(
        strip_kernel,
        out_shape=[
            jax.ShapeDtypeStruct((8, 80, 128), F32),
            jax.ShapeDtypeStruct((8 * NC, 8, 128), F32),
            jax.ShapeDtypeStruct((8, 8, 128), F32),
        ],
        in_specs=[HBM] * 3,
        out_specs=[LOCAL] * 3,
        scratch_shapes=[
            pltpu.VMEM((6, 640, 128), F32),
            pltpu.VMEM((640, 128), jnp.int32),
            pltpu.SemaphoreType.DMA((7,)),
        ],
        compiler_params=params(),
        cost_estimate=cost(3),
        name="own_strips",
    )(el, mg, mat)


def pack_kernel(el, mg, mat, own_u, up_u, down_u, own_l, up_l, down_l, ext, matv, planes, sems):
    loads = [(mat, matv)]
    for c, (which, comp) in enumerate(SOURCE):
        loads.append(((el, mg)[which].at[comp], ext.at[c]))
    copy_all(loads, sems)

    def rows_of(first, last):
        def row(r, _):
            for t in range(first, last):
                rows = pl.ds(64 * t + r, 8, stride=8)
                for c in range(NC):
                    if c == 6:
                        v = matv[rows, :].astype(F32)
                    else:
                        v = ext[c, rows, :]
                        if c >= 3:
                            v = v * 2.0
                    planes[plane_of(r, c), 8 * t : 8 * t + 8, :] = v
            return 0

        lax.fori_loop(0, 8, row, 0)

    def sends(first, last, own, up, down):
        z = pl.ds(8 * first, 8 * (last - first))
        pairs = []
        for a, b, n in ((6, 0, 18), (30, 18, 2), (33, 20, 15), (51, 35, 5)):
            pairs.append((planes.at[pl.ds(a, n), z], up.at[pl.ds(b, n)]))
        for a, b, n in ((0, 0, 17), (24, 17, 15), (48, 32, 5)):
            pairs.append((planes.at[pl.ds(a, n), z], down.at[pl.ds(b, n)]))
        pairs.append((planes.at[:, z], own))
        return pairs

    rows_of(CUT, 10)
    pairs = sends(CUT, 10, own_u, up_u, down_u)
    upper = [pltpu.make_async_copy(a, b, sems.at[i]) for i, (a, b) in enumerate(pairs)]
    for copy in upper:
        copy.start()
    rows_of(0, CUT)
    pairs = sends(0, CUT, own_l, up_l, down_l)
    lower = [pltpu.make_async_copy(a, b, sems.at[8 + i]) for i, (a, b) in enumerate(pairs)]
    for copy in lower:
        copy.start()
    for copy in upper + lower:
        copy.wait()


def pack(el, mg, mat):
    shapes = []
    for layers, more in ((8 * (10 - CUT), 0), (8 * CUT, W)):
        shapes += [
            jax.ShapeDtypeStruct((8 * NC, layers, 128), F32),
            jax.ShapeDtypeStruct((40 + more, layers, 128), F32),
            jax.ShapeDtypeStruct((37 + more, layers, 128), F32),
        ]
    return pl.pallas_call(
        pack_kernel,
        out_shape=shapes,
        in_specs=[HBM] * 3,
        out_specs=[HBM] * 6,
        scratch_shapes=[
            pltpu.VMEM((6, 640, 128), F32),
            pltpu.VMEM((640, 128), jnp.int32),
            pltpu.VMEM((8 * NC, 80, 128), F32),
            pltpu.SemaphoreType.DMA((16,)),
        ],
        compiler_params=params(),
        cost_estimate=cost(20),
        name="pack",
    )(el, mg, mat)


def corner_kernel(from_low, from_high, edge_low, edge_high, edge, *refs):
    strips, up, down, up_l, down_l, sems = refs[2:]
    lane = lax.broadcasted_iota(jnp.int32, (8, 80, 128), 2)
    strips[:, 0:80, :] = jnp.where(lane % 16 < 8, from_high[...], from_low[...])
    lane = lax.broadcasted_iota(jnp.int32, (8, 8, 128), 2)
    strips[:, 80:88, :] = jnp.where(lane % 16 < 8, edge_high[...], edge_low[...])
    z = pl.ds(0, 8 * CUT)
    copies = [
        pltpu.make_async_copy(strips.at[pl.ds(8 - W, W), z], up_l.at[pl.ds(40, W)], sems.at[0]),
        pltpu.make_async_copy(strips.at[pl.ds(0, W), z], down_l.at[pl.ds(37, W)], sems.at[1]),
    ]
    for copy in copies:
        copy.start()
    for a, b, n in ((6, 0, 18), (30, 18, 2), (33, 20, 15), (51, 35, 5)):
        up[b : b + n] = edge[a : a + n]
    for a, b, n in ((0, 0, 17), (24, 17, 15), (48, 32, 5)):
        down[b : b + n] = edge[a : a + n]
    for r in range(W):
        for t in range(HIGH):
            z = 8 * (CUT + t)
            up[40 + HIGH * r + t] = strips[8 - W + r, z : z + 8, :]
            down[37 + HIGH * r + t] = strips[r, z : z + 8, :]
    for copy in copies:
        copy.wait()


def corners(from_low, from_high, edge_low, edge_high, edge, up_l, down_l):
    return pl.pallas_call(
        corner_kernel,
        out_shape=[
            jax.ShapeDtypeStruct((8, 88, 128), F32),
            jax.ShapeDtypeStruct((40 + W * HIGH, 8, 128), F32),
            jax.ShapeDtypeStruct((37 + W * HIGH, 8, 128), F32),
            jax.ShapeDtypeStruct(up_l.shape, F32),
            jax.ShapeDtypeStruct(down_l.shape, F32),
        ],
        in_specs=[LOCAL] * 5 + [HBM] * 2,
        out_specs=[LOCAL] * 3 + [HBM] * 2,
        scratch_shapes=[pltpu.SemaphoreType.DMA((2,))],
        input_output_aliases={5: 3, 6: 4},
        compiler_params=params(),
        cost_estimate=cost(1),
        name="corners",
    )(from_low, from_high, edge_low, edge_high, edge, up_l, down_l)


def steps_kernel(upper, decay, gain, low_c, high_c, strips, edge, *refs):
    gz = lax.axis_index("gz")
    nu, nl = 8 * (10 - CUT), 8 * CUT
    own_u, low_u, high_u = refs[:3]
    if upper:
        out, plane, *scratch = refs[3:]
        tiles, halo, counts = 11 - CUT, 10 - CUT, gz == 0
        sets = [((own_u, low_u, high_u), 0, nu, 0, nl)]
    else:
        own_l, low_l, high_l, _, out, *scratch = refs[3:]
        tiles, halo, counts = CUT + 3, 0, gz == 1
        sets = [
            ((own_l, low_l, high_l), 0, nl, 8, 0),
            ((own_u, low_u, high_u), 0, 16, 8 + nl, nl),
        ]
    on = 9 - CUT if upper else CUT + 1
    ea0, ea1, eb0, eb1, ma0, ma1, mb0, mb1, d0, d1, g0, g1, ya, yb, ym, sv, stage, sems = scratch
    es, ms, yes = ((ea0, ea1), (eb0, eb1)), ((ma0, ma1), (mb0, mb1)), (ya, yb)
    ds_, gs = (d0, d1), (g0, g1)

    first, mid, last_ = BASE, BASE + W, BASE + W + 8
    hz = 8 * halo
    moves = [(strips.at[:, pl.ds(80, 8)], sv.at[pl.ds(W, 8), pl.ds(hz, 8)])]
    for (own, low, high), start, layers, to, strip in sets:
        zd = pl.ds(to, layers)
        moves.append((strips.at[:, pl.ds(strip, layers)], sv.at[pl.ds(W, 8), zd]))
        if not upper and own is own_l:
            moves.append((low.at[pl.ds(40, W)], sv.at[pl.ds(0, W), zd]))
            moves.append((high.at[pl.ds(37, W)], sv.at[pl.ds(W + 8, W), zd]))
    early = len(moves)
    own_parts = ((0, 24, ea0, 3 * mid), (24, 24, ma0, 3 * mid), (48, 8, d0, mid))
    low_parts = (
        (0, 18, ea0, 3 * first),
        (18, 2, ma0, 3 * first),
        (20, 15, ma0, 3 * first + 3),
        (35, 5, d0, first + 1),
    )
    high_parts = ((0, 17, ea0, 3 * last_), (17, 15, ma0, 3 * last_), (32, 5, d0, last_))
    for (own, low, high), start, layers, to, strip in sets:
        for ref, parts in ((own, own_parts), (low, low_parts), (high, high_parts)):
            for a, n, dst, b in parts:
                z = pl.ds(to if dst is d0 else 8 + to, layers)
                moves.append((ref.at[pl.ds(a, n), pl.ds(start, layers)], dst.at[pl.ds(b, n), z]))
    for a, n, dst, b in own_parts:
        z = pl.ds(hz if dst is d0 else 8 + hz, 8)
        moves.append((edge.at[pl.ds(a, n)], dst.at[pl.ds(b, n), z]))
    copies = [pltpu.make_async_copy(a, b, sems.at[i]) for i, (a, b) in enumerate(moves)]
    for copy in copies:
        copy.start()
    for ref, parts in ((low_c, low_parts), (high_c, high_parts)):
        for a, n, dst, b in parts:
            z = hz if dst is d0 else 8 + hz
            for i in range(n):
                dst[b + i, z : z + 8, :] = ref[a + i]
    here = [(t, t) for t in range(HIGH)]
    if not upper:
        here = [(0, HIGH - 1), (CUT + 1, 0), (CUT + 2, 1)]
    for r in range(W):
        for t, u in here:
            sv[r, 8 * t : 8 * t + 8, :] = low_c[40 + HIGH * r + u]
            sv[W + 8 + r, 8 * t : 8 * t + 8, :] = high_c[37 + HIGH * r + u]

    zero = jnp.zeros((8, 128), F32)
    top = 8 + 8 * tiles

    def ends(r, _):
        for pair in ms:
            for m in pair:
                m[3 * r + X, 0:8, :] = zero
                m[3 * r + Y, 0:8, :] = zero
        for pair in es:
            for e in pair:
                e[3 * r + X, top : top + 8, :] = zero
                e[3 * r + Y, top : top + 8, :] = zero
        return 0

    lax.fori_loop(0, HELD, ends, 0)
    for copy in copies[:early]:
        copy.wait()

    def unpack(i, _):
        for row in range(2):
            r = 2 * i + row
            at = BASE + r
            for t in range(tiles):
                z = 8 * t
                v = sv[r, z : z + 8, :]
                for c in range(NC):
                    turned = pltpu.roll(v, 128 - 16 * c, 1) if c else v
                    if c < 3:
                        ea1[3 * at + c, 8 + z : 16 + z, :] = turned
                    elif c < 6:
                        ma1[3 * at + c - 3, 8 + z : 16 + z, :] = turned
                    else:
                        d1[at, z : z + 8, :] = turned
        return 0

    lax.fori_loop(0, ROWS // 2, unpack, 0)
    for copy in copies[early:]:
        copy.wait()

    @pl.when(jnp.logical_not(counts))
    def _():
        def clear(i, _):
            for ref in (ea0, ea1, ma0, ma1):
                ref[3 * BASE + i, hz + 8 : hz + 16, :] = zero
            return 0

        lax.fori_loop(0, 3 * ROWS, clear, 0)

    live = jnp.where(counts, 1.0, 0.0).astype(F32)

    lane = lax.broadcasted_iota(jnp.int32, (8, 128), 1)
    last, first_lane = lane == 127, lane == 0
    units = [(row, t) for row in range(2) for t in range(tiles)]

    def tables(r):
        for t in range(tiles):
            z = 8 * t
            for d, g in zip(ds_, gs):
                ids = d[r, z : z + 8, :]
                d_cells, g_cells = zero, zero
                for i in range(5):
                    hit = ids == float(i)
                    d_cells = jnp.where(hit, decay[i], d_cells)
                    g_cells = jnp.where(hit, gain[i] * 0.5, g_cells)
                if t == halo:
                    d_cells, g_cells = d_cells * live, g_cells * live
                d[r, z : z + 8, :] = d_cells
                g[r, z : z + 8, :] = g_cells

    def turn_two(which, r0, beside=None):
        kept = []
        for row, t in units:
            for j, c in enumerate((X, Z)):
                pair = [
                    pltpu.roll(e[3 * r0 + (3 * row + c), 8 + 8 * t : 16 + 8 * t, :], 127, 1)
                    for e in es[which]
                ]
                kept.append((4 * row + 2 * j, 8 * t, pair))
        if beside:
            beside()
        y = yes[which]
        for i, z, (a, b) in kept:
            y[4 * r0 + i, z : z + 8, :] = jnp.where(last, b, a)
            y[4 * r0 + (i + 1), z : z + 8, :] = jnp.where(last, a, b)

    def first_turn(i, _):
        r0 = BASE + 2 * i

        def both():
            tables(r0)
            tables(r0 + 1)

        turn_two(0, r0, both)
        return 0

    lax.fori_loop(0, ROWS // 2, first_turn, 0)

    def block(old, with_e, with_m, m, start):
        new = 1 - old
        base = start + 2 * m
        b3, b4 = 3 * base, 4 * base
        waiting = []
        half = len(units) // 2
        jobs_m = [(ms, row, t) for row, t in units] if with_e else []
        jobs_e = [(es, row, t) for row, t in units] if with_e else []

        def turn(refs, row, t):
            z = 8 * t
            if refs is ms:
                pairs = [
                    [pltpu.roll(f[b3 + (3 * (row - 2) + c), 8 + z : 16 + z, :], 1, 1) for f in ms[new]]
                    for c in (X, Z)
                ]
                waiting.append((ym, 0, 4 * row, z, pairs, first_lane))
            else:
                pairs = [
                    [pltpu.roll(f[b3 + (3 * (row - 4) + c), 8 + z : 16 + z, :], 127, 1) for f in es[new]]
                    for c in (X, Z)
                ]
                waiting.append((yes[new], b4, 4 * (row - 4), z, pairs, last))

        def keep():
            y, b, i, z, pairs, edge_lane = waiting.pop(0)
            for j, (v0, v1) in enumerate(pairs):
                y[b + (i + 2 * j), z : z + 8, :] = jnp.where(edge_lane, v1, v0)
                y[b + (i + 2 * j + 1), z : z + 8, :] = jnp.where(edge_lane, v0, v1)

        def settle(most):
            while len(waiting) > most:
                keep()

        for u, (row, t) in enumerate(units if with_m else ()):
            if jobs_m:
                turn(*jobs_m.pop(0))
                if u >= half:
                    turn(*jobs_e.pop(0))
            settle(LAG)
            z = 8 * t
            for k in range(2):

                def electric(c, r=row, shift=0):
                    return es[old][k][b3 + (3 * r + c), 8 + z + shift : 16 + z + shift, :]

                def magnetic(c):
                    return ms[old][k][b3 + (3 * row + c), 8 + z : 16 + z, :]

                ex_y = yes[old][b4 + (4 * row + k), z : z + 8, :]
                ez_y = yes[old][b4 + (4 * row + 2 + k), z : z + 8, :]
                ex, ey, ez = electric(X), electric(Y), electric(Z)
                cx = (ez_y - ez) - (electric(Y, row, 1) - ey)
                cy = (electric(X, row, 1) - ex) - (electric(Z, row + 1) - ez)
                cz = (electric(Y, row + 1) - ey) - (ex_y - ex)
                if t == halo and not upper:
                    cx, cy, cz = cx * live, cy * live, cz * live
                mx, my, mz = magnetic(X) - cx, magnetic(Y) - cy, magnetic(Z) - cz
                for c, v in ((X, mx), (Y, my), (Z, mz)):
                    ms[new][k][b3 + (3 * row + c), 8 + z : 16 + z, :] = v
        for job in jobs_m:
            turn(*job)
            settle(LAG)
        for row, t in units if with_e else ():
            if jobs_e:
                turn(*jobs_e.pop(0))
            settle(LAG if jobs_e else max(len(waiting) - 2, 0))
            e, z = row - 2, 8 * t
            for k in range(2):

                def magnetic(c, r=e, shift=0):
                    return ms[new][k][b3 + (3 * r + c), 8 + z + shift : 16 + z + shift, :]

                def electric(c):
                    return es[old][k][b3 + (3 * e + c), 8 + z : 16 + z, :]

                mx_y = ym[4 * row + k, z : z + 8, :]
                mz_y = ym[4 * row + 2 + k, z : z + 8, :]
                mx, my, mz = magnetic(X), magnetic(Y), magnetic(Z)
                d = ds_[k][base + e, z : z + 8, :]
                g = gs[k][base + e, z : z + 8, :]
                ex = d * electric(X) + g * ((mz - mz_y) - (my - magnetic(Y, e, -1)))
                ey = d * electric(Y) + g * ((mx - magnetic(X, e, -1)) - (mz - magnetic(Z, e - 1)))
                ez = d * electric(Z) + g * ((my - magnetic(Y, e - 1)) - (mx - mx_y))
                for c, v in ((X, ex), (Y, ey), (Z, ez)):
                    es[new][k][b3 + (3 * e + c), 8 + z : 16 + z, :] = v
        settle(0)
        return start

    def two_steps(s, _):
        for old in range(2):
            left = STEPS - 1 - old - 2 * s
            start = BASE + W - left - 2
            lax.fori_loop(0, 2, functools.partial(block, old, False, True), start)
            lax.fori_loop(2, W - 1 + left, functools.partial(block, old, True, True), start)
            block(old, True, False, W - 1 + left, start)
            turn_two(1 - old, start + 2 * (W - 2 + left))
        return 0

    lax.fori_loop(0, STEPS // 2, two_steps, 0)

    def emit(r, _):
        for c, source in enumerate((X, Y, Z)):
            for t in range(on):
                stage[c, pl.ds(64 * t + r, 8, stride=8), :] = ea0[
                    3 * (r + BASE + W) + source, 16 + 8 * t : 24 + 8 * t, :
                ]
        return 0

    lax.fori_loop(0, 8, emit, 0)
    if upper:
        plane[0] = stage[0, 64 * on - 8 : 64 * on, :]
        plane[1] = stage[1, 64 * on - 8 : 64 * on, :]
    copy_all([(stage, out.at[:, pl.ds(64 * (CUT + 1) if upper else 0, 64 * on)])], sems)


def run_steps(upper, decay, gain, sides, arrays):
    smem = pl.BlockSpec(memory_space=pltpu.SMEM)
    out_shape = [jax.ShapeDtypeStruct((3, 640, 128), F32)]
    out_specs = [HBM]
    aliases = {}
    if upper:
        out_shape.append(jax.ShapeDtypeStruct((2, 8, 128), F32))
        out_specs.append(LOCAL)
    else:
        aliases = {6 + len(arrays) - 1: 0}
    tiles, on = (11 - CUT, 9 - CUT) if upper else (CUT + 3, CUT + 1)
    z = 16 + 8 * tiles
    field = pltpu.VMEM((3 * HELD, z, 128), F32)
    table = pltpu.VMEM((HELD, 8 * tiles, 128), F32)
    turned = pltpu.VMEM((4 * HELD, 8 * tiles, 128), F32)
    return pl.pallas_call(
        functools.partial(steps_kernel, upper),
        out_shape=out_shape,
        in_specs=[smem, smem, LOCAL, LOCAL] + [HBM] * (2 + len(arrays)),
        out_specs=out_specs,
        scratch_shapes=[field] * 8
        + [table] * 4
        + [turned] * 2
        + [
            pltpu.VMEM((8, 8 * tiles, 128), F32),
            pltpu.VMEM((ROWS, 8 * tiles, 128), F32),
            pltpu.VMEM((3, 64 * on, 128), F32),
            pltpu.SemaphoreType.DMA((39,)),
        ],
        input_output_aliases=aliases,
        compiler_params=params(),
        cost_estimate=cost(100),
        name="steps_upper" if upper else "steps_lower",
    )(decay, gain, *sides, *arrays)


def image_kernel(weights, own, received, out, sh, rhs):
    gz = lax.axis_index("gz")
    centre, before, after = [
        [jnp.where(gz == 1, own[i, c], received[i, c]) for c in range(2)] for i in range(3)
    ]
    lane = lax.broadcasted_iota(jnp.int32, (24, 128), 1)
    for q in range(15):
        shift = q - 7
        for c in range(2):
            v = centre[c]
            if shift > 0:
                v = jnp.where(
                    lane >= 128 - shift,
                    pltpu.roll(after[c], 128 - shift, 1),
                    pltpu.roll(v, 128 - shift, 1),
                )
            elif shift < 0:
                v = jnp.where(
                    lane < -shift, pltpu.roll(before[c], -shift, 1), pltpu.roll(v, -shift, 1)
                )
            sh[q, c] = v

    def fill(side):
        for q in range(15):
            for c in range(2):
                for i in range(4):
                    start = 4 * side + 1 + i
                    rhs[16 * q : 16 * q + 16, (4 * c + i) * 128 : (4 * c + i + 1) * 128] = sh[
                        q, c, start : start + 16, :
                    ]

    @pl.when(gz == 0)
    def _():
        fill(0)

    @pl.when(gz == 1)
    def _():
        fill(1)

    amplitude = jnp.dot(
        weights[...],
        rhs[...],
        precision=lax.Precision.HIGHEST,
        preferred_element_type=jnp.float32,
    )
    power = jnp.sum(amplitude * amplitude, axis=0, keepdims=True)
    for i in range(4):
        out[i : i + 1, :] = (
            power[:, i * 128 : (i + 1) * 128] + power[:, (4 + i) * 128 : (5 + i) * 128]
        )


def image_of(weights, own, received):
    return pl.pallas_call(
        image_kernel,
        out_shape=jax.ShapeDtypeStruct((4, 128), jnp.float32),
        in_specs=[LOCAL] * 3,
        out_specs=LOCAL,
        scratch_shapes=[
            pltpu.VMEM((15, 2, 24, 128), jnp.float32),
            pltpu.VMEM((240, 1024), jnp.float32),
        ],
        compiler_params=pltpu.CompilerParams(vmem_limit_bytes=VMEM),
        name="image",
    )(weights, own, received)


def on_device(electric, magnetic, material, decay, gain, kernels):
    el = electric.reshape(3, 640, 128)
    mg = magnetic.reshape(3, 640, 128)
    mat = material.reshape(640, 128)
    weights = jnp.pad(
        kernels.transpose(0, 1, 3, 2).reshape(48, 15, 15), ((0, 0), (0, 0), (0, 1))
    ).reshape(48, 240)

    strips, edge, edge_strips = own_strips(el, mg, mat)
    edge = around(edge, "gz", 1)
    from_low, from_high = around(strips, "gy", 1), around(strips, "gy", -1)
    edge_low, edge_high = beyond(edge_strips, 1), beyond(edge_strips, -1)
    own_u, up_u, down_u, own_l, up_l, down_l = pack(el, mg, mat)
    up_u, down_u, edge_low, edge_high = lax.optimization_barrier(
        (up_u, down_u, edge_low, edge_high)
    )
    low_u, high_u = around(up_u, "gx", 1), around(down_u, "gx", -1)
    strips, up_c, down_c, up_l, down_l = corners(
        from_low, from_high, edge_low, edge_high, edge, up_l, down_l
    )
    low_c, high_c = around(up_c, "gx", 1), around(down_c, "gx", -1)
    low_l, high_l = around(up_l, "gx", 1), around(down_l, "gx", -1)

    low_u, high_u, weights = lax.optimization_barrier((low_u, high_u, weights))
    sides = [low_c, high_c, strips, edge]
    field, plane = run_steps(True, decay, gain, sides, [own_u, low_u, high_u])
    top = jnp.stack([plane, around(plane, "gy", 1), around(plane, "gy", -1)])
    top = jnp.concatenate([around(top, "gx", 1), top, around(top, "gx", -1)], 2)
    top, low_l, high_l = lax.optimization_barrier((top, low_l, high_l))
    received = lax.ppermute(top, "gz", [(1, 0)])
    (field,) = run_steps(
        False, decay, gain, sides, [own_u, low_u, high_u, own_l, low_l, high_l, field]
    )
    image = image_of(weights, top, received)
    return (field.reshape(3, 80, 8, 128), image)


def solution(mesh):
    in_specs = (
        P(None, "gz", "gx", "gy"),
        P(None, "gz", "gx", "gy"),
        P("gz", "gx", "gy"),
        P(),
        P(),
        P(),
    )
    out_specs = (P(None, "gz", "gx", "gy"), P(("gx", "gz"), "gy"))
    return jax.shard_map(
        on_device, mesh=mesh, in_specs=in_specs, out_specs=out_specs, check_vma=False
    )
```

```python
import functools

import jax
import jax.numpy as jnp
from jax import lax
from jax.experimental import pallas as pl
from jax.experimental.pallas import tpu as pltpu
from jax.sharding import PartitionSpec as P

STEPS = 6
W = STEPS
Y, Z, X = range(3)
NC = 7
SOURCE = ((0, 1), (0, 2), (0, 0), (1, 1), (1, 2), (1, 0))
ROWS = 8 + 2 * W
BASE = 4
HELD = BASE + ROWS + 2
CUT = 6
HIGH = 11 - CUT
LAG = 4
VMEM = 63 * 1024 * 1024
F32 = jnp.float32
HBM = pl.BlockSpec(memory_space=pl.ANY)
LOCAL = pl.BlockSpec(memory_space=pltpu.VMEM)


def around(value, axis, steps):
    count = lax.axis_size(axis)
    return lax.ppermute(value, axis, [(i, (i + steps) % count) for i in range(count)])


def beyond(value, steps):
    ny, nz = lax.axis_size("gy"), lax.axis_size("gz")
    pairs = [
        (y * nz + z, (y + steps) % ny * nz + (z + 1) % nz) for y in range(ny) for z in range(nz)
    ]
    return lax.ppermute(value, ("gy", "gz"), pairs)


def copy_all(pairs, sems):
    copies = [pltpu.make_async_copy(a, b, sems.at[i]) for i, (a, b) in enumerate(pairs)]
    for copy in copies:
        copy.start()
    for copy in copies:
        copy.wait()


def params():
    return pltpu.CompilerParams(vmem_limit_bytes=VMEM)


def cost(us):
    return pl.CostEstimate(flops=int(us * 1e9), bytes_accessed=int(us * 3e6), transcendentals=0)


def plane_of(r, c):
    return 48 + r if c == 6 else 24 * (c // 3) + 3 * r + c % 3


def strip_masks():
    lane = lax.broadcasted_iota(jnp.int32, (8, 128), 1)
    return [((lane - 16 * c + W + 128) % 128) < 2 * W for c in range(NC)]


def strip_kernel(el, mg, mat, strips, edge, edge_strips, ext, matv, sems):
    gz = lax.axis_index("gz")
    loads = [(mat, matv)]
    for c, (which, comp) in enumerate(SOURCE):
        loads.append(((el, mg)[which].at[comp], ext.at[c]))
    copy_all(loads, sems)
    masks = strip_masks()

    def layers(c, t, r):
        rows = pl.ds(64 * t + r, 8, stride=8)
        if c == 6:
            return matv[rows, :].astype(F32)
        v = ext[c, rows, :]
        return v * 2.0 if c >= 3 else v

    def row(r, _):
        for t in range(10):
            total = layers(0, t, r)
            for c in range(1, NC):
                total = jnp.where(masks[c], pltpu.roll(layers(c, t, r), 16 * c, 1), total)
            strips[r, 8 * t : 8 * t + 8, :] = total
        return 0

    lax.fori_loop(0, 8, row, 0)

    def edges(t):
        for r in range(8):
            for c in range(NC):
                edge[plane_of(r, c)] = layers(c, t, r)
        edge_strips[...] = strips[:, 8 * t : 8 * t + 8, :]

    @pl.when(gz == 0)
    def _():
        edges(9)

    @pl.when(gz == 1)
    def _():
        edges(0)


def own_strips(el, mg, mat):
    return pl.pallas_call(
        strip_kernel,
        out_shape=[
            jax.ShapeDtypeStruct((8, 80, 128), F32),
            jax.ShapeDtypeStruct((8 * NC, 8, 128), F32),
            jax.ShapeDtypeStruct((8, 8, 128), F32),
        ],
        in_specs=[HBM] * 3,
        out_specs=[LOCAL] * 3,
        scratch_shapes=[
            pltpu.VMEM((6, 640, 128), F32),
            pltpu.VMEM((640, 128), jnp.int32),
            pltpu.SemaphoreType.DMA((7,)),
        ],
        compiler_params=params(),
        cost_estimate=cost(3),
        name="own_strips",
    )(el, mg, mat)


def pack_kernel(first, last, el, mg, mat, *refs):
    if first:
        own, up, down, ext, matv, planes, sems = refs
    else:
        strips, own, up, down, ext, matv, planes, sems = refs
    tiles = last - first
    here = pl.ds(64 * first, 64 * tiles)
    loads = [(mat.at[here], matv)]
    for c, (which, comp) in enumerate(SOURCE):
        loads.append(((el, mg)[which].at[comp, here], ext.at[c]))
    copy_all(loads, sems)

    def row(r, _):
        for t in range(tiles):
            rows = pl.ds(64 * t + r, 8, stride=8)
            for c in range(NC):
                if c == 6:
                    v = matv[rows, :].astype(F32)
                else:
                    v = ext[c, rows, :]
                    if c >= 3:
                        v = v * 2.0
                planes[plane_of(r, c), 8 * t : 8 * t + 8, :] = v
        return 0

    lax.fori_loop(0, 8, row, 0)
    z = pl.ds(0, 8 * tiles)
    pairs = [(planes, own)]
    for a, b, n in ((6, 0, 18), (30, 18, 2), (33, 20, 15), (51, 35, 5)):
        pairs.append((planes.at[pl.ds(a, n)], up.at[pl.ds(b, n), z]))
    for a, b, n in ((0, 0, 17), (24, 17, 15), (48, 32, 5)):
        pairs.append((planes.at[pl.ds(a, n)], down.at[pl.ds(b, n), z]))
    if not first:
        pairs.append((strips.at[pl.ds(8 - W, W), z], up.at[pl.ds(40, W)]))
        pairs.append((strips.at[pl.ds(0, W), z], down.at[pl.ds(37, W)]))
    copy_all(pairs, sems)


def pack(first, last, el, mg, mat, *strips):
    layers = 8 * (last - first)
    more = 0 if first else W
    return pl.pallas_call(
        functools.partial(pack_kernel, first, last),
        out_shape=[
            jax.ShapeDtypeStruct((8 * NC, layers, 128), F32),
            jax.ShapeDtypeStruct((40 + more, layers, 128), F32),
            jax.ShapeDtypeStruct((37 + more, layers, 128), F32),
        ],
        in_specs=[HBM] * 3 + [LOCAL] * len(strips),
        out_specs=[HBM] * 3,
        scratch_shapes=[
            pltpu.VMEM((6, 8 * layers, 128), F32),
            pltpu.VMEM((8 * layers, 128), jnp.int32),
            pltpu.VMEM((8 * NC, layers, 128), F32),
            pltpu.SemaphoreType.DMA((10,)),
        ],
        compiler_params=params(),
        cost_estimate=cost(20 if first else 3),
        name="pack_upper" if first else "pack_lower",
    )(el, mg, mat, *strips)


def corner_kernel(from_low, from_high, edge_low, edge_high, edge, strips, up, down):
    lane = lax.broadcasted_iota(jnp.int32, (8, 80, 128), 2)
    strips[:, 0:80, :] = jnp.where(lane % 16 < 8, from_high[...], from_low[...])
    lane = lax.broadcasted_iota(jnp.int32, (8, 8, 128), 2)
    strips[:, 80:88, :] = jnp.where(lane % 16 < 8, edge_high[...], edge_low[...])
    for a, b, n in ((6, 0, 18), (30, 18, 2), (33, 20, 15), (51, 35, 5)):
        up[b : b + n] = edge[a : a + n]
    for a, b, n in ((0, 0, 17), (24, 17, 15), (48, 32, 5)):
        down[b : b + n] = edge[a : a + n]
    for r in range(W):
        for t in range(HIGH):
            z = 8 * (CUT + t)
            up[40 + HIGH * r + t] = strips[8 - W + r, z : z + 8, :]
            down[37 + HIGH * r + t] = strips[r, z : z + 8, :]


def corners(from_low, from_high, edge_low, edge_high, edge):
    return pl.pallas_call(
        corner_kernel,
        out_shape=[
            jax.ShapeDtypeStruct((8, 88, 128), F32),
            jax.ShapeDtypeStruct((40 + W * HIGH, 8, 128), F32),
            jax.ShapeDtypeStruct((37 + W * HIGH, 8, 128), F32),
        ],
        in_specs=[LOCAL] * 5,
        out_specs=[LOCAL] * 3,
        compiler_params=params(),
        cost_estimate=cost(1),
        name="corners",
    )(from_low, from_high, edge_low, edge_high, edge)


def steps_kernel(upper, decay, gain, low_c, high_c, strips, edge, *refs):
    gz = lax.axis_index("gz")
    nu, nl = 8 * (10 - CUT), 8 * CUT
    own_u, low_u, high_u = refs[:3]
    if upper:
        out, plane, *scratch = refs[3:]
        tiles, halo, counts = 11 - CUT, 10 - CUT, gz == 0
        sets = [((own_u, low_u, high_u), 0, nu, 0, nl)]
    else:
        own_l, low_l, high_l, _, out, *scratch = refs[3:]
        tiles, halo, counts = CUT + 3, 0, gz == 1
        sets = [
            ((own_l, low_l, high_l), 0, nl, 8, 0),
            ((own_u, low_u, high_u), 0, 16, 8 + nl, nl),
        ]
    on = 9 - CUT if upper else CUT + 1
    ea0, ea1, eb0, eb1, ma0, ma1, mb0, mb1, d0, d1, g0, g1, ya, yb, ym, sv, stage, sems = scratch
    es, ms, yes = ((ea0, ea1), (eb0, eb1)), ((ma0, ma1), (mb0, mb1)), (ya, yb)
    ds_, gs = (d0, d1), (g0, g1)

    first, mid, last_ = BASE, BASE + W, BASE + W + 8
    hz = 8 * halo
    moves = [(strips.at[:, pl.ds(80, 8)], sv.at[pl.ds(W, 8), pl.ds(hz, 8)])]
    for (own, low, high), start, layers, to, strip in sets:
        zd = pl.ds(to, layers)
        moves.append((strips.at[:, pl.ds(strip, layers)], sv.at[pl.ds(W, 8), zd]))
        if not upper and own is own_l:
            moves.append((low.at[pl.ds(40, W)], sv.at[pl.ds(0, W), zd]))
            moves.append((high.at[pl.ds(37, W)], sv.at[pl.ds(W + 8, W), zd]))
    early = len(moves)
    own_parts = ((0, 24, ea0, 3 * mid), (24, 24, ma0, 3 * mid), (48, 8, d0, mid))
    low_parts = (
        (0, 18, ea0, 3 * first),
        (18, 2, ma0, 3 * first),
        (20, 15, ma0, 3 * first + 3),
        (35, 5, d0, first + 1),
    )
    high_parts = ((0, 17, ea0, 3 * last_), (17, 15, ma0, 3 * last_), (32, 5, d0, last_))
    for (own, low, high), start, layers, to, strip in sets:
        for ref, parts in ((own, own_parts), (low, low_parts), (high, high_parts)):
            for a, n, dst, b in parts:
                z = pl.ds(to if dst is d0 else 8 + to, layers)
                moves.append((ref.at[pl.ds(a, n), pl.ds(start, layers)], dst.at[pl.ds(b, n), z]))
    for a, n, dst, b in own_parts:
        z = pl.ds(hz if dst is d0 else 8 + hz, 8)
        moves.append((edge.at[pl.ds(a, n)], dst.at[pl.ds(b, n), z]))
    copies = [pltpu.make_async_copy(a, b, sems.at[i]) for i, (a, b) in enumerate(moves)]
    for copy in copies:
        copy.start()
    for ref, parts in ((low_c, low_parts), (high_c, high_parts)):
        for a, n, dst, b in parts:
            z = hz if dst is d0 else 8 + hz
            for i in range(n):
                dst[b + i, z : z + 8, :] = ref[a + i]
    here = [(t, t) for t in range(HIGH)]
    if not upper:
        here = [(0, HIGH - 1), (CUT + 1, 0), (CUT + 2, 1)]
    for r in range(W):
        for t, u in here:
            sv[r, 8 * t : 8 * t + 8, :] = low_c[40 + HIGH * r + u]
            sv[W + 8 + r, 8 * t : 8 * t + 8, :] = high_c[37 + HIGH * r + u]

    zero = jnp.zeros((8, 128), F32)
    top = 8 + 8 * tiles

    def ends(r, _):
        for pair in ms:
            for m in pair:
                m[3 * r + X, 0:8, :] = zero
                m[3 * r + Y, 0:8, :] = zero
        for pair in es:
            for e in pair:
                e[3 * r + X, top : top + 8, :] = zero
                e[3 * r + Y, top : top + 8, :] = zero
        return 0

    lax.fori_loop(0, HELD, ends, 0)
    for copy in copies[:early]:
        copy.wait()

    def unpack(i, _):
        for row in range(2):
            r = 2 * i + row
            at = BASE + r
            for t in range(tiles):
                z = 8 * t
                v = sv[r, z : z + 8, :]
                for c in range(NC):
                    turned = pltpu.roll(v, 128 - 16 * c, 1) if c else v
                    if c < 3:
                        ea1[3 * at + c, 8 + z : 16 + z, :] = turned
                    elif c < 6:
                        ma1[3 * at + c - 3, 8 + z : 16 + z, :] = turned
                    else:
                        d1[at, z : z + 8, :] = turned
        return 0

    lax.fori_loop(0, ROWS // 2, unpack, 0)
    for copy in copies[early:]:
        copy.wait()

    @pl.when(jnp.logical_not(counts))
    def _():
        def clear(i, _):
            for ref in (ea0, ea1, ma0, ma1):
                ref[3 * BASE + i, hz + 8 : hz + 16, :] = zero
            return 0

        lax.fori_loop(0, 3 * ROWS, clear, 0)

    live = jnp.where(counts, 1.0, 0.0).astype(F32)

    lane = lax.broadcasted_iota(jnp.int32, (8, 128), 1)
    last, first_lane = lane == 127, lane == 0
    units = [(row, t) for row in range(2) for t in range(tiles)]

    def tables(r):
        for t in range(tiles):
            z = 8 * t
            for d, g in zip(ds_, gs):
                ids = d[r, z : z + 8, :]
                d_cells, g_cells = zero, zero
                for i in range(5):
                    hit = ids == float(i)
                    d_cells = jnp.where(hit, decay[i], d_cells)
                    g_cells = jnp.where(hit, gain[i] * 0.5, g_cells)
                if t == halo:
                    d_cells, g_cells = d_cells * live, g_cells * live
                d[r, z : z + 8, :] = d_cells
                g[r, z : z + 8, :] = g_cells

    def turn_two(which, r0, beside=None):
        kept = []
        for row, t in units:
            for j, c in enumerate((X, Z)):
                pair = [
                    pltpu.roll(e[3 * r0 + (3 * row + c), 8 + 8 * t : 16 + 8 * t, :], 127, 1)
                    for e in es[which]
                ]
                kept.append((4 * row + 2 * j, 8 * t, pair))
        if beside:
            beside()
        y = yes[which]
        for i, z, (a, b) in kept:
            y[4 * r0 + i, z : z + 8, :] = jnp.where(last, b, a)
            y[4 * r0 + (i + 1), z : z + 8, :] = jnp.where(last, a, b)

    def first_turn(i, _):
        r0 = BASE + 2 * i

        def both():
            tables(r0)
            tables(r0 + 1)

        turn_two(0, r0, both)
        return 0

    lax.fori_loop(0, ROWS // 2, first_turn, 0)

    def block(old, with_e, with_m, m, start):
        new = 1 - old
        base = start + 2 * m
        b3, b4 = 3 * base, 4 * base
        waiting = []
        half = len(units) // 2
        jobs_m = [(ms, row, t) for row, t in units] if with_e else []
        jobs_e = [(es, row, t) for row, t in units] if with_e else []

        def turn(refs, row, t):
            z = 8 * t
            if refs is ms:
                pairs = [
                    [pltpu.roll(f[b3 + (3 * (row - 2) + c), 8 + z : 16 + z, :], 1, 1) for f in ms[new]]
                    for c in (X, Z)
                ]
                waiting.append((ym, 0, 4 * row, z, pairs, first_lane))
            else:
                pairs = [
                    [pltpu.roll(f[b3 + (3 * (row - 4) + c), 8 + z : 16 + z, :], 127, 1) for f in es[new]]
                    for c in (X, Z)
                ]
                waiting.append((yes[new], b4, 4 * (row - 4), z, pairs, last))

        def keep():
            y, b, i, z, pairs, edge_lane = waiting.pop(0)
            for j, (v0, v1) in enumerate(pairs):
                y[b + (i + 2 * j), z : z + 8, :] = jnp.where(edge_lane, v1, v0)
                y[b + (i + 2 * j + 1), z : z + 8, :] = jnp.where(edge_lane, v0, v1)

        def settle(most):
            while len(waiting) > most:
                keep()

        for u, (row, t) in enumerate(units if with_m else ()):
            if jobs_m:
                turn(*jobs_m.pop(0))
                if u >= half:
                    turn(*jobs_e.pop(0))
            settle(LAG)
            z = 8 * t
            for k in range(2):

                def electric(c, r=row, shift=0):
                    return es[old][k][b3 + (3 * r + c), 8 + z + shift : 16 + z + shift, :]

                def magnetic(c):
                    return ms[old][k][b3 + (3 * row + c), 8 + z : 16 + z, :]

                ex_y = yes[old][b4 + (4 * row + k), z : z + 8, :]
                ez_y = yes[old][b4 + (4 * row + 2 + k), z : z + 8, :]
                ex, ey, ez = electric(X), electric(Y), electric(Z)
                cx = (ez_y - ez) - (electric(Y, row, 1) - ey)
                cy = (electric(X, row, 1) - ex) - (electric(Z, row + 1) - ez)
                cz = (electric(Y, row + 1) - ey) - (ex_y - ex)
                if t == halo and not upper:
                    cx, cy, cz = cx * live, cy * live, cz * live
                mx, my, mz = magnetic(X) - cx, magnetic(Y) - cy, magnetic(Z) - cz
                for c, v in ((X, mx), (Y, my), (Z, mz)):
                    ms[new][k][b3 + (3 * row + c), 8 + z : 16 + z, :] = v
        for job in jobs_m:
            turn(*job)
            settle(LAG)
        for row, t in units if with_e else ():
            if jobs_e:
                turn(*jobs_e.pop(0))
            settle(LAG if jobs_e else max(len(waiting) - 2, 0))
            e, z = row - 2, 8 * t
            for k in range(2):

                def magnetic(c, r=e, shift=0):
                    return ms[new][k][b3 + (3 * r + c), 8 + z + shift : 16 + z + shift, :]

                def electric(c):
                    return es[old][k][b3 + (3 * e + c), 8 + z : 16 + z, :]

                mx_y = ym[4 * row + k, z : z + 8, :]
                mz_y = ym[4 * row + 2 + k, z : z + 8, :]
                mx, my, mz = magnetic(X), magnetic(Y), magnetic(Z)
                d = ds_[k][base + e, z : z + 8, :]
                g = gs[k][base + e, z : z + 8, :]
                ex = d * electric(X) + g * ((mz - mz_y) - (my - magnetic(Y, e, -1)))
                ey = d * electric(Y) + g * ((mx - magnetic(X, e, -1)) - (mz - magnetic(Z, e - 1)))
                ez = d * electric(Z) + g * ((my - magnetic(Y, e - 1)) - (mx - mx_y))
                for c, v in ((X, ex), (Y, ey), (Z, ez)):
                    es[new][k][b3 + (3 * e + c), 8 + z : 16 + z, :] = v
        settle(0)
        return start

    def two_steps(s, _):
        for old in range(2):
            left = STEPS - 1 - old - 2 * s
            start = BASE + W - left - 2
            lax.fori_loop(0, 2, functools.partial(block, old, False, True), start)
            lax.fori_loop(2, W - 1 + left, functools.partial(block, old, True, True), start)
            block(old, True, False, W - 1 + left, start)
            turn_two(1 - old, start + 2 * (W - 2 + left))
        return 0

    lax.fori_loop(0, STEPS // 2, two_steps, 0)

    def emit(r, _):
        for c, source in enumerate((X, Y, Z)):
            for t in range(on):
                stage[c, pl.ds(64 * t + r, 8, stride=8), :] = ea0[
                    3 * (r + BASE + W) + source, 16 + 8 * t : 24 + 8 * t, :
                ]
        return 0

    lax.fori_loop(0, 8, emit, 0)
    if upper:
        plane[0] = stage[0, 64 * on - 8 : 64 * on, :]
        plane[1] = stage[1, 64 * on - 8 : 64 * on, :]
    copy_all([(stage, out.at[:, pl.ds(64 * (CUT + 1) if upper else 0, 64 * on)])], sems)


def run_steps(upper, decay, gain, sides, arrays):
    smem = pl.BlockSpec(memory_space=pltpu.SMEM)
    out_shape = [jax.ShapeDtypeStruct((3, 640, 128), F32)]
    out_specs = [HBM]
    aliases = {}
    if upper:
        out_shape.append(jax.ShapeDtypeStruct((2, 8, 128), F32))
        out_specs.append(LOCAL)
    else:
        aliases = {6 + len(arrays) - 1: 0}
    tiles, on = (11 - CUT, 9 - CUT) if upper else (CUT + 3, CUT + 1)
    z = 16 + 8 * tiles
    field = pltpu.VMEM((3 * HELD, z, 128), F32)
    table = pltpu.VMEM((HELD, 8 * tiles, 128), F32)
    turned = pltpu.VMEM((4 * HELD, 8 * tiles, 128), F32)
    return pl.pallas_call(
        functools.partial(steps_kernel, upper),
        out_shape=out_shape,
        in_specs=[smem, smem, LOCAL, LOCAL] + [HBM] * (2 + len(arrays)),
        out_specs=out_specs,
        scratch_shapes=[field] * 8
        + [table] * 4
        + [turned] * 2
        + [
            pltpu.VMEM((8, 8 * tiles, 128), F32),
            pltpu.VMEM((ROWS, 8 * tiles, 128), F32),
            pltpu.VMEM((3, 64 * on, 128), F32),
            pltpu.SemaphoreType.DMA((39,)),
        ],
        input_output_aliases=aliases,
        compiler_params=params(),
        cost_estimate=cost(100),
        name="steps_upper" if upper else "steps_lower",
    )(decay, gain, *sides, *arrays)


def image_kernel(weights, own, received, out, sh, rhs):
    gz = lax.axis_index("gz")
    centre, before, after = [
        [jnp.where(gz == 1, own[i, c], received[i, c]) for c in range(2)] for i in range(3)
    ]
    lane = lax.broadcasted_iota(jnp.int32, (24, 128), 1)
    for q in range(15):
        shift = q - 7
        for c in range(2):
            v = centre[c]
            if shift > 0:
                v = jnp.where(
                    lane >= 128 - shift,
                    pltpu.roll(after[c], 128 - shift, 1),
                    pltpu.roll(v, 128 - shift, 1),
                )
            elif shift < 0:
                v = jnp.where(
                    lane < -shift, pltpu.roll(before[c], -shift, 1), pltpu.roll(v, -shift, 1)
                )
            sh[q, c] = v

    def fill(side):
        for q in range(15):
            for c in range(2):
                for i in range(4):
                    start = 4 * side + 1 + i
                    rhs[16 * q : 16 * q + 16, (4 * c + i) * 128 : (4 * c + i + 1) * 128] = sh[
                        q, c, start : start + 16, :
                    ]

    @pl.when(gz == 0)
    def _():
        fill(0)

    @pl.when(gz == 1)
    def _():
        fill(1)

    amplitude = jnp.dot(
        weights[...],
        rhs[...],
        precision=lax.Precision.HIGHEST,
        preferred_element_type=jnp.float32,
    )
    power = jnp.sum(amplitude * amplitude, axis=0, keepdims=True)
    for i in range(4):
        out[i : i + 1, :] = (
            power[:, i * 128 : (i + 1) * 128] + power[:, (4 + i) * 128 : (5 + i) * 128]
        )


def image_of(weights, own, received):
    return pl.pallas_call(
        image_kernel,
        out_shape=jax.ShapeDtypeStruct((4, 128), jnp.float32),
        in_specs=[LOCAL] * 3,
        out_specs=LOCAL,
        scratch_shapes=[
            pltpu.VMEM((15, 2, 24, 128), jnp.float32),
            pltpu.VMEM((240, 1024), jnp.float32),
        ],
        compiler_params=pltpu.CompilerParams(vmem_limit_bytes=VMEM),
        name="image",
    )(weights, own, received)


def on_device(electric, magnetic, material, decay, gain, kernels):
    el = electric.reshape(3, 640, 128)
    mg = magnetic.reshape(3, 640, 128)
    mat = material.reshape(640, 128)
    weights = jnp.pad(
        kernels.transpose(0, 1, 3, 2).reshape(48, 15, 15), ((0, 0), (0, 0), (0, 1))
    ).reshape(48, 240)

    strips, edge, edge_strips = own_strips(el, mg, mat)
    edge = around(edge, "gz", 1)
    from_low, from_high = around(strips, "gy", 1), around(strips, "gy", -1)
    edge_low, edge_high = beyond(edge_strips, 1), beyond(edge_strips, -1)
    own_u, up_u, down_u = pack(CUT, 10, el, mg, mat)
    up_u, down_u, edge, edge_low, edge_high = lax.optimization_barrier(
        (up_u, down_u, edge, edge_low, edge_high)
    )
    low_u, high_u = around(up_u, "gx", 1), around(down_u, "gx", -1)
    strips, up_c, down_c = corners(from_low, from_high, edge_low, edge_high, edge)
    low_c, high_c = around(up_c, "gx", 1), around(down_c, "gx", -1)
    own_l, up_l, down_l = pack(0, CUT, el, mg, mat, strips)
    low_l, high_l = around(up_l, "gx", 1), around(down_l, "gx", -1)

    low_u, high_u, weights = lax.optimization_barrier((low_u, high_u, weights))
    sides = [low_c, high_c, strips, edge]
    field, plane = run_steps(True, decay, gain, sides, [own_u, low_u, high_u])
    top = jnp.stack([plane, around(plane, "gy", 1), around(plane, "gy", -1)])
    top = jnp.concatenate([around(top, "gx", 1), top, around(top, "gx", -1)], 2)
    top, low_l, high_l = lax.optimization_barrier((top, low_l, high_l))
    received = lax.ppermute(top, "gz", [(1, 0)])
    (field,) = run_steps(
        False, decay, gain, sides, [own_u, low_u, high_u, own_l, low_l, high_l, field]
    )
    image = image_of(weights, top, received)
    return (field.reshape(3, 80, 8, 128), image)


def solution(mesh):
    in_specs = (
        P(None, "gz", "gx", "gy"),
        P(None, "gz", "gx", "gy"),
        P("gz", "gx", "gy"),
        P(),
        P(),
        P(),
    )
    out_specs = (P(None, "gz", "gx", "gy"), P(("gx", "gz"), "gy"))
    return jax.shard_map(
        on_device, mesh=mesh, in_specs=in_specs, out_specs=out_specs, check_vma=False
    )
```

```python
import functools

import jax
import jax.numpy as jnp
from jax import lax
from jax.experimental import pallas as pl
from jax.experimental.pallas import tpu as pltpu
from jax.sharding import PartitionSpec as P

STEPS = 6
W = STEPS
Y, Z, X = range(3)
NC = 7
SOURCE = ((0, 1), (0, 2), (0, 0), (1, 1), (1, 2), (1, 0))
ROWS = 8 + 2 * W
BASE = 4
HELD = BASE + ROWS + 2
CUT = 7
HIGH = 11 - CUT
LAG = 4
VMEM = 63 * 1024 * 1024
F32 = jnp.float32
HBM = pl.BlockSpec(memory_space=pl.ANY)
LOCAL = pl.BlockSpec(memory_space=pltpu.VMEM)


def around(value, axis, steps):
    count = lax.axis_size(axis)
    return lax.ppermute(value, axis, [(i, (i + steps) % count) for i in range(count)])


def beyond(value, steps):
    ny, nz = lax.axis_size("gy"), lax.axis_size("gz")
    pairs = [
        (y * nz + z, (y + steps) % ny * nz + (z + 1) % nz) for y in range(ny) for z in range(nz)
    ]
    return lax.ppermute(value, ("gy", "gz"), pairs)


def copy_all(pairs, sems):
    copies = [pltpu.make_async_copy(a, b, sems.at[i]) for i, (a, b) in enumerate(pairs)]
    for copy in copies:
        copy.start()
    for copy in copies:
        copy.wait()


def params():
    return pltpu.CompilerParams(vmem_limit_bytes=VMEM)


def cost(us):
    return pl.CostEstimate(flops=int(us * 1e9), bytes_accessed=int(us * 3e6), transcendentals=0)


def plane_of(r, c):
    return 48 + r if c == 6 else 24 * (c // 3) + 3 * r + c % 3


def strip_masks():
    lane = lax.broadcasted_iota(jnp.int32, (8, 128), 1)
    return [((lane - 16 * c + W + 128) % 128) < 2 * W for c in range(NC)]


def strip_kernel(el, mg, mat, strips, edge, edge_strips, ext, matv, sems):
    gz = lax.axis_index("gz")
    loads = [(mat, matv)]
    for c, (which, comp) in enumerate(SOURCE):
        loads.append(((el, mg)[which].at[comp], ext.at[c]))
    copy_all(loads, sems)
    masks = strip_masks()

    def layers(c, t, r):
        rows = pl.ds(64 * t + r, 8, stride=8)
        if c == 6:
            return matv[rows, :].astype(F32)
        v = ext[c, rows, :]
        return v * 2.0 if c >= 3 else v

    def row(r, _):
        for t in range(10):
            total = layers(0, t, r)
            for c in range(1, NC):
                total = jnp.where(masks[c], pltpu.roll(layers(c, t, r), 16 * c, 1), total)
            strips[r, 8 * t : 8 * t + 8, :] = total
        return 0

    lax.fori_loop(0, 8, row, 0)

    def edges(t):
        for r in range(8):
            for c in range(NC):
                edge[plane_of(r, c)] = layers(c, t, r)
        edge_strips[...] = strips[:, 8 * t : 8 * t + 8, :]

    @pl.when(gz == 0)
    def _():
        edges(9)

    @pl.when(gz == 1)
    def _():
        edges(0)


def own_strips(el, mg, mat):
    return pl.pallas_call(
        strip_kernel,
        out_shape=[
            jax.ShapeDtypeStruct((8, 80, 128), F32),
            jax.ShapeDtypeStruct((8 * NC, 8, 128), F32),
            jax.ShapeDtypeStruct((8, 8, 128), F32),
        ],
        in_specs=[HBM] * 3,
        out_specs=[LOCAL] * 3,
        scratch_shapes=[
            pltpu.VMEM((6, 640, 128), F32),
            pltpu.VMEM((640, 128), jnp.int32),
            pltpu.SemaphoreType.DMA((7,)),
        ],
        compiler_params=params(),
        cost_estimate=cost(3),
        name="own_strips",
    )(el, mg, mat)


def pack_kernel(el, mg, mat, own_u, up_u, down_u, own_l, up_l, down_l, ext, matv, planes, sems):
    loads = [(mat, matv)]
    for c, (which, comp) in enumerate(SOURCE):
        loads.append(((el, mg)[which].at[comp], ext.at[c]))
    copy_all(loads, sems)

    def rows_of(first, last):
        def row(r, _):
            for t in range(first, last):
                rows = pl.ds(64 * t + r, 8, stride=8)
                for c in range(NC):
                    if c == 6:
                        v = matv[rows, :].astype(F32)
                    else:
                        v = ext[c, rows, :]
                        if c >= 3:
                            v = v * 2.0
                    planes[plane_of(r, c), 8 * t : 8 * t + 8, :] = v
            return 0

        lax.fori_loop(0, 8, row, 0)

    def sends(first, last, own, up, down):
        z = pl.ds(8 * first, 8 * (last - first))
        pairs = []
        for a, b, n in ((6, 0, 18), (30, 18, 2), (33, 20, 15), (51, 35, 5)):
            pairs.append((planes.at[pl.ds(a, n), z], up.at[pl.ds(b, n)]))
        for a, b, n in ((0, 0, 17), (24, 17, 15), (48, 32, 5)):
            pairs.append((planes.at[pl.ds(a, n), z], down.at[pl.ds(b, n)]))
        pairs.append((planes.at[:, z], own))
        return pairs

    rows_of(CUT, 10)
    pairs = sends(CUT, 10, own_u, up_u, down_u)
    upper = [pltpu.make_async_copy(a, b, sems.at[i]) for i, (a, b) in enumerate(pairs)]
    for copy in upper:
        copy.start()
    rows_of(0, CUT)
    pairs = sends(0, CUT, own_l, up_l, down_l)
    lower = [pltpu.make_async_copy(a, b, sems.at[8 + i]) for i, (a, b) in enumerate(pairs)]
    for copy in lower:
        copy.start()
    for copy in upper + lower:
        copy.wait()


def pack(el, mg, mat):
    shapes = []
    for layers, more in ((8 * (10 - CUT), 0), (8 * CUT, W)):
        shapes += [
            jax.ShapeDtypeStruct((8 * NC, layers, 128), F32),
            jax.ShapeDtypeStruct((40 + more, layers, 128), F32),
            jax.ShapeDtypeStruct((37 + more, layers, 128), F32),
        ]
    return pl.pallas_call(
        pack_kernel,
        out_shape=shapes,
        in_specs=[HBM] * 3,
        out_specs=[HBM] * 6,
        scratch_shapes=[
            pltpu.VMEM((6, 640, 128), F32),
            pltpu.VMEM((640, 128), jnp.int32),
            pltpu.VMEM((8 * NC, 80, 128), F32),
            pltpu.SemaphoreType.DMA((16,)),
        ],
        compiler_params=params(),
        cost_estimate=cost(20),
        name="pack",
    )(el, mg, mat)


def corner_kernel(from_low, from_high, edge_low, edge_high, edge, *refs):
    strips, up, down, up_l, down_l, sems = refs[2:]
    lane = lax.broadcasted_iota(jnp.int32, (8, 80, 128), 2)
    strips[:, 0:80, :] = jnp.where(lane % 16 < 8, from_high[...], from_low[...])
    lane = lax.broadcasted_iota(jnp.int32, (8, 8, 128), 2)
    strips[:, 80:88, :] = jnp.where(lane % 16 < 8, edge_high[...], edge_low[...])
    z = pl.ds(0, 8 * CUT)
    copies = [
        pltpu.make_async_copy(strips.at[pl.ds(8 - W, W), z], up_l.at[pl.ds(40, W)], sems.at[0]),
        pltpu.make_async_copy(strips.at[pl.ds(0, W), z], down_l.at[pl.ds(37, W)], sems.at[1]),
    ]
    for copy in copies:
        copy.start()
    for a, b, n in ((6, 0, 18), (30, 18, 2), (33, 20, 15), (51, 35, 5)):
        up[b : b + n] = edge[a : a + n]
    for a, b, n in ((0, 0, 17), (24, 17, 15), (48, 32, 5)):
        down[b : b + n] = edge[a : a + n]
    for r in range(W):
        for t in range(HIGH):
            z = 8 * (CUT + t)
            up[40 + HIGH * r + t] = strips[8 - W + r, z : z + 8, :]
            down[37 + HIGH * r + t] = strips[r, z : z + 8, :]
    for copy in copies:
        copy.wait()


def corners(from_low, from_high, edge_low, edge_high, edge, up_l, down_l):
    return pl.pallas_call(
        corner_kernel,
        out_shape=[
            jax.ShapeDtypeStruct((8, 88, 128), F32),
            jax.ShapeDtypeStruct((40 + W * HIGH, 8, 128), F32),
            jax.ShapeDtypeStruct((37 + W * HIGH, 8, 128), F32),
            jax.ShapeDtypeStruct(up_l.shape, F32),
            jax.ShapeDtypeStruct(down_l.shape, F32),
        ],
        in_specs=[LOCAL] * 5 + [HBM] * 2,
        out_specs=[LOCAL] * 3 + [HBM] * 2,
        scratch_shapes=[pltpu.SemaphoreType.DMA((2,))],
        input_output_aliases={5: 3, 6: 4},
        compiler_params=params(),
        cost_estimate=cost(1),
        name="corners",
    )(from_low, from_high, edge_low, edge_high, edge, up_l, down_l)


def steps_kernel(upper, decay, gain, low_c, high_c, strips, edge, *refs):
    gz = lax.axis_index("gz")
    nu, nl = 8 * (10 - CUT), 8 * CUT
    own_u, low_u, high_u = refs[:3]
    if upper:
        out, plane, *scratch = refs[3:]
        tiles, halo, counts = 11 - CUT, 10 - CUT, gz == 0
        sets = [((own_u, low_u, high_u), 0, nu, 0, nl)]
    else:
        own_l, low_l, high_l, _, out, *scratch = refs[3:]
        tiles, halo, counts = CUT + 3, 0, gz == 1
        sets = [
            ((own_l, low_l, high_l), 0, nl, 8, 0),
            ((own_u, low_u, high_u), 0, 16, 8 + nl, nl),
        ]
    on = 9 - CUT if upper else CUT + 1
    ea0, ea1, eb0, eb1, ma0, ma1, mb0, mb1, d0, d1, g0, g1, ya, yb, ym, sv, stage, sems = scratch
    es, ms, yes = ((ea0, ea1), (eb0, eb1)), ((ma0, ma1), (mb0, mb1)), (ya, yb)
    ds_, gs = (d0, d1), (g0, g1)

    first, mid, last_ = BASE, BASE + W, BASE + W + 8
    hz = 8 * halo
    moves = [(strips.at[:, pl.ds(80, 8)], sv.at[pl.ds(W, 8), pl.ds(hz, 8)])]
    for (own, low, high), start, layers, to, strip in sets:
        zd = pl.ds(to, layers)
        moves.append((strips.at[:, pl.ds(strip, layers)], sv.at[pl.ds(W, 8), zd]))
        if not upper and own is own_l:
            moves.append((low.at[pl.ds(40, W)], sv.at[pl.ds(0, W), zd]))
            moves.append((high.at[pl.ds(37, W)], sv.at[pl.ds(W + 8, W), zd]))
    early = len(moves)
    own_parts = ((0, 24, ea0, 3 * mid), (24, 24, ma0, 3 * mid), (48, 8, d0, mid))
    low_parts = (
        (0, 18, ea0, 3 * first),
        (18, 2, ma0, 3 * first),
        (20, 15, ma0, 3 * first + 3),
        (35, 5, d0, first + 1),
    )
    high_parts = ((0, 17, ea0, 3 * last_), (17, 15, ma0, 3 * last_), (32, 5, d0, last_))
    for (own, low, high), start, layers, to, strip in sets:
        for ref, parts in ((own, own_parts), (low, low_parts), (high, high_parts)):
            for a, n, dst, b in parts:
                z = pl.ds(to if dst is d0 else 8 + to, layers)
                moves.append((ref.at[pl.ds(a, n), pl.ds(start, layers)], dst.at[pl.ds(b, n), z]))
    for a, n, dst, b in own_parts:
        z = pl.ds(hz if dst is d0 else 8 + hz, 8)
        moves.append((edge.at[pl.ds(a, n)], dst.at[pl.ds(b, n), z]))
    copies = [pltpu.make_async_copy(a, b, sems.at[i]) for i, (a, b) in enumerate(moves)]
    for copy in copies:
        copy.start()
    for ref, parts in ((low_c, low_parts), (high_c, high_parts)):
        for a, n, dst, b in parts:
            z = hz if dst is d0 else 8 + hz
            for i in range(n):
                dst[b + i, z : z + 8, :] = ref[a + i]
    here = [(t, t) for t in range(HIGH)]
    if not upper:
        here = [(0, HIGH - 1), (CUT + 1, 0), (CUT + 2, 1)]
    for r in range(W):
        for t, u in here:
            sv[r, 8 * t : 8 * t + 8, :] = low_c[40 + HIGH * r + u]
            sv[W + 8 + r, 8 * t : 8 * t + 8, :] = high_c[37 + HIGH * r + u]

    zero = jnp.zeros((8, 128), F32)
    top = 8 + 8 * tiles

    def ends(r, _):
        for pair in ms:
            for m in pair:
                m[3 * r + X, 0:8, :] = zero
                m[3 * r + Y, 0:8, :] = zero
        for pair in es:
            for e in pair:
                e[3 * r + X, top : top + 8, :] = zero
                e[3 * r + Y, top : top + 8, :] = zero
        return 0

    lax.fori_loop(0, HELD, ends, 0)
    for copy in copies[:early]:
        copy.wait()

    def unpack(i, _):
        for row in range(2):
            r = 2 * i + row
            at = BASE + r
            for t in range(tiles):
                z = 8 * t
                v = sv[r, z : z + 8, :]
                for c in range(NC):
                    turned = pltpu.roll(v, 128 - 16 * c, 1) if c else v
                    if c < 3:
                        ea1[3 * at + c, 8 + z : 16 + z, :] = turned
                    elif c < 6:
                        ma1[3 * at + c - 3, 8 + z : 16 + z, :] = turned
                    else:
                        d1[at, z : z + 8, :] = turned
        return 0

    lax.fori_loop(0, ROWS // 2, unpack, 0)
    for copy in copies[early:]:
        copy.wait()

    @pl.when(jnp.logical_not(counts))
    def _():
        def clear(i, _):
            for ref in (ea0, ea1, ma0, ma1):
                ref[3 * BASE + i, hz + 8 : hz + 16, :] = zero
            return 0

        lax.fori_loop(0, 3 * ROWS, clear, 0)

    live = jnp.where(counts, 1.0, 0.0).astype(F32)

    lane = lax.broadcasted_iota(jnp.int32, (8, 128), 1)
    last, first_lane = lane == 127, lane == 0
    units = [(row, t) for row in range(2) for t in range(tiles)]

    def tables(r):
        for t in range(tiles):
            z = 8 * t
            for d, g in zip(ds_, gs):
                ids = d[r, z : z + 8, :]
                d_cells, g_cells = zero, zero
                for i in range(5):
                    hit = ids == float(i)
                    d_cells = jnp.where(hit, decay[i], d_cells)
                    g_cells = jnp.where(hit, gain[i] * 0.5, g_cells)
                if t == halo:
                    d_cells, g_cells = d_cells * live, g_cells * live
                d[r, z : z + 8, :] = d_cells
                g[r, z : z + 8, :] = g_cells

    def turn_two(which, r0, beside=None):
        kept = []
        for row, t in units:
            for j, c in enumerate((X, Z)):
                pair = [
                    pltpu.roll(e[3 * r0 + (3 * row + c), 8 + 8 * t : 16 + 8 * t, :], 127, 1)
                    for e in es[which]
                ]
                kept.append((4 * row + 2 * j, 8 * t, pair))
        if beside:
            beside()
        y = yes[which]
        for i, z, (a, b) in kept:
            y[4 * r0 + i, z : z + 8, :] = jnp.where(last, b, a)
            y[4 * r0 + (i + 1), z : z + 8, :] = jnp.where(last, a, b)

    def first_turn(i, _):
        r0 = BASE + 2 * i

        def both():
            tables(r0)
            tables(r0 + 1)

        turn_two(0, r0, both)
        return 0

    lax.fori_loop(0, ROWS // 2, first_turn, 0)

    def block(old, with_e, with_m, m, start):
        new = 1 - old
        base = start + 2 * m
        b3, b4 = 3 * base, 4 * base
        waiting = []
        half = len(units) // 2
        jobs_m = [(ms, row, t) for row, t in units] if with_e else []
        jobs_e = [(es, row, t) for row, t in units] if with_e else []

        def turn(refs, row, t):
            z = 8 * t
            if refs is ms:
                pairs = [
                    [pltpu.roll(f[b3 + (3 * (row - 2) + c), 8 + z : 16 + z, :], 1, 1) for f in ms[new]]
                    for c in (X, Z)
                ]
                waiting.append((ym, 0, 4 * row, z, pairs, first_lane))
            else:
                pairs = [
                    [pltpu.roll(f[b3 + (3 * (row - 4) + c), 8 + z : 16 + z, :], 127, 1) for f in es[new]]
                    for c in (X, Z)
                ]
                waiting.append((yes[new], b4, 4 * (row - 4), z, pairs, last))

        def keep():
            y, b, i, z, pairs, edge_lane = waiting.pop(0)
            for j, (v0, v1) in enumerate(pairs):
                y[b + (i + 2 * j), z : z + 8, :] = jnp.where(edge_lane, v1, v0)
                y[b + (i + 2 * j + 1), z : z + 8, :] = jnp.where(edge_lane, v0, v1)

        def settle(most):
            while len(waiting) > most:
                keep()

        for u, (row, t) in enumerate(units if with_m else ()):
            if jobs_m:
                turn(*jobs_m.pop(0))
                if u >= half:
                    turn(*jobs_e.pop(0))
            settle(LAG)
            z = 8 * t
            for k in range(2):

                def electric(c, r=row, shift=0):
                    return es[old][k][b3 + (3 * r + c), 8 + z + shift : 16 + z + shift, :]

                def magnetic(c):
                    return ms[old][k][b3 + (3 * row + c), 8 + z : 16 + z, :]

                ex_y = yes[old][b4 + (4 * row + k), z : z + 8, :]
                ez_y = yes[old][b4 + (4 * row + 2 + k), z : z + 8, :]
                ex, ey, ez = electric(X), electric(Y), electric(Z)
                cx = (ez_y - ez) - (electric(Y, row, 1) - ey)
                cy = (electric(X, row, 1) - ex) - (electric(Z, row + 1) - ez)
                cz = (electric(Y, row + 1) - ey) - (ex_y - ex)
                if t == halo and not upper:
                    cx, cy, cz = cx * live, cy * live, cz * live
                mx, my, mz = magnetic(X) - cx, magnetic(Y) - cy, magnetic(Z) - cz
                for c, v in ((X, mx), (Y, my), (Z, mz)):
                    ms[new][k][b3 + (3 * row + c), 8 + z : 16 + z, :] = v
        for job in jobs_m:
            turn(*job)
            settle(LAG)
        for row, t in units if with_e else ():
            if jobs_e:
                turn(*jobs_e.pop(0))
            settle(LAG if jobs_e else max(len(waiting) - 2, 0))
            e, z = row - 2, 8 * t
            for k in range(2):

                def magnetic(c, r=e, shift=0):
                    return ms[new][k][b3 + (3 * r + c), 8 + z + shift : 16 + z + shift, :]

                def electric(c):
                    return es[old][k][b3 + (3 * e + c), 8 + z : 16 + z, :]

                mx_y = ym[4 * row + k, z : z + 8, :]
                mz_y = ym[4 * row + 2 + k, z : z + 8, :]
                mx, my, mz = magnetic(X), magnetic(Y), magnetic(Z)
                d = ds_[k][base + e, z : z + 8, :]
                g = gs[k][base + e, z : z + 8, :]
                ex = d * electric(X) + g * ((mz - mz_y) - (my - magnetic(Y, e, -1)))
                ey = d * electric(Y) + g * ((mx - magnetic(X, e, -1)) - (mz - magnetic(Z, e - 1)))
                ez = d * electric(Z) + g * ((my - magnetic(Y, e - 1)) - (mx - mx_y))
                for c, v in ((X, ex), (Y, ey), (Z, ez)):
                    es[new][k][b3 + (3 * e + c), 8 + z : 16 + z, :] = v
        settle(0)
        return start

    def two_steps(s, _):
        for old in range(2):
            left = STEPS - 1 - old - 2 * s
            start = BASE + W - left - 2
            lax.fori_loop(0, 2, functools.partial(block, old, False, True), start)
            lax.fori_loop(2, W - 1 + left, functools.partial(block, old, True, True), start)
            block(old, True, False, W - 1 + left, start)
            turn_two(1 - old, start + 2 * (W - 2 + left))
        return 0

    lax.fori_loop(0, STEPS // 2, two_steps, 0)

    def emit(r, _):
        for c, source in enumerate((X, Y, Z)):
            for t in range(on):
                stage[c, pl.ds(64 * t + r, 8, stride=8), :] = ea0[
                    3 * (r + BASE + W) + source, 16 + 8 * t : 24 + 8 * t, :
                ]
        return 0

    lax.fori_loop(0, 8, emit, 0)
    if upper:
        plane[0] = stage[0, 64 * on - 8 : 64 * on, :]
        plane[1] = stage[1, 64 * on - 8 : 64 * on, :]
    copy_all([(stage, out.at[:, pl.ds(64 * (CUT + 1) if upper else 0, 64 * on)])], sems)


def run_steps(upper, decay, gain, sides, arrays):
    smem = pl.BlockSpec(memory_space=pltpu.SMEM)
    out_shape = [jax.ShapeDtypeStruct((3, 640, 128), F32)]
    out_specs = [HBM]
    aliases = {}
    if upper:
        out_shape.append(jax.ShapeDtypeStruct((2, 8, 128), F32))
        out_specs.append(LOCAL)
    else:
        aliases = {6 + len(arrays) - 1: 0}
    tiles, on = (11 - CUT, 9 - CUT) if upper else (CUT + 3, CUT + 1)
    z = 16 + 8 * tiles
    field = pltpu.VMEM((3 * HELD, z, 128), F32)
    table = pltpu.VMEM((HELD, 8 * tiles, 128), F32)
    turned = pltpu.VMEM((4 * HELD, 8 * tiles, 128), F32)
    return pl.pallas_call(
        functools.partial(steps_kernel, upper),
        out_shape=out_shape,
        in_specs=[smem, smem, LOCAL, LOCAL] + [HBM] * (2 + len(arrays)),
        out_specs=out_specs,
        scratch_shapes=[field] * 8
        + [table] * 4
        + [turned] * 2
        + [
            pltpu.VMEM((8, 8 * tiles, 128), F32),
            pltpu.VMEM((ROWS, 8 * tiles, 128), F32),
            pltpu.VMEM((3, 64 * on, 128), F32),
            pltpu.SemaphoreType.DMA((39,)),
        ],
        input_output_aliases=aliases,
        compiler_params=params(),
        cost_estimate=cost(100),
        name="steps_upper" if upper else "steps_lower",
    )(decay, gain, *sides, *arrays)


def image_kernel(weights, own, received, out, sh, rhs):
    gz = lax.axis_index("gz")
    centre, before, after = [
        [jnp.where(gz == 1, own[i, c], received[i, c]) for c in range(2)] for i in range(3)
    ]
    lane = lax.broadcasted_iota(jnp.int32, (24, 128), 1)
    for q in range(15):
        shift = q - 7
        for c in range(2):
            v = centre[c]
            if shift > 0:
                v = jnp.where(
                    lane >= 128 - shift,
                    pltpu.roll(after[c], 128 - shift, 1),
                    pltpu.roll(v, 128 - shift, 1),
                )
            elif shift < 0:
                v = jnp.where(
                    lane < -shift, pltpu.roll(before[c], -shift, 1), pltpu.roll(v, -shift, 1)
                )
            sh[q, c] = v

    def fill(side):
        for q in range(15):
            for c in range(2):
                for i in range(4):
                    start = 4 * side + 1 + i
                    rhs[16 * q : 16 * q + 16, (4 * c + i) * 128 : (4 * c + i + 1) * 128] = sh[
                        q, c, start : start + 16, :
                    ]

    @pl.when(gz == 0)
    def _():
        fill(0)

    @pl.when(gz == 1)
    def _():
        fill(1)

    amplitude = jnp.dot(
        weights[...],
        rhs[...],
        precision=lax.Precision.HIGHEST,
        preferred_element_type=jnp.float32,
    )
    power = jnp.sum(amplitude * amplitude, axis=0, keepdims=True)
    for i in range(4):
        out[i : i + 1, :] = (
            power[:, i * 128 : (i + 1) * 128] + power[:, (4 + i) * 128 : (5 + i) * 128]
        )


def image_of(weights, own, received):
    return pl.pallas_call(
        image_kernel,
        out_shape=jax.ShapeDtypeStruct((4, 128), jnp.float32),
        in_specs=[LOCAL] * 3,
        out_specs=LOCAL,
        scratch_shapes=[
            pltpu.VMEM((15, 2, 24, 128), jnp.float32),
            pltpu.VMEM((240, 1024), jnp.float32),
        ],
        compiler_params=pltpu.CompilerParams(vmem_limit_bytes=VMEM),
        name="image",
    )(weights, own, received)


def on_device(electric, magnetic, material, decay, gain, kernels):
    el = electric.reshape(3, 640, 128)
    mg = magnetic.reshape(3, 640, 128)
    mat = material.reshape(640, 128)
    weights = jnp.pad(
        kernels.transpose(0, 1, 3, 2).reshape(48, 15, 15), ((0, 0), (0, 0), (0, 1))
    ).reshape(48, 240)

    strips, edge, edge_strips = own_strips(el, mg, mat)
    edge = around(edge, "gz", 1)
    from_low, from_high = around(strips, "gy", 1), around(strips, "gy", -1)
    edge_low, edge_high = beyond(edge_strips, 1), beyond(edge_strips, -1)
    own_u, up_u, down_u, own_l, up_l, down_l = pack(el, mg, mat)
    up_u, down_u, edge_low, edge_high = lax.optimization_barrier(
        (up_u, down_u, edge_low, edge_high)
    )
    low_u, high_u = around(up_u, "gx", 1), around(down_u, "gx", -1)
    strips, up_c, down_c, up_l, down_l = corners(
        from_low, from_high, edge_low, edge_high, edge, up_l, down_l
    )
    low_c, high_c = around(up_c, "gx", 1), around(down_c, "gx", -1)
    low_l, high_l = around(up_l, "gx", 1), around(down_l, "gx", -1)

    sides = [low_c, high_c, strips, edge]
    field, plane = run_steps(True, decay, gain, sides, [own_u, low_u, high_u])
    top = jnp.stack([plane, around(plane, "gy", 1), around(plane, "gy", -1)])
    top = jnp.concatenate([around(top, "gx", 1), top, around(top, "gx", -1)], 2)
    top, low_l, high_l = lax.optimization_barrier((top, low_l, high_l))
    received = lax.ppermute(top, "gz", [(1, 0)])
    (field,) = run_steps(
        False, decay, gain, sides, [own_u, low_u, high_u, own_l, low_l, high_l, field]
    )
    image = image_of(weights, top, received)
    return (field.reshape(3, 80, 8, 128), image)


def solution(mesh):
    in_specs = (
        P(None, "gz", "gx", "gy"),
        P(None, "gz", "gx", "gy"),
        P("gz", "gx", "gy"),
        P(),
        P(),
        P(),
    )
    out_specs = (P(None, "gz", "gx", "gy"), P(("gx", "gz"), "gy"))
    return jax.shard_map(
        on_device, mesh=mesh, in_specs=in_specs, out_specs=out_specs, check_vma=False
    )
```

```python
import functools

import jax
import jax.numpy as jnp
from jax import lax
from jax.experimental import pallas as pl
from jax.experimental.pallas import tpu as pltpu
from jax.sharding import PartitionSpec as P

STEPS = 6
W = STEPS
Y, Z, X = range(3)
NC = 7
SOURCE = ((0, 1), (0, 2), (0, 0), (1, 1), (1, 2), (1, 0))
ROWS = 8 + 2 * W
BASE = 4
HELD = BASE + ROWS + 2
CUT = 7
HIGH = 11 - CUT
LAG = 4
VMEM = 63 * 1024 * 1024
F32 = jnp.float32
HBM = pl.BlockSpec(memory_space=pl.ANY)
LOCAL = pl.BlockSpec(memory_space=pltpu.VMEM)


def around(value, axis, steps):
    count = lax.axis_size(axis)
    return lax.ppermute(value, axis, [(i, (i + steps) % count) for i in range(count)])


def beyond(value, steps):
    ny, nz = lax.axis_size("gy"), lax.axis_size("gz")
    pairs = [
        (y * nz + z, (y + steps) % ny * nz + (z + 1) % nz) for y in range(ny) for z in range(nz)
    ]
    return lax.ppermute(value, ("gy", "gz"), pairs)


def copy_all(pairs, sems):
    copies = [pltpu.make_async_copy(a, b, sems.at[i]) for i, (a, b) in enumerate(pairs)]
    for copy in copies:
        copy.start()
    for copy in copies:
        copy.wait()


def params():
    return pltpu.CompilerParams(vmem_limit_bytes=VMEM)


def cost(us):
    return pl.CostEstimate(flops=int(us * 1e9), bytes_accessed=int(us * 3e6), transcendentals=0)


def plane_of(r, c):
    return 48 + r if c == 6 else 24 * (c // 3) + 3 * r + c % 3


def strip_masks():
    lane = lax.broadcasted_iota(jnp.int32, (8, 128), 1)
    return [((lane - 16 * c + W + 128) % 128) < 2 * W for c in range(NC)]


def strip_kernel(el, mg, mat, strips, edge, edge_strips, ext, matv, sems):
    gz = lax.axis_index("gz")
    loads = [(mat, matv)]
    for c, (which, comp) in enumerate(SOURCE):
        loads.append(((el, mg)[which].at[comp], ext.at[c]))
    copy_all(loads, sems)
    masks = strip_masks()

    def layers(c, t, r):
        rows = pl.ds(64 * t + r, 8, stride=8)
        if c == 6:
            return matv[rows, :].astype(F32)
        v = ext[c, rows, :]
        return v * 2.0 if c >= 3 else v

    def row(r, _):
        for t in range(10):
            total = layers(0, t, r)
            for c in range(1, NC):
                total = jnp.where(masks[c], pltpu.roll(layers(c, t, r), 16 * c, 1), total)
            strips[r, 8 * t : 8 * t + 8, :] = total
        return 0

    lax.fori_loop(0, 8, row, 0)

    def edges(t):
        for r in range(8):
            for c in range(NC):
                edge[plane_of(r, c)] = layers(c, t, r)
        edge_strips[...] = strips[:, 8 * t : 8 * t + 8, :]

    @pl.when(gz == 0)
    def _():
        edges(9)

    @pl.when(gz == 1)
    def _():
        edges(0)


def own_strips(el, mg, mat):
    return pl.pallas_call(
        strip_kernel,
        out_shape=[
            jax.ShapeDtypeStruct((8, 80, 128), F32),
            jax.ShapeDtypeStruct((8 * NC, 8, 128), F32),
            jax.ShapeDtypeStruct((8, 8, 128), F32),
        ],
        in_specs=[HBM] * 3,
        out_specs=[LOCAL] * 3,
        scratch_shapes=[
            pltpu.VMEM((6, 640, 128), F32),
            pltpu.VMEM((640, 128), jnp.int32),
            pltpu.SemaphoreType.DMA((7,)),
        ],
        compiler_params=params(),
        cost_estimate=cost(3),
        name="own_strips",
    )(el, mg, mat)


def pack_kernel(first, last, el, mg, mat, *refs):
    if first:
        own, up, down, ext, matv, planes, sems = refs
    else:
        strips, own, up, down, ext, matv, planes, sems = refs
    tiles = last - first
    here = pl.ds(64 * first, 64 * tiles)
    loads = [(mat.at[here], matv)]
    for c, (which, comp) in enumerate(SOURCE):
        loads.append(((el, mg)[which].at[comp, here], ext.at[c]))
    copy_all(loads, sems)

    def row(r, _):
        for t in range(tiles):
            rows = pl.ds(64 * t + r, 8, stride=8)
            for c in range(NC):
                if c == 6:
                    v = matv[rows, :].astype(F32)
                else:
                    v = ext[c, rows, :]
                    if c >= 3:
                        v = v * 2.0
                planes[plane_of(r, c), 8 * t : 8 * t + 8, :] = v
        return 0

    lax.fori_loop(0, 8, row, 0)
    z = pl.ds(0, 8 * tiles)
    pairs = [(planes, own)]
    for a, b, n in ((6, 0, 18), (30, 18, 2), (33, 20, 15), (51, 35, 5)):
        pairs.append((planes.at[pl.ds(a, n)], up.at[pl.ds(b, n), z]))
    for a, b, n in ((0, 0, 17), (24, 17, 15), (48, 32, 5)):
        pairs.append((planes.at[pl.ds(a, n)], down.at[pl.ds(b, n), z]))
    if not first:
        pairs.append((strips.at[pl.ds(8 - W, W), z], up.at[pl.ds(40, W)]))
        pairs.append((strips.at[pl.ds(0, W), z], down.at[pl.ds(37, W)]))
    copy_all(pairs, sems)


def pack(first, last, el, mg, mat, *strips):
    layers = 8 * (last - first)
    more = 0 if first else W
    return pl.pallas_call(
        functools.partial(pack_kernel, first, last),
        out_shape=[
            jax.ShapeDtypeStruct((8 * NC, layers, 128), F32),
            jax.ShapeDtypeStruct((40 + more, layers, 128), F32),
            jax.ShapeDtypeStruct((37 + more, layers, 128), F32),
        ],
        in_specs=[HBM] * 3 + [LOCAL] * len(strips),
        out_specs=[HBM] * 3,
        scratch_shapes=[
            pltpu.VMEM((6, 8 * layers, 128), F32),
            pltpu.VMEM((8 * layers, 128), jnp.int32),
            pltpu.VMEM((8 * NC, layers, 128), F32),
            pltpu.SemaphoreType.DMA((10,)),
        ],
        compiler_params=params(),
        cost_estimate=cost(20 if first else 3),
        name="pack_upper" if first else "pack_lower",
    )(el, mg, mat, *strips)


def corner_kernel(from_low, from_high, edge_low, edge_high, edge, strips, up, down):
    lane = lax.broadcasted_iota(jnp.int32, (8, 80, 128), 2)
    strips[:, 0:80, :] = jnp.where(lane % 16 < 8, from_high[...], from_low[...])
    lane = lax.broadcasted_iota(jnp.int32, (8, 8, 128), 2)
    strips[:, 80:88, :] = jnp.where(lane % 16 < 8, edge_high[...], edge_low[...])
    for a, b, n in ((6, 0, 18), (30, 18, 2), (33, 20, 15), (51, 35, 5)):
        up[b : b + n] = edge[a : a + n]
    for a, b, n in ((0, 0, 17), (24, 17, 15), (48, 32, 5)):
        down[b : b + n] = edge[a : a + n]
    for r in range(W):
        for t in range(HIGH):
            z = 8 * (CUT + t)
            up[40 + HIGH * r + t] = strips[8 - W + r, z : z + 8, :]
            down[37 + HIGH * r + t] = strips[r, z : z + 8, :]


def corners(from_low, from_high, edge_low, edge_high, edge):
    return pl.pallas_call(
        corner_kernel,
        out_shape=[
            jax.ShapeDtypeStruct((8, 88, 128), F32),
            jax.ShapeDtypeStruct((40 + W * HIGH, 8, 128), F32),
            jax.ShapeDtypeStruct((37 + W * HIGH, 8, 128), F32),
        ],
        in_specs=[LOCAL] * 5,
        out_specs=[LOCAL] * 3,
        compiler_params=params(),
        cost_estimate=cost(1),
        name="corners",
    )(from_low, from_high, edge_low, edge_high, edge)


def steps_kernel(upper, decay, gain, low_c, high_c, strips, edge, *refs):
    gz = lax.axis_index("gz")
    nu, nl = 8 * (10 - CUT), 8 * CUT
    own_u, low_u, high_u = refs[:3]
    if upper:
        out, plane, *scratch = refs[3:]
        tiles, halo, counts = 11 - CUT, 10 - CUT, gz == 0
        sets = [((own_u, low_u, high_u), 0, nu, 0, nl)]
    else:
        own_l, low_l, high_l, _, out, *scratch = refs[3:]
        tiles, halo, counts = CUT + 3, 0, gz == 1
        sets = [
            ((own_l, low_l, high_l), 0, nl, 8, 0),
            ((own_u, low_u, high_u), 0, 16, 8 + nl, nl),
        ]
    on = 9 - CUT if upper else CUT + 1
    ea0, ea1, eb0, eb1, ma0, ma1, mb0, mb1, d0, d1, g0, g1, ya, yb, ym, sv, stage, sems = scratch
    es, ms, yes = ((ea0, ea1), (eb0, eb1)), ((ma0, ma1), (mb0, mb1)), (ya, yb)
    ds_, gs = (d0, d1), (g0, g1)

    first, mid, last_ = BASE, BASE + W, BASE + W + 8
    hz = 8 * halo
    moves = [(strips.at[:, pl.ds(80, 8)], sv.at[pl.ds(W, 8), pl.ds(hz, 8)])]
    for (own, low, high), start, layers, to, strip in sets:
        zd = pl.ds(to, layers)
        moves.append((strips.at[:, pl.ds(strip, layers)], sv.at[pl.ds(W, 8), zd]))
        if not upper and own is own_l:
            moves.append((low.at[pl.ds(40, W)], sv.at[pl.ds(0, W), zd]))
            moves.append((high.at[pl.ds(37, W)], sv.at[pl.ds(W + 8, W), zd]))
    early = len(moves)
    own_parts = ((0, 24, ea0, 3 * mid), (24, 24, ma0, 3 * mid), (48, 8, d0, mid))
    low_parts = (
        (0, 18, ea0, 3 * first),
        (18, 2, ma0, 3 * first),
        (20, 15, ma0, 3 * first + 3),
        (35, 5, d0, first + 1),
    )
    high_parts = ((0, 17, ea0, 3 * last_), (17, 15, ma0, 3 * last_), (32, 5, d0, last_))
    for (own, low, high), start, layers, to, strip in sets:
        for ref, parts in ((own, own_parts), (low, low_parts), (high, high_parts)):
            for a, n, dst, b in parts:
                z = pl.ds(to if dst is d0 else 8 + to, layers)
                moves.append((ref.at[pl.ds(a, n), pl.ds(start, layers)], dst.at[pl.ds(b, n), z]))
    for a, n, dst, b in own_parts:
        z = pl.ds(hz if dst is d0 else 8 + hz, 8)
        moves.append((edge.at[pl.ds(a, n)], dst.at[pl.ds(b, n), z]))
    copies = [pltpu.make_async_copy(a, b, sems.at[i]) for i, (a, b) in enumerate(moves)]
    for copy in copies:
        copy.start()
    for ref, parts in ((low_c, low_parts), (high_c, high_parts)):
        for a, n, dst, b in parts:
            z = hz if dst is d0 else 8 + hz
            for i in range(n):
                dst[b + i, z : z + 8, :] = ref[a + i]
    here = [(t, t) for t in range(HIGH)]
    if not upper:
        here = [(0, HIGH - 1), (CUT + 1, 0), (CUT + 2, 1)]
    for r in range(W):
        for t, u in here:
            sv[r, 8 * t : 8 * t + 8, :] = low_c[40 + HIGH * r + u]
            sv[W + 8 + r, 8 * t : 8 * t + 8, :] = high_c[37 + HIGH * r + u]

    zero = jnp.zeros((8, 128), F32)
    top = 8 + 8 * tiles

    def ends(r, _):
        for pair in ms:
            for m in pair:
                m[3 * r + X, 0:8, :] = zero
                m[3 * r + Y, 0:8, :] = zero
        for pair in es:
            for e in pair:
                e[3 * r + X, top : top + 8, :] = zero
                e[3 * r + Y, top : top + 8, :] = zero
        return 0

    lax.fori_loop(0, HELD, ends, 0)
    for copy in copies[:early]:
        copy.wait()

    def unpack(i, _):
        for row in range(2):
            r = 2 * i + row
            at = BASE + r
            for t in range(tiles):
                z = 8 * t
                v = sv[r, z : z + 8, :]
                for c in range(NC):
                    turned = pltpu.roll(v, 128 - 16 * c, 1) if c else v
                    if c < 3:
                        ea1[3 * at + c, 8 + z : 16 + z, :] = turned
                    elif c < 6:
                        ma1[3 * at + c - 3, 8 + z : 16 + z, :] = turned
                    else:
                        d1[at, z : z + 8, :] = turned
        return 0

    lax.fori_loop(0, ROWS // 2, unpack, 0)
    for copy in copies[early:]:
        copy.wait()

    @pl.when(jnp.logical_not(counts))
    def _():
        def clear(i, _):
            for ref in (ea0, ea1, ma0, ma1):
                ref[3 * BASE + i, hz + 8 : hz + 16, :] = zero
            return 0

        lax.fori_loop(0, 3 * ROWS, clear, 0)

    live = jnp.where(counts, 1.0, 0.0).astype(F32)

    lane = lax.broadcasted_iota(jnp.int32, (8, 128), 1)
    last, first_lane = lane == 127, lane == 0
    units = [(row, t) for row in range(2) for t in range(tiles)]

    def tables(r):
        for t in range(tiles):
            z = 8 * t
            for d, g in zip(ds_, gs):
                ids = d[r, z : z + 8, :]
                d_cells, g_cells = zero, zero
                for i in range(5):
                    hit = ids == float(i)
                    d_cells = jnp.where(hit, decay[i], d_cells)
                    g_cells = jnp.where(hit, gain[i] * 0.5, g_cells)
                if t == halo:
                    d_cells, g_cells = d_cells * live, g_cells * live
                d[r, z : z + 8, :] = d_cells
                g[r, z : z + 8, :] = g_cells

    def turn_two(which, r0, beside=None):
        kept = []
        for row, t in units:
            for j, c in enumerate((X, Z)):
                pair = [
                    pltpu.roll(e[3 * r0 + (3 * row + c), 8 + 8 * t : 16 + 8 * t, :], 127, 1)
                    for e in es[which]
                ]
                kept.append((4 * row + 2 * j, 8 * t, pair))
        if beside:
            beside()
        y = yes[which]
        for i, z, (a, b) in kept:
            y[4 * r0 + i, z : z + 8, :] = jnp.where(last, b, a)
            y[4 * r0 + (i + 1), z : z + 8, :] = jnp.where(last, a, b)

    def first_turn(i, _):
        r0 = BASE + 2 * i

        def both():
            tables(r0)
            tables(r0 + 1)

        turn_two(0, r0, both)
        return 0

    lax.fori_loop(0, ROWS // 2, first_turn, 0)

    def block(old, with_e, with_m, m, start):
        new = 1 - old
        base = start + 2 * m
        b3, b4 = 3 * base, 4 * base
        waiting = []
        half = len(units) // 2
        jobs_m = [(ms, row, t) for row, t in units] if with_e else []
        jobs_e = [(es, row, t) for row, t in units] if with_e else []

        def turn(refs, row, t):
            z = 8 * t
            if refs is ms:
                pairs = [
                    [pltpu.roll(f[b3 + (3 * (row - 2) + c), 8 + z : 16 + z, :], 1, 1) for f in ms[new]]
                    for c in (X, Z)
                ]
                waiting.append((ym, 0, 4 * row, z, pairs, first_lane))
            else:
                pairs = [
                    [pltpu.roll(f[b3 + (3 * (row - 4) + c), 8 + z : 16 + z, :], 127, 1) for f in es[new]]
                    for c in (X, Z)
                ]
                waiting.append((yes[new], b4, 4 * (row - 4), z, pairs, last))

        def keep():
            y, b, i, z, pairs, edge_lane = waiting.pop(0)
            for j, (v0, v1) in enumerate(pairs):
                y[b + (i + 2 * j), z : z + 8, :] = jnp.where(edge_lane, v1, v0)
                y[b + (i + 2 * j + 1), z : z + 8, :] = jnp.where(edge_lane, v0, v1)

        def settle(most):
            while len(waiting) > most:
                keep()

        for u, (row, t) in enumerate(units if with_m else ()):
            if jobs_m:
                turn(*jobs_m.pop(0))
                if u >= half:
                    turn(*jobs_e.pop(0))
            settle(LAG)
            z = 8 * t
            for k in range(2):

                def electric(c, r=row, shift=0):
                    return es[old][k][b3 + (3 * r + c), 8 + z + shift : 16 + z + shift, :]

                def magnetic(c):
                    return ms[old][k][b3 + (3 * row + c), 8 + z : 16 + z, :]

                ex_y = yes[old][b4 + (4 * row + k), z : z + 8, :]
                ez_y = yes[old][b4 + (4 * row + 2 + k), z : z + 8, :]
                ex, ey, ez = electric(X), electric(Y), electric(Z)
                cx = (ez_y - ez) - (electric(Y, row, 1) - ey)
                cy = (electric(X, row, 1) - ex) - (electric(Z, row + 1) - ez)
                cz = (electric(Y, row + 1) - ey) - (ex_y - ex)
                if t == halo and not upper:
                    cx, cy, cz = cx * live, cy * live, cz * live
                mx, my, mz = magnetic(X) - cx, magnetic(Y) - cy, magnetic(Z) - cz
                for c, v in ((X, mx), (Y, my), (Z, mz)):
                    ms[new][k][b3 + (3 * row + c), 8 + z : 16 + z, :] = v
        for job in jobs_m:
            turn(*job)
            settle(LAG)
        for row, t in units if with_e else ():
            if jobs_e:
                turn(*jobs_e.pop(0))
            settle(LAG if jobs_e else max(len(waiting) - 2, 0))
            e, z = row - 2, 8 * t
            for k in range(2):

                def magnetic(c, r=e, shift=0):
                    return ms[new][k][b3 + (3 * r + c), 8 + z + shift : 16 + z + shift, :]

                def electric(c):
                    return es[old][k][b3 + (3 * e + c), 8 + z : 16 + z, :]

                mx_y = ym[4 * row + k, z : z + 8, :]
                mz_y = ym[4 * row + 2 + k, z : z + 8, :]
                mx, my, mz = magnetic(X), magnetic(Y), magnetic(Z)
                d = ds_[k][base + e, z : z + 8, :]
                g = gs[k][base + e, z : z + 8, :]
                ex = d * electric(X) + g * ((mz - mz_y) - (my - magnetic(Y, e, -1)))
                ey = d * electric(Y) + g * ((mx - magnetic(X, e, -1)) - (mz - magnetic(Z, e - 1)))
                ez = d * electric(Z) + g * ((my - magnetic(Y, e - 1)) - (mx - mx_y))
                for c, v in ((X, ex), (Y, ey), (Z, ez)):
                    es[new][k][b3 + (3 * e + c), 8 + z : 16 + z, :] = v
        settle(0)
        return start

    def two_steps(s, _):
        for old in range(2):
            left = STEPS - 1 - old - 2 * s
            start = BASE + W - left - 2
            lax.fori_loop(0, 2, functools.partial(block, old, False, True), start)
            lax.fori_loop(2, W - 1 + left, functools.partial(block, old, True, True), start)
            block(old, True, False, W - 1 + left, start)
            turn_two(1 - old, start + 2 * (W - 2 + left))
        return 0

    lax.fori_loop(0, STEPS // 2, two_steps, 0)

    def emit(r, _):
        for c, source in enumerate((X, Y, Z)):
            for t in range(on):
                stage[c, pl.ds(64 * t + r, 8, stride=8), :] = ea0[
                    3 * (r + BASE + W) + source, 16 + 8 * t : 24 + 8 * t, :
                ]
        return 0

    lax.fori_loop(0, 8, emit, 0)
    if upper:
        plane[0] = stage[0, 64 * on - 8 : 64 * on, :]
        plane[1] = stage[1, 64 * on - 8 : 64 * on, :]
    copy_all([(stage, out.at[:, pl.ds(64 * (CUT + 1) if upper else 0, 64 * on)])], sems)


def run_steps(upper, decay, gain, sides, arrays):
    smem = pl.BlockSpec(memory_space=pltpu.SMEM)
    out_shape = [jax.ShapeDtypeStruct((3, 640, 128), F32)]
    out_specs = [HBM]
    aliases = {}
    if upper:
        out_shape.append(jax.ShapeDtypeStruct((2, 8, 128), F32))
        out_specs.append(LOCAL)
    else:
        aliases = {6 + len(arrays) - 1: 0}
    tiles, on = (11 - CUT, 9 - CUT) if upper else (CUT + 3, CUT + 1)
    z = 16 + 8 * tiles
    field = pltpu.VMEM((3 * HELD, z, 128), F32)
    table = pltpu.VMEM((HELD, 8 * tiles, 128), F32)
    turned = pltpu.VMEM((4 * HELD, 8 * tiles, 128), F32)
    return pl.pallas_call(
        functools.partial(steps_kernel, upper),
        out_shape=out_shape,
        in_specs=[smem, smem, LOCAL, LOCAL] + [HBM] * (2 + len(arrays)),
        out_specs=out_specs,
        scratch_shapes=[field] * 8
        + [table] * 4
        + [turned] * 2
        + [
            pltpu.VMEM((8, 8 * tiles, 128), F32),
            pltpu.VMEM((ROWS, 8 * tiles, 128), F32),
            pltpu.VMEM((3, 64 * on, 128), F32),
            pltpu.SemaphoreType.DMA((39,)),
        ],
        input_output_aliases=aliases,
        compiler_params=params(),
        cost_estimate=cost(100),
        name="steps_upper" if upper else "steps_lower",
    )(decay, gain, *sides, *arrays)


def image_kernel(weights, own, received, out, sh, rhs):
    gz = lax.axis_index("gz")
    centre, before, after = [
        [jnp.where(gz == 1, own[i, c], received[i, c]) for c in range(2)] for i in range(3)
    ]
    lane = lax.broadcasted_iota(jnp.int32, (24, 128), 1)
    for q in range(15):
        shift = q - 7
        for c in range(2):
            v = centre[c]
            if shift > 0:
                v = jnp.where(
                    lane >= 128 - shift,
                    pltpu.roll(after[c], 128 - shift, 1),
                    pltpu.roll(v, 128 - shift, 1),
                )
            elif shift < 0:
                v = jnp.where(
                    lane < -shift, pltpu.roll(before[c], -shift, 1), pltpu.roll(v, -shift, 1)
                )
            sh[q, c] = v

    def fill(side):
        for q in range(15):
            for c in range(2):
                for i in range(4):
                    start = 4 * side + 1 + i
                    rhs[16 * q : 16 * q + 16, (4 * c + i) * 128 : (4 * c + i + 1) * 128] = sh[
                        q, c, start : start + 16, :
                    ]

    @pl.when(gz == 0)
    def _():
        fill(0)

    @pl.when(gz == 1)
    def _():
        fill(1)

    amplitude = jnp.dot(
        weights[...],
        rhs[...],
        precision=lax.Precision.HIGHEST,
        preferred_element_type=jnp.float32,
    )
    power = jnp.sum(amplitude * amplitude, axis=0, keepdims=True)
    for i in range(4):
        out[i : i + 1, :] = (
            power[:, i * 128 : (i + 1) * 128] + power[:, (4 + i) * 128 : (5 + i) * 128]
        )


def image_of(weights, own, received):
    return pl.pallas_call(
        image_kernel,
        out_shape=jax.ShapeDtypeStruct((4, 128), jnp.float32),
        in_specs=[LOCAL] * 3,
        out_specs=LOCAL,
        scratch_shapes=[
            pltpu.VMEM((15, 2, 24, 128), jnp.float32),
            pltpu.VMEM((240, 1024), jnp.float32),
        ],
        compiler_params=pltpu.CompilerParams(vmem_limit_bytes=VMEM),
        name="image",
    )(weights, own, received)


def on_device(electric, magnetic, material, decay, gain, kernels):
    el = electric.reshape(3, 640, 128)
    mg = magnetic.reshape(3, 640, 128)
    mat = material.reshape(640, 128)
    weights = jnp.pad(
        kernels.transpose(0, 1, 3, 2).reshape(48, 15, 15), ((0, 0), (0, 0), (0, 1))
    ).reshape(48, 240)

    strips, edge, edge_strips = own_strips(el, mg, mat)
    edge = around(edge, "gz", 1)
    from_low, from_high = around(strips, "gy", 1), around(strips, "gy", -1)
    edge_low, edge_high = beyond(edge_strips, 1), beyond(edge_strips, -1)
    own_u, up_u, down_u = pack(CUT, 10, el, mg, mat)
    up_u, down_u, edge_low, edge_high = lax.optimization_barrier(
        (up_u, down_u, edge_low, edge_high)
    )
    low_u, high_u = around(up_u, "gx", 1), around(down_u, "gx", -1)
    strips, up_c, down_c = corners(from_low, from_high, edge_low, edge_high, edge)
    low_c, high_c = around(up_c, "gx", 1), around(down_c, "gx", -1)
    own_l, up_l, down_l = pack(0, CUT, el, mg, mat, strips)
    low_l, high_l = around(up_l, "gx", 1), around(down_l, "gx", -1)

    sides = [low_c, high_c, strips, edge]
    field, plane = run_steps(True, decay, gain, sides, [own_u, low_u, high_u])
    top = jnp.stack([plane, around(plane, "gy", 1), around(plane, "gy", -1)])
    top = jnp.concatenate([around(top, "gx", 1), top, around(top, "gx", -1)], 2)
    top, low_l, high_l = lax.optimization_barrier((top, low_l, high_l))
    received = lax.ppermute(top, "gz", [(1, 0)])
    (field,) = run_steps(
        False, decay, gain, sides, [own_u, low_u, high_u, own_l, low_l, high_l, field]
    )
    image = image_of(weights, top, received)
    return (field.reshape(3, 80, 8, 128), image)


def solution(mesh):
    in_specs = (
        P(None, "gz", "gx", "gy"),
        P(None, "gz", "gx", "gy"),
        P("gz", "gx", "gy"),
        P(),
        P(),
        P(),
    )
    out_specs = (P(None, "gz", "gx", "gy"), P(("gx", "gz"), "gy"))
    return jax.shard_map(
        on_device, mesh=mesh, in_specs=in_specs, out_specs=out_specs, check_vma=False
    )
```
